256 devices in a mesh: space: 16 (over y, x_hi, core), period: 16 (over z, x_lo).
Axes of the slice: x: 4 (x_hi: 2, x_lo: 2; x = x_hi * 2 + x_lo), y: 4, z: 8, core: 2. Of those that a mesh axis runs over, the one named last changes fastest.
Arguments:
- source: float32 [2, 3, 32, 256, 128], P(None, None, 'space'), may hold values from -6 to 6
- conductivity: float32 [32, 256, 128], P('space'), may hold values from 0.1 to 2
- period_shift: float32 [16], P('period'), may hold values from 0.5 to 2
- site_cells: int32 [4, 2048], replicated, may hold values from 0 to 1048575, as said below
- site_weights: float32 [4, 2048], replicated, may hold values from 0.1 to 1
- observed: float32 [16, 4, 2048], P('period', None, 'space'), may hold values from -6 to 6
- data_weight: float32 [16, 4, 2048], P('period', None, 'space'), may hold values from 0.2 to 1
Outputs:
- predicted: float32 [16, 4, 2048], P('period', None, 'space')
- gradient: float32 [32, 256, 128], P('space', 'period')
The draws below stay inside these ranges and needn't reach their ends.
Inputs may be any that keep to these rules, and one draw needn't show every extreme that they name: `site_cells`: station s names its cell (x, y, z) and the cells (x+1, y, z), (x, y+1, z), (x+1, y+1, z), with x+1 replaced by 32 - 1 past the grid's end; y < 255 and z < 128. Stations fall more often at low x, so slabs hold unequal numbers of station cells.
All inputs are finite; a program needn't handle non-finite values.
Results may differ from the reference program's by a relative error of at most 0.0001.
Values sent between devices are 32-bit elements; how exact they have to be, the bound alone decides.
No kernel may reach another device: no remote copies, remote signals or barrier semaphores. Data moves between devices by JAX's collectives and lax.ppermute only.
A program may use at most 128 MiB of HBM per device.

```python
import math
import jax
import jax.numpy as jnp
from jax import lax

NY = 256
NZ = 128
SWEEPS = 4
Q = 4
NX = 32
STATIONS = 2048
PERIODS = 16


def draw_site_cells(key, part):
    subkeys = jax.random.split(key, 4)
    draw_one = jax.random.randint(subkeys[0], (STATIONS,), 0, NX)
    draw_two = jax.random.randint(subkeys[1], (STATIONS,), 0, NX)
    column_east = jnp.minimum(draw_one, draw_two)
    column_north = jax.random.randint(subkeys[2], (STATIONS,), 0, NY - 1)
    depth_index = jax.random.randint(subkeys[3], (STATIONS,), 0, NZ)
    column_east = column_east.at[0].set(0).at[STATIONS - 1].set(NX - 1)
    column_north = column_north.at[0].set(0).at[STATIONS - 1].set(NY - 2)
    depth_index = depth_index.at[0].set(0).at[STATIONS - 1].set(NZ - 1)
    offset_east = jnp.array([0, 1, 0, 1], jnp.int32)
    offset_north = jnp.array([0, 0, 1, 1], jnp.int32)
    cells_east = jnp.minimum(column_east[None, :] + offset_east[:, None], NX - 1)
    cells_north = column_north[None, :] + offset_north[:, None]
    cells_flat = (cells_east * NY + cells_north) * NZ + depth_index[None, :]
    return cells_flat.astype(jnp.int32)


def steps_of(key, shape, cuts, least, high):
    level, own = 1.0, jax.random.fold_in(key, 6)
    for dim, blocks in cuts:
        draws = jnp.exp(jax.random.uniform(jax.random.fold_in(own, dim), (blocks,), jnp.float32, least / len(cuts), high / len(cuts)))
        level = level * jnp.repeat(draws, shape[dim] // blocks).reshape([-1 if axis == dim else 1 for axis in range(len(shape))])
    return level


def noise(key, dims, deviation, limit, pieces=(), kind=jnp.bfloat16):
    result = deviation * jax.random.normal(key, dims, jnp.float32)
    if pieces:
        result = result * steps_of(key, dims, pieces, -0.22, 0.18)
    return jnp.clip(result, -limit, limit).astype(kind)


def setup_inputs(seed: int = 0) -> dict:
    splits = jax.random.split(jax.random.key(seed), 8)
    source = noise(splits[0], (2, 3, NX, NY, NZ), 1.0, 6.0, ((2, 16),), jnp.float32)
    conductivity = jnp.clip(jnp.exp(math.log(2.0) - 2.9957323 * jax.random.uniform(splits[1], (NX, NY, NZ), jnp.float32) ** steps_of(splits[1], (NX, NY, NZ), ((0, 16),), -0.2, 0.2)), 0.1, 2.0)
    period_shift = jnp.clip(jnp.exp(math.log(2.0) - 1.3862944 * jax.random.uniform(splits[2], (PERIODS,), jnp.float32) ** steps_of(splits[2], (PERIODS,), ((0, 16),), -0.2, 0.2)), 0.5, 2.0)
    site_cells = draw_site_cells(jax.random.fold_in(splits[7], 71), 0)
    site_weights = jnp.clip(jax.random.uniform(splits[4], (Q, STATIONS), jnp.float32, 0.1, 1.0), 0.1, 1.0)
    observed = noise(splits[5], (PERIODS, 4, STATIONS), 1.0, 6.0, ((0, 16), (2, 16)), jnp.float32)
    data_weight = jnp.clip(jnp.exp(math.log(1.0) - 1.609438 * jax.random.uniform(splits[6], (PERIODS, 4, STATIONS), jnp.float32) ** steps_of(splits[6], (PERIODS, 4, STATIONS), ((0, 16), (2, 16)), -0.2, 0.2)), 0.2, 1.0)
    return {"source": source, "conductivity": conductivity, "period_shift": period_shift, "site_cells": site_cells, "site_weights": site_weights, "observed": observed, "data_weight": data_weight}


LOWER_BOUND = 0.05
UPPER_BOUND = 16.0


def chebyshev_steps(sweep_count):
    center = 0.5 * (UPPER_BOUND + LOWER_BOUND)
    spread = 0.5 * (UPPER_BOUND - LOWER_BOUND)
    step_sizes = []
    momenta = []
    step_size = 1.0 / center
    for number in range(sweep_count):
        if number == 0:
            momentum = 0.0
        elif number == 1:
            momentum = 0.5 * (spread * step_size) ** 2
        else:
            momentum = (0.5 * spread * step_size) ** 2
        if number > 0:
            step_size = 1.0 / (center - momentum / step_size)
        step_sizes.append(step_size)
        momenta.append(momentum)
    return step_sizes, momenta


def forward_diff(values, along):
    extent = values.shape[along]
    shifted = lax.slice_in_dim(values, 1, extent, axis=along)
    pad_width = [(0, 0)] * values.ndim
    pad_width[along] = (0, 1)
    return jnp.pad(shifted, pad_width) - values


def backward_diff(values, along):
    extent = values.shape[along]
    shifted = lax.slice_in_dim(values, 0, extent - 1, axis=along)
    pad_width = [(0, 0)] * values.ndim
    pad_width[along] = (1, 0)
    return values - jnp.pad(shifted, pad_width)


def curl_plus(components):
    east_part, north_part, down_part = components
    return (forward_diff(down_part, 2) - forward_diff(north_part, 3),
            forward_diff(east_part, 3) - forward_diff(down_part, 1),
            forward_diff(north_part, 1) - forward_diff(east_part, 2))


def curl_minus(components):
    east_part, north_part, down_part = components
    return (backward_diff(down_part, 2) - backward_diff(north_part, 3),
            backward_diff(east_part, 3) - backward_diff(down_part, 1),
            backward_diff(north_part, 1) - backward_diff(east_part, 2))


def apply_operator(fields, mass_term):
    components = (fields[:, 0], fields[:, 1], fields[:, 2])
    curled = jnp.stack(curl_minus(curl_plus(components)), axis=1)
    return curled + mass_term * fields


def chebyshev_solve(right_side, mass_term):
    step_sizes, momenta = chebyshev_steps(SWEEPS)
    iterate = jnp.zeros_like(right_side)
    residual = right_side
    direction = jnp.zeros_like(right_side)
    for number in range(SWEEPS):
        direction = residual + momenta[number] * direction
        applied = apply_operator(direction, mass_term)
        iterate = iterate + step_sizes[number] * direction
        residual = residual - step_sizes[number] * applied
    return iterate


def reference(source, conductivity, period_shift, site_cells, site_weights, observed, data_weight):
    def one_period(running, inputs):
        shift_value, observed_now, weight_now = inputs
        mass_term = shift_value * conductivity
        forward = chebyshev_solve(source, mass_term)
        flat_field = forward[:, :2].reshape(4, NX * NY * NZ)
        predicted_now = jnp.sum(flat_field[:, site_cells] * site_weights[None], axis=1)
        adjoint_data = weight_now * weight_now * (predicted_now - observed_now)
        right_flat = jnp.zeros_like(flat_field).at[:, site_cells].add(site_weights[None] * adjoint_data[:, None, :])
        right_side = jnp.concatenate([right_flat.reshape(2, 2, NX, NY, NZ), jnp.zeros((2, 1, NX, NY, NZ), jnp.float32)], axis=1)
        adjoint = chebyshev_solve(right_side, mass_term)
        period_term = -shift_value * jnp.sum(adjoint * forward, axis=(0, 1))
        return running + period_term, predicted_now

    summed, predicted = lax.scan(one_period, jnp.zeros((NX, NY, NZ), jnp.float32), (period_shift, observed, data_weight))
    return predicted, summed / PERIODS
```

```python
import jax
import jax.numpy as jnp
from jax import lax
from jax.experimental import pallas as pl
from jax.experimental.pallas import tpu as pltpu
from jax.sharding import PartitionSpec as P

SWEEPS = 4
LOWER_BOUND = 0.05
UPPER_BOUND = 16.0

CENTER = 1.25
HALO = SWEEPS - 1
PLANES = 2 + 2 * HALO
WINDOW = 32
DEGREE = SWEEPS
MOMENTS = 2 * SWEEPS - 1
LANES = 128
VMEM_LIMIT = 48 * 1024 * 1024


def chebyshev_steps(sweep_count):
    center = 0.5 * (UPPER_BOUND + LOWER_BOUND)
    spread = 0.5 * (UPPER_BOUND - LOWER_BOUND)
    step_sizes = []
    momenta = []
    step_size = 1.0 / center
    for number in range(sweep_count):
        if number == 0:
            momentum = 0.0
        elif number == 1:
            momentum = 0.5 * (spread * step_size) ** 2
        else:
            momentum = (0.5 * spread * step_size) ** 2
        if number > 0:
            step_size = 1.0 / (center - momentum / step_size)
        step_sizes.append(step_size)
        momenta.append(momentum)
    return (step_sizes, momenta)


STEP, MOMENTUM = chebyshev_steps(SWEEPS)


def place(grid_rows, own_rows):
    first_own = lax.axis_index("period") * own_rows
    first_row = jnp.clip(first_own - (WINDOW - own_rows) // 2, 0, grid_rows - WINDOW)
    return lax.axis_index("space") * 2 - HALO, pl.multiple_of(first_row, 8), first_own


def iota(shape, dim):
    return lax.broadcasted_iota(jnp.int32, shape, dim)


def parts_of(values):
    high = values.astype(jnp.bfloat16)
    rest = values - high.astype(jnp.float32)
    middle = rest.astype(jnp.bfloat16)
    low = (rest - middle.astype(jnp.float32)).astype(jnp.bfloat16)
    return high, middle, low


def dot_nt(left, right):
    return lax.dot_general(left, right, (((1,), (1,)), ((), ())), preferred_element_type=jnp.float32)


def dot_nn(left, right):
    return lax.dot_general(left, right, (((1,), (0,)), ((), ())), preferred_element_type=jnp.float32)


def next_z(v):
    return jnp.where(iota(v.shape, 1) == v.shape[1] - 1, 0.0, pltpu.roll(v, v.shape[1] - 1, 1))


def last_z(v):
    return jnp.where(iota(v.shape, 1) == 0, 0.0, pltpu.roll(v, 1, 1))


def next_y(v):
    return jnp.where(iota(v.shape, 0) == v.shape[0] - 1, 0.0, pltpu.roll(v, v.shape[0] - 1, 0))


def last_y(v):
    return jnp.where(iota(v.shape, 0) == 0, 0.0, pltpu.roll(v, 1, 0))


def curl_curl(get, first, last, first_plane, planes_in_grid):
    before = None
    here = get(first - 1)
    for plane in range(first - 1, last + 1):
        after = get(plane + 1)
        east, north, down = here
        c2 = next_z(east) - east
        if down is not None:
            c2 = c2 - (after[2] - down)
        c3 = (after[1] - north) - (next_y(east) - east)
        if plane < HALO and plane % 2 == 0:
            inside = jnp.where(first_plane + plane < 0, 0.0, 1.0)
            c2 = c2 * inside
            c3 = c3 * inside
        if plane >= first:
            c1 = north - next_z(north)
            if down is not None:
                c1 = c1 + (next_y(down) - down)
            a1 = (c3 - last_y(c3)) - (c2 - last_z(c2))
            a2 = (c1 - last_z(c1)) - (c3 - before[1])
            a3 = (c2 - before[0]) - (c1 - last_y(c1))
            if plane == HALO + 2:
                inside = jnp.where(first_plane + plane >= planes_in_grid, 0.0, 1.0)
                a1, a2, a3 = a1 * inside, a2 * inside, a3 * inside
            yield plane, here, (a1, a2, a3)
        before = (c2, c3)
        here = after


def pack_kernel(
    grid_rows, own_rows, source, conductivity, shift, observed, weight,
    slab, low, high, data, sems,
):
    _, first_row, _ = place(grid_rows, own_rows)
    rows = pl.ds(first_row, WINDOW)
    copies = []
    for plane in range(2):
        for pol in range(2):
            copies.append((source.at[pol, :, plane, rows, :], slab.at[plane, pl.ds(3 * pol, 3)]))
        copies.append((conductivity.at[plane, rows, :], slab.at[plane, 6]))
    for pol in range(2):
        copies.append((source.at[pol, :, 0, rows, :], low.at[pl.ds(3 * pol, 3)]))
        copies.append((source.at[pol, :, 1, rows, :], high.at[pl.ds(3 * pol, 3)]))
    started = [pltpu.make_async_copy(a, b, sems.at[i]) for i, (a, b) in enumerate(copies)]
    for copy in started:
        copy.start()
    for member in range(data.shape[0]):
        data[member, 0:4, :] = observed[0]
        data[member, 4:8, :] = weight[0]
        data[member, 8:16, :] = jnp.full((8, LANES), shift[0], jnp.float32)
    for copy in started:
        copy.wait()


def pack(source, conductivity, shift, observed, weight, members):
    grid_rows = source.shape[3]
    shape = jax.ShapeDtypeStruct
    hbm = pl.BlockSpec(memory_space=pl.ANY)
    vmem = pl.BlockSpec(memory_space=pltpu.VMEM)
    smem = pl.BlockSpec(memory_space=pltpu.SMEM)
    return pl.pallas_call(
        lambda *refs: pack_kernel(grid_rows, grid_rows // members, *refs),
        out_shape=(
            shape((2, 7, WINDOW, LANES), jnp.float32),
            shape((6, WINDOW, LANES), jnp.float32),
            shape((6, WINDOW, LANES), jnp.float32),
            shape((members, 16, LANES), jnp.float32),
        ),
        in_specs=[hbm, hbm, smem, vmem, vmem],
        out_specs=(hbm, hbm, hbm, vmem),
        scratch_shapes=[pltpu.SemaphoreType.DMA((10,))],
        name="pack",
    )(source, conductivity, shift, observed, weight)


def stations_kernel(grid_rows, own_rows, cells, weights, places, count, features, marks, staged):
    first_plane, first_row, first_own = place(grid_rows, own_rows)
    plane_size = grid_rows * LANES
    cell = cells[...]
    x = cell // plane_size - first_plane
    y = (cell // LANES) % grid_rows
    reached = (
        (x >= 0) & (x < PLANES)
        & (y >= first_own - HALO - 1) & (y < first_own + own_rows + HALO + 1)
    )
    row = jnp.where(reached, x * WINDOW + y - first_row, 0).astype(jnp.float32)
    weight = jnp.where(reached, weights[...], 0.0)
    present = jnp.max(jnp.where(reached, 1.0, 0.0), axis=0, keepdims=True)
    blocks = cell.shape[1] // LANES
    staged[...] = jnp.zeros(staged.shape, jnp.float32)
    staged[0:4, :] = row
    staged[4:8, :] = (cell % LANES).astype(jnp.float32)
    for number, part in enumerate(parts_of(weight)):
        staged[8 + 4 * number : 12 + 4 * number, :] = part.astype(jnp.float32)
    for block in range(blocks):
        marks[block : block + 1, :] = present[:, block * LANES : (block + 1) * LANES]
    mark = marks[...]
    square = (LANES, LANES)
    upto = jnp.where(iota(square, 0) <= iota(square, 1), 1.0, 0.0).astype(jnp.bfloat16)
    inner = dot_nn(mark.astype(jnp.bfloat16), upto)
    totals = dot_nn(mark.astype(jnp.bfloat16), jnp.ones(square, jnp.bfloat16))
    earlier = jnp.where(iota((blocks, blocks), 0) > iota((blocks, blocks), 1), 1.0, 0.0)
    offsets = dot_nn(earlier.astype(jnp.bfloat16), totals.astype(jnp.bfloat16))
    places[...] = jnp.where(mark > 0.0, inner + offsets - 1.0, -1.0).astype(jnp.int32)
    chunks = (jnp.sum(mark).astype(jnp.int32) + LANES - 1) // LANES
    count[0] = chunks

    def one_chunk(chunk, carry):
        gathered = jnp.zeros((staged.shape[0], LANES), jnp.float32)
        for block in range(blocks):
            feature = staged[:, block * LANES : (block + 1) * LANES].astype(jnp.bfloat16)
            gathered += dot_nt(feature, picks(places, block, chunk))
        features[chunk] = gathered
        return carry

    features[0] = jnp.zeros(features.shape[1:], jnp.float32)
    lax.fori_loop(0, chunks, one_chunk, 0)


def picks(places, block, chunk):
    wanted = places[block : block + 1, :] - chunk * LANES
    return jnp.where(iota((LANES, LANES), 0) == wanted, 1.0, 0.0).astype(jnp.bfloat16)


def stations(cells, weights, grid_rows, members):
    blocks = cells.shape[1] // LANES
    shape = jax.ShapeDtypeStruct
    vmem = pl.BlockSpec(memory_space=pltpu.VMEM)
    return pl.pallas_call(
        lambda *refs: stations_kernel(grid_rows, grid_rows // members, *refs),
        out_shape=(
            shape((blocks, LANES), jnp.int32),
            shape((1,), jnp.int32),
            shape((blocks, 32, LANES), jnp.float32),
        ),
        in_specs=[vmem, vmem],
        out_specs=(vmem, pl.BlockSpec(memory_space=pltpu.SMEM), vmem),
        scratch_shapes=[
            pltpu.VMEM((blocks, LANES), jnp.float32),
            pltpu.VMEM((32, cells.shape[1]), jnp.float32),
        ],
        compiler_params=pltpu.CompilerParams(vmem_limit_bytes=VMEM_LIMIT),
        cost_estimate=pl.CostEstimate(flops=10_000_000, bytes_accessed=200_000, transcendentals=0),
        name="stations",
    )(cells, weights)


def row_weights(feature, first, count):
    rows = (iota((count, LANES), 0) + first).astype(jnp.float32)
    total = jnp.zeros((count, LANES), jnp.float32)
    for q in range(4):
        weight = feature[8 + q : 9 + q] + feature[12 + q : 13 + q] + feature[16 + q : 17 + q]
        total += jnp.where(rows == feature[q : q + 1], weight, 0.0)
    return total


def depth_picks(feature):
    depth = iota((LANES, LANES), 0).astype(jnp.float32)
    return jnp.where(depth == feature[4:5], 1.0, 0.0).astype(jnp.bfloat16)


def forward_kernel(
    grid_rows, own_rows, grid_planes, slab, below, above, below2, above2, places, count, features,
    field, sent, mass, d1, d2,
):
    first_plane, _, _ = place(grid_rows, own_rows)

    def part(number, plane):
        if plane == 0:
            return below2[number]
        if plane <= 2:
            return below[plane - 1, number]
        if plane <= 4:
            return slab[plane - 3, number]
        if plane <= 6:
            return above[plane - 5, number]
        return above2[number]

    for plane in range(1, PLANES - 1):
        mass[plane - 1] = part(6, plane)

    for pol in range(2):
        def b(plane, pol=pol):
            return tuple(part(3 * pol + c, plane) for c in range(3))

        for plane, here, curled in curl_curl(b, 1, 6, first_plane, grid_planes):
            m = mass[plane - 1]
            for c in range(3):
                heavy = m * here[c]
                d1[0, pol, c, plane - 1] = (
                    (1.0 + MOMENTUM[1]) * here[c] - STEP[0] * (curled[c] + CENTER * heavy)
                )
                d1[1, pol, c, plane - 1] = -STEP[0] * heavy

        def level1(j, pol=pol):
            return lambda plane: tuple(d1[j, pol, c, plane - 1] for c in range(3))

        for j in range(2):
            for plane, here, curled in curl_curl(level1(j), 2, 5, first_plane, grid_planes):
                m = mass[plane - 1]
                for c in range(3):
                    mixed = CENTER * here[c]
                    if j == 1:
                        mixed = mixed + d1[0, pol, c, plane - 1]
                    value = (1.0 + MOMENTUM[2]) * here[c] - STEP[1] * (curled[c] + m * mixed)
                    if j == 0:
                        value = value - MOMENTUM[1] * part(3 * pol + c, plane)
                    d2[j, pol, c, plane - 2] = value
                    if j == 1:
                        d2[2, pol, c, plane - 2] = -STEP[1] * (m * here[c])

        def level2(j, pol=pol):
            return lambda plane: tuple(d2[j, pol, c, plane - 2] for c in range(3))

        for j in range(3):
            for plane, here, curled in curl_curl(level2(j), 3, 4, first_plane, grid_planes):
                m = mass[plane - 1]
                for c in range(3):
                    mixed = CENTER * here[c]
                    if j > 0:
                        mixed = mixed + d2[j - 1, pol, c, plane - 2]
                    last = (1.0 + MOMENTUM[3]) * here[c] - STEP[2] * (curled[c] + m * mixed)
                    value = STEP[2] * here[c]
                    if j < 2:
                        first = d1[j, pol, c, plane - 1]
                        last = last - MOMENTUM[2] * first
                        value = value + STEP[1] * first
                    if j == 0:
                        value = value + STEP[0] * part(3 * pol + c, plane)
                    field[j, pol, c, plane - 3] = value + STEP[3] * last
                    if j == 2:
                        field[3, pol, c, plane - 3] = -(STEP[3] * STEP[2]) * (m * here[c])

    members = sent.shape[0]
    sent[...] = jnp.zeros(sent.shape, jnp.float32)

    def one_chunk(chunk, carry):
        feature = features[chunk]
        weight = row_weights(feature, HALO * WINDOW, 2 * WINDOW)
        depth = depth_picks(feature)
        rows = []
        for j in range(DEGREE):
            for pol in range(2):
                for c in range(2):
                    values = field[j, pol, c].reshape(2 * WINDOW, LANES)
                    at_depth = sum(dot_nn(piece, depth) for piece in parts_of(values))
                    rows.append(jnp.sum(at_depth * weight, axis=0, keepdims=True))
        read = jnp.concatenate(rows, axis=0)
        pieces = jnp.concatenate(parts_of(read), axis=0)
        for block in range(members):
            spread = dot_nn(pieces, picks(places, block, chunk))
            sent[block] += spread[0:16] + spread[16:32] + spread[32:48]
        return carry

    lax.fori_loop(0, count[0], one_chunk, 0)


def forward_solve(slab, below, above, below2, above2, station_parts, grid_rows, members, grid_planes):
    shape = jax.ShapeDtypeStruct
    vmem = pl.BlockSpec(memory_space=pltpu.VMEM)
    smem = pl.BlockSpec(memory_space=pltpu.SMEM)
    blocks = station_parts[0].shape[0]
    return pl.pallas_call(
        lambda *refs: forward_kernel(grid_rows, grid_rows // members, grid_planes, *refs),
        out_shape=(
            shape((DEGREE, 2, 3, 2, WINDOW, LANES), jnp.float32),
            shape((blocks, 4 * DEGREE, LANES), jnp.float32),
            shape((PLANES - 2, WINDOW, LANES), jnp.float32),
        ),
        in_specs=[vmem] * 6 + [smem, vmem],
        out_specs=(vmem, vmem, vmem),
        scratch_shapes=[
            pltpu.VMEM((2, 2, 3, PLANES - 2, WINDOW, LANES), jnp.float32),
            pltpu.VMEM((3, 2, 3, PLANES - 4, WINDOW, LANES), jnp.float32),
        ],
        compiler_params=pltpu.CompilerParams(vmem_limit_bytes=VMEM_LIMIT),
        cost_estimate=pl.CostEstimate(flops=50_000_000, bytes_accessed=3_000_000, transcendentals=0),
        name="forward_solve",
    )(slab, below, above, below2, above2, *station_parts)


def residual_kernel(grid_rows, own_rows, read, data, cells, moments, owned, staged):
    members = data.shape[0]
    total = read[0]
    for member in range(1, read.shape[0]):
        total = total + read[member]
    coefficients = [total[4 * j : 4 * j + 4] for j in range(DEGREE)]
    first = pl.multiple_of(lax.axis_index("space") * LANES, LANES)
    cell = cells[:, pl.ds(first, LANES)]
    y = jnp.min((cell // LANES) % grid_rows, axis=0, keepdims=True)
    mine = (y // own_rows) == lax.axis_index("period")
    sums = [jnp.zeros((4, LANES), jnp.float32) for _ in range(MOMENTS)]
    for member in range(members):
        shift = data[member, 8:9, :]
        delta = shift - CENTER
        value = coefficients[DEGREE - 1]
        for j in range(DEGREE - 2, -1, -1):
            value = value * delta + coefficients[j]
        owned[member] = jnp.where(mine, value, 0.0)
        weight = data[member, 4:8, :]
        term = shift * (weight * weight * (value - data[member, 0:4, :]))
        for number in range(MOMENTS):
            sums[number] = sums[number] + term
            if number + 1 < MOMENTS:
                term = term * delta
    staged[...] = jnp.zeros(staged.shape, jnp.float32)
    for number in range(MOMENTS):
        staged[4 * number : 4 * number + 4, :] = sums[number]
    value = staged[...]
    for member in range(moments.shape[0]):
        moments[member] = value


def residuals(read, data, cells, grid_rows, members):
    shape = jax.ShapeDtypeStruct
    vmem = pl.BlockSpec(memory_space=pltpu.VMEM)
    return pl.pallas_call(
        lambda *refs: residual_kernel(grid_rows, grid_rows // members, *refs),
        out_shape=(
            shape((read.shape[0], 32, LANES), jnp.float32),
            shape((members, 4, LANES), jnp.float32),
        ),
        in_specs=[vmem, vmem, vmem],
        out_specs=(vmem, vmem),
        scratch_shapes=[pltpu.VMEM((32, LANES), jnp.float32)],
        name="residuals",
    )(read, data, cells)


def adjoint_kernel(
    grid_rows, own_rows, grid_planes, periods, moments, places, count, features, mass, field,
    gradient, d0, d1, d2, picked, total,
):
    first_plane, first_row, first_own = place(grid_rows, own_rows)
    blocks = moments.shape[0]
    window_rows = PLANES * WINDOW

    def add_chunk(chunk, fresh):
        feature = features[chunk]
        weight = row_weights(feature, 0, window_rows)
        depth = depth_picks(feature)
        depth = jnp.concatenate([depth, depth], axis=1)
        gathered = jnp.zeros((96, LANES), jnp.float32)
        for block in range(blocks):
            pieces = jnp.concatenate(parts_of(moments[block]), axis=0)
            gathered += dot_nt(pieces, picks(places, block, chunk))
        picked[...] = gathered[0:32] + gathered[32:64] + gathered[64:96]

        def one_field(number, carry):
            values = weight * picked[pl.ds(number, 1), :]
            high = values.astype(jnp.bfloat16)
            low = (values - high.astype(jnp.float32)).astype(jnp.bfloat16)
            placed = dot_nt(jnp.concatenate([high, low], axis=1), depth)
            if fresh:
                d0[number] = placed
            else:
                d0[number] += placed
            return carry

        lax.fori_loop(0, 4 * MOMENTS, one_field, 0)

    add_chunk(0, True)

    def one_chunk(chunk, carry):
        add_chunk(chunk, False)
        return carry

    lax.fori_loop(1, count[0], one_chunk, 0)

    def start(f, c, plane):
        return d0[2 * f + c, plane * WINDOW : (plane + 1) * WINDOW, :]

    def level_one(f, carry):
        def b(plane):
            return start(f, 0, plane), start(f, 1, plane), None

        for plane, here, curled in curl_curl(b, 1, 6, first_plane, grid_planes):
            m = mass[plane - 1]
            for c in range(2):
                mixed = CENTER * here[c] + start(f + 2, c, plane)
                d1[f, c, plane - 1] = (
                    (1.0 + MOMENTUM[1]) * here[c] - STEP[0] * (curled[c] + m * mixed)
                )
            d1[f, 2, plane - 1] = -STEP[0] * curled[2]
        return carry

    lax.fori_loop(0, 2 * (MOMENTS - 1), level_one, 0)

    def level_two(f, carry):
        def get(plane):
            return tuple(d1[f, c, plane - 1] for c in range(3))

        for plane, here, curled in curl_curl(get, 2, 5, first_plane, grid_planes):
            m = mass[plane - 1]
            for c in range(3):
                mixed = CENTER * here[c] + d1[f + 2, c, plane - 1]
                value = (1.0 + MOMENTUM[2]) * here[c] - STEP[1] * (curled[c] + m * mixed)
                if c < 2:
                    value = value - MOMENTUM[1] * start(f, c, plane)
                d2[f, c, plane - 2] = value
        return carry

    lax.fori_loop(0, 2 * (MOMENTS - 2), level_two, 0)

    total[...] = jnp.zeros(total.shape, jnp.float32)

    def level_three(f, carry):
        def get(plane):
            return tuple(d2[f, c, plane - 2] for c in range(3))

        for plane, here, curled in curl_curl(get, 3, 4, first_plane, grid_planes):
            m = mass[plane - 1]
            added = None
            for c in range(3):
                mixed = CENTER * here[c] + d2[f + 2, c, plane - 2]
                first = d1[f, c, plane - 1]
                last = (
                    (1.0 + MOMENTUM[3]) * here[c] - MOMENTUM[2] * first
                    - STEP[2] * (curled[c] + m * mixed)
                )
                value = STEP[1] * first + STEP[2] * here[c] + STEP[3] * last
                if c < 2:
                    value = value + STEP[0] * start(f, c, plane)
                term = value * field[f, c, plane - 3]
                added = term if added is None else added + term
            total[plane - 3] += added
        return carry

    lax.fori_loop(0, 2 * DEGREE, level_three, 0)
    offset = pl.multiple_of(first_own - first_row, 8)
    gradient[...] = total[:, pl.ds(offset, own_rows), :] * (-1.0 / periods)


def adjoint_solve(moments, station_parts, mass, field, grid_rows, members, grid_planes):
    vmem = pl.BlockSpec(memory_space=pltpu.VMEM)
    smem = pl.BlockSpec(memory_space=pltpu.SMEM)
    own_rows = grid_rows // members
    return pl.pallas_call(
        lambda *refs: adjoint_kernel(grid_rows, own_rows, grid_planes, members, *refs),
        out_shape=jax.ShapeDtypeStruct((2, own_rows, LANES), jnp.float32),
        in_specs=[vmem, vmem, smem, vmem, vmem, vmem],
        out_specs=vmem,
        scratch_shapes=[
            pltpu.VMEM((4 * MOMENTS, PLANES * WINDOW, LANES), jnp.float32),
            pltpu.VMEM((2 * (MOMENTS - 1), 3, PLANES - 2, WINDOW, LANES), jnp.float32),
            pltpu.VMEM((2 * (MOMENTS - 2), 3, PLANES - 4, WINDOW, LANES), jnp.float32),
            pltpu.VMEM((32, LANES), jnp.float32),
            pltpu.VMEM((2, WINDOW, LANES), jnp.float32),
        ],
        compiler_params=pltpu.CompilerParams(vmem_limit_bytes=VMEM_LIMIT),
        cost_estimate=pl.CostEstimate(flops=200_000_000, bytes_accessed=3_000_000, transcendentals=0),
        name="adjoint_solve",
    )(moments, *station_parts, mass, field.reshape(2 * DEGREE, 3, 2, WINDOW, LANES))


def shards(source, conductivity, period_shift, site_cells, site_weights, observed, data_weight):
    grid_rows = conductivity.shape[1]
    count = lax.axis_size("space")
    members = lax.axis_size("period")
    grid_planes = conductivity.shape[0] * count
    slab, low, high, data = pack(source, conductivity, period_shift, observed, data_weight, members)

    def moved(values, by):
        pairs = [(i, i + by) for i in range(count) if 0 <= i + by < count]
        return lax.ppermute(values, "space", pairs)

    below = moved(slab, 1)
    above = moved(slab, -1)
    below2 = moved(high, 2)
    above2 = moved(low, -2)
    data = lax.all_to_all(data, "period", 0, 0, tiled=True)
    station_parts = stations(site_cells, site_weights, grid_rows, members)
    field, sent, mass = forward_solve(
        slab, below, above, below2, above2, station_parts, grid_rows, members, grid_planes
    )
    read = lax.all_to_all(sent, "space", 0, 0, tiled=True)
    moments, owned = residuals(read, data, site_cells, grid_rows, members)
    moments = lax.all_to_all(moments, "space", 0, 0, tiled=True)
    owned = lax.all_to_all(owned, "period", 0, 0, tiled=True)
    gradient = adjoint_solve(moments, station_parts, mass, field, grid_rows, members, grid_planes)
    return jnp.sum(owned, axis=0, keepdims=True), gradient


def solution(mesh):
    placed = (
        P(None, None, "space", None, None),
        P("space", None, None),
        P("period"),
        P(),
        P(),
        P("period", None, "space"),
        P("period", None, "space"),
    )
    return jax.shard_map(
        shards,
        mesh=mesh,
        in_specs=placed,
        out_specs=(P("period", None, "space"), P("space", "period", None)),
        check_vma=False,
    )
```

```python
import jax
import jax.numpy as jnp
from jax import lax
from jax.experimental import pallas as pl
from jax.experimental.pallas import tpu as pltpu
from jax.sharding import PartitionSpec as P

SWEEPS = 4
LOWER_BOUND = 0.05
UPPER_BOUND = 16.0

CENTER = 1.25
HALO = SWEEPS - 1
PLANES = 2 + 2 * HALO
WINDOW = 32
DEGREE = SWEEPS
MOMENTS = 2 * SWEEPS - 1
LANES = 128
VMEM_LIMIT = 48 * 1024 * 1024


def chebyshev_steps(sweep_count):
    center = 0.5 * (UPPER_BOUND + LOWER_BOUND)
    spread = 0.5 * (UPPER_BOUND - LOWER_BOUND)
    step_sizes = []
    momenta = []
    step_size = 1.0 / center
    for number in range(sweep_count):
        if number == 0:
            momentum = 0.0
        elif number == 1:
            momentum = 0.5 * (spread * step_size) ** 2
        else:
            momentum = (0.5 * spread * step_size) ** 2
        if number > 0:
            step_size = 1.0 / (center - momentum / step_size)
        step_sizes.append(step_size)
        momenta.append(momentum)
    return (step_sizes, momenta)


STEP, MOMENTUM = chebyshev_steps(SWEEPS)


def window_row(member, grid_rows, own_rows):
    first = member * own_rows - (WINDOW - own_rows) // 2
    return pl.multiple_of(jnp.clip(first, 0, grid_rows - WINDOW), 8)


def place(grid_rows, own_rows):
    member = lax.axis_index("period")
    first_row = window_row(member, grid_rows, own_rows)
    return lax.axis_index("space") * 2 - HALO, first_row, member * own_rows


def iota(shape, dim):
    return lax.broadcasted_iota(jnp.int32, shape, dim)


def parts_of(values):
    high = values.astype(jnp.bfloat16)
    rest = values - high.astype(jnp.float32)
    middle = rest.astype(jnp.bfloat16)
    low = (rest - middle.astype(jnp.float32)).astype(jnp.bfloat16)
    return high, middle, low


def dot_nt(left, right):
    return lax.dot_general(left, right, (((1,), (1,)), ((), ())), preferred_element_type=jnp.float32)


def dot_nn(left, right):
    return lax.dot_general(left, right, (((1,), (0,)), ((), ())), preferred_element_type=jnp.float32)


def next_z(v):
    return jnp.where(iota(v.shape, 1) == v.shape[1] - 1, 0.0, pltpu.roll(v, v.shape[1] - 1, 1))


def last_z(v):
    return jnp.where(iota(v.shape, 1) == 0, 0.0, pltpu.roll(v, 1, 1))


def next_y(v):
    return jnp.where(iota(v.shape, 0) == v.shape[0] - 1, 0.0, pltpu.roll(v, v.shape[0] - 1, 0))


def last_y(v):
    return jnp.where(iota(v.shape, 0) == 0, 0.0, pltpu.roll(v, 1, 0))


def curl_curl(get, first, last, first_plane, planes_in_grid):
    before = None
    here = get(first - 1)
    for plane in range(first - 1, last + 1):
        after = get(plane + 1)
        east, north, down = here
        c2 = next_z(east) - east
        if down is not None:
            c2 = c2 - (after[2] - down)
        c3 = (after[1] - north) - (next_y(east) - east)
        if plane < HALO and plane % 2 == 0:
            inside = jnp.where(first_plane + plane < 0, 0.0, 1.0)
            c2 = c2 * inside
            c3 = c3 * inside
        if plane >= first:
            c1 = north - next_z(north)
            if down is not None:
                c1 = c1 + (next_y(down) - down)
            a1 = (c3 - last_y(c3)) - (c2 - last_z(c2))
            a2 = (c1 - last_z(c1)) - (c3 - before[1])
            a3 = (c2 - before[0]) - (c1 - last_y(c1))
            if plane == HALO + 2:
                inside = jnp.where(first_plane + plane >= planes_in_grid, 0.0, 1.0)
                a1, a2, a3 = a1 * inside, a2 * inside, a3 * inside
            yield plane, here, (a1, a2, a3)
        before = (c2, c3)
        here = after


def pack_kernel(
    grid_rows, own_rows, source, conductivity, shift, observed, weight,
    slab, up, down, up2, down2, data, sems,
):
    member = lax.axis_index("period")
    even = lax.axis_index("space") % 2 == 0
    mine = window_row(member, grid_rows, own_rows)
    beside = window_row(member + 1 - 2 * (member % 2), grid_rows, own_rows)
    copies = []
    for target, row in (
        (slab, mine),
        (up, jnp.where(even, mine, beside)),
        (down, jnp.where(even, beside, mine)),
    ):
        rows = pl.ds(pl.multiple_of(row, 8), WINDOW)
        for pol in range(2):
            copies.append((source.at[pol, :, :, rows, :], target.at[pl.ds(3 * pol, 3)]))
        copies.append((conductivity.at[:, rows, :], target.at[6]))
    rows = pl.ds(beside, WINDOW)
    for pol in range(2):
        copies.append((source.at[pol, :, 1, rows, :], up2.at[pl.ds(3 * pol, 3)]))
        copies.append((source.at[pol, :, 0, rows, :], down2.at[pl.ds(3 * pol, 3)]))
    started = [pltpu.make_async_copy(a, b, sems.at[i]) for i, (a, b) in enumerate(copies)]
    for copy in started:
        copy.start()
    for member in range(data.shape[0]):
        data[member, 0:4, :] = observed[0]
        data[member, 4:8, :] = weight[0]
        data[member, 8:16, :] = jnp.full((8, LANES), shift[0], jnp.float32)
    for copy in started:
        copy.wait()


def pack(source, conductivity, shift, observed, weight, members):
    grid_rows = source.shape[3]
    shape = jax.ShapeDtypeStruct
    hbm = pl.BlockSpec(memory_space=pl.ANY)
    vmem = pl.BlockSpec(memory_space=pltpu.VMEM)
    smem = pl.BlockSpec(memory_space=pltpu.SMEM)
    return pl.pallas_call(
        lambda *refs: pack_kernel(grid_rows, grid_rows // members, *refs),
        out_shape=(shape((7, 2, WINDOW, LANES), jnp.float32),) * 3
        + (shape((6, WINDOW, LANES), jnp.float32),) * 2
        + (shape((members, 16, LANES), jnp.float32),),
        in_specs=[hbm, hbm, smem, vmem, vmem],
        out_specs=(vmem,) * 6,
        scratch_shapes=[pltpu.SemaphoreType.DMA((13,))],
        name="pack",
    )(source, conductivity, shift, observed, weight)


def stations_kernel(grid_rows, own_rows, cells, weights, places, count, features, marks, staged):
    first_plane, first_row, first_own = place(grid_rows, own_rows)
    plane_size = grid_rows * LANES
    cell = cells[...]
    x = cell // plane_size - first_plane
    y = (cell // LANES) % grid_rows
    reached = (
        (x >= 0) & (x < PLANES)
        & (y >= first_own - HALO - 1) & (y < first_own + own_rows + HALO + 1)
    )
    row = jnp.where(reached, x * WINDOW + y - first_row, 0).astype(jnp.float32)
    weight = jnp.where(reached, weights[...], 0.0)
    present = jnp.max(jnp.where(reached, 1.0, 0.0), axis=0, keepdims=True)
    blocks = cell.shape[1] // LANES
    staged[...] = jnp.zeros(staged.shape, jnp.float32)
    staged[0:4, :] = row
    staged[4:8, :] = (cell % LANES).astype(jnp.float32)
    for number, part in enumerate(parts_of(weight)):
        staged[8 + 4 * number : 12 + 4 * number, :] = part.astype(jnp.float32)
    for block in range(blocks):
        marks[block : block + 1, :] = present[:, block * LANES : (block + 1) * LANES]
    mark = marks[...]
    square = (LANES, LANES)
    upto = jnp.where(iota(square, 0) <= iota(square, 1), 1.0, 0.0).astype(jnp.bfloat16)
    inner = dot_nn(mark.astype(jnp.bfloat16), upto)
    totals = dot_nn(mark.astype(jnp.bfloat16), jnp.ones(square, jnp.bfloat16))
    earlier = jnp.where(iota((blocks, blocks), 0) > iota((blocks, blocks), 1), 1.0, 0.0)
    offsets = dot_nn(earlier.astype(jnp.bfloat16), totals.astype(jnp.bfloat16))
    places[...] = jnp.where(mark > 0.0, inner + offsets - 1.0, -1.0).astype(jnp.int32)
    chunks = (jnp.sum(mark).astype(jnp.int32) + LANES - 1) // LANES
    count[0] = chunks

    def one_chunk(chunk, carry):
        gathered = jnp.zeros((staged.shape[0], LANES), jnp.float32)
        for block in range(blocks):
            feature = staged[:, block * LANES : (block + 1) * LANES].astype(jnp.bfloat16)
            gathered += dot_nt(feature, picks(places, block, chunk))
        features[chunk] = gathered
        return carry

    features[0] = jnp.zeros(features.shape[1:], jnp.float32)
    lax.fori_loop(0, chunks, one_chunk, 0)


def picks(places, block, chunk):
    wanted = places[block : block + 1, :] - chunk * LANES
    return jnp.where(iota((LANES, LANES), 0) == wanted, 1.0, 0.0).astype(jnp.bfloat16)


def stations(cells, weights, grid_rows, members):
    blocks = cells.shape[1] // LANES
    shape = jax.ShapeDtypeStruct
    vmem = pl.BlockSpec(memory_space=pltpu.VMEM)
    return pl.pallas_call(
        lambda *refs: stations_kernel(grid_rows, grid_rows // members, *refs),
        out_shape=(
            shape((blocks, LANES), jnp.int32),
            shape((1,), jnp.int32),
            shape((blocks, 32, LANES), jnp.float32),
        ),
        in_specs=[vmem, vmem],
        out_specs=(vmem, pl.BlockSpec(memory_space=pltpu.SMEM), vmem),
        scratch_shapes=[
            pltpu.VMEM((blocks, LANES), jnp.float32),
            pltpu.VMEM((32, cells.shape[1]), jnp.float32),
        ],
        compiler_params=pltpu.CompilerParams(vmem_limit_bytes=VMEM_LIMIT),
        cost_estimate=pl.CostEstimate(flops=10_000_000, bytes_accessed=200_000, transcendentals=0),
        name="stations",
    )(cells, weights)


def row_weights(feature, first, count):
    rows = (iota((count, LANES), 0) + first).astype(jnp.float32)
    total = jnp.zeros((count, LANES), jnp.float32)
    for q in range(4):
        weight = feature[8 + q : 9 + q] + feature[12 + q : 13 + q] + feature[16 + q : 17 + q]
        total += jnp.where(rows == feature[q : q + 1], weight, 0.0)
    return total


def depth_picks(feature):
    depth = iota((LANES, LANES), 0).astype(jnp.float32)
    return jnp.where(depth == feature[4:5], 1.0, 0.0).astype(jnp.bfloat16)


def forward_kernel(
    grid_rows, own_rows, grid_planes, slab, below, above, below2, above2, places, count, features,
    field, sent, mass, d1, d2,
):
    first_plane, _, _ = place(grid_rows, own_rows)

    def part(number, plane):
        if plane == 0:
            return below2[number]
        if plane <= 2:
            return below[number, plane - 1]
        if plane <= 4:
            return slab[number, plane - 3]
        if plane <= 6:
            return above[number, plane - 5]
        return above2[number]

    for plane in range(1, PLANES - 1):
        mass[plane - 1] = part(6, plane)

    for pol in range(2):
        def b(plane, pol=pol):
            return tuple(part(3 * pol + c, plane) for c in range(3))

        for plane, here, curled in curl_curl(b, 1, 6, first_plane, grid_planes):
            m = mass[plane - 1]
            for c in range(3):
                heavy = m * here[c]
                d1[0, pol, c, plane - 1] = (
                    (1.0 + MOMENTUM[1]) * here[c] - STEP[0] * (curled[c] + CENTER * heavy)
                )
                d1[1, pol, c, plane - 1] = -STEP[0] * heavy

        def level1(j, pol=pol):
            return lambda plane: tuple(d1[j, pol, c, plane - 1] for c in range(3))

        for j in range(2):
            for plane, here, curled in curl_curl(level1(j), 2, 5, first_plane, grid_planes):
                m = mass[plane - 1]
                for c in range(3):
                    mixed = CENTER * here[c]
                    if j == 1:
                        mixed = mixed + d1[0, pol, c, plane - 1]
                    value = (1.0 + MOMENTUM[2]) * here[c] - STEP[1] * (curled[c] + m * mixed)
                    if j == 0:
                        value = value - MOMENTUM[1] * part(3 * pol + c, plane)
                    d2[j, pol, c, plane - 2] = value
                    if j == 1:
                        d2[2, pol, c, plane - 2] = -STEP[1] * (m * here[c])

        def level2(j, pol=pol):
            return lambda plane: tuple(d2[j, pol, c, plane - 2] for c in range(3))

        for j in range(3):
            for plane, here, curled in curl_curl(level2(j), 3, 4, first_plane, grid_planes):
                m = mass[plane - 1]
                for c in range(3):
                    mixed = CENTER * here[c]
                    if j > 0:
                        mixed = mixed + d2[j - 1, pol, c, plane - 2]
                    last = (1.0 + MOMENTUM[3]) * here[c] - STEP[2] * (curled[c] + m * mixed)
                    value = STEP[2] * here[c]
                    if j < 2:
                        first = d1[j, pol, c, plane - 1]
                        last = last - MOMENTUM[2] * first
                        value = value + STEP[1] * first
                    if j == 0:
                        value = value + STEP[0] * part(3 * pol + c, plane)
                    field[j, pol, c, plane - 3] = value + STEP[3] * last
                    if j == 2:
                        field[3, pol, c, plane - 3] = -(STEP[3] * STEP[2]) * (m * here[c])

    members = sent.shape[0]
    sent[...] = jnp.zeros(sent.shape, jnp.float32)

    def one_chunk(chunk, carry):
        feature = features[chunk]
        weight = row_weights(feature, HALO * WINDOW, 2 * WINDOW)
        depth = depth_picks(feature)
        rows = []
        for j in range(DEGREE):
            for pol in range(2):
                for c in range(2):
                    values = field[j, pol, c].reshape(2 * WINDOW, LANES)
                    at_depth = sum(dot_nn(piece, depth) for piece in parts_of(values))
                    rows.append(jnp.sum(at_depth * weight, axis=0, keepdims=True))
        read = jnp.concatenate(rows, axis=0)
        pieces = jnp.concatenate(parts_of(read), axis=0)
        for block in range(members):
            spread = dot_nn(pieces, picks(places, block, chunk))
            sent[block] += spread[0:16] + spread[16:32] + spread[32:48]
        return carry

    lax.fori_loop(0, count[0], one_chunk, 0)


def forward_solve(slab, below, above, below2, above2, station_parts, grid_rows, members, grid_planes):
    shape = jax.ShapeDtypeStruct
    vmem = pl.BlockSpec(memory_space=pltpu.VMEM)
    smem = pl.BlockSpec(memory_space=pltpu.SMEM)
    blocks = station_parts[0].shape[0]
    return pl.pallas_call(
        lambda *refs: forward_kernel(grid_rows, grid_rows // members, grid_planes, *refs),
        out_shape=(
            shape((DEGREE, 2, 3, 2, WINDOW, LANES), jnp.float32),
            shape((blocks, 4 * DEGREE, LANES), jnp.float32),
            shape((PLANES - 2, WINDOW, LANES), jnp.float32),
        ),
        in_specs=[vmem] * 6 + [smem, vmem],
        out_specs=(vmem, vmem, vmem),
        scratch_shapes=[
            pltpu.VMEM((2, 2, 3, PLANES - 2, WINDOW, LANES), jnp.float32),
            pltpu.VMEM((3, 2, 3, PLANES - 4, WINDOW, LANES), jnp.float32),
        ],
        compiler_params=pltpu.CompilerParams(vmem_limit_bytes=VMEM_LIMIT),
        cost_estimate=pl.CostEstimate(flops=50_000_000, bytes_accessed=3_000_000, transcendentals=0),
        name="forward_solve",
    )(slab, below, above, below2, above2, *station_parts)


def residual_kernel(grid_rows, own_rows, read, data, cells, moments, owned, staged):
    members = data.shape[0]
    total = read[0]
    for member in range(1, read.shape[0]):
        total = total + read[member]
    coefficients = [total[4 * j : 4 * j + 4] for j in range(DEGREE)]
    first = pl.multiple_of(lax.axis_index("space") * LANES, LANES)
    cell = cells[:, pl.ds(first, LANES)]
    y = jnp.min((cell // LANES) % grid_rows, axis=0, keepdims=True)
    mine = (y // own_rows) == lax.axis_index("period")
    sums = [jnp.zeros((4, LANES), jnp.float32) for _ in range(MOMENTS)]
    for member in range(members):
        shift = data[member, 8:9, :]
        delta = shift - CENTER
        value = coefficients[DEGREE - 1]
        for j in range(DEGREE - 2, -1, -1):
            value = value * delta + coefficients[j]
        owned[member] = jnp.where(mine, value, 0.0)
        weight = data[member, 4:8, :]
        term = shift * (weight * weight * (value - data[member, 0:4, :]))
        for number in range(MOMENTS):
            sums[number] = sums[number] + term
            if number + 1 < MOMENTS:
                term = term * delta
    staged[...] = jnp.zeros(staged.shape, jnp.float32)
    for number in range(MOMENTS):
        staged[4 * number : 4 * number + 4, :] = sums[number]
    value = staged[...]
    for member in range(moments.shape[0]):
        moments[member] = value


def residuals(read, data, cells, grid_rows, members):
    shape = jax.ShapeDtypeStruct
    vmem = pl.BlockSpec(memory_space=pltpu.VMEM)
    return pl.pallas_call(
        lambda *refs: residual_kernel(grid_rows, grid_rows // members, *refs),
        out_shape=(
            shape((read.shape[0], 32, LANES), jnp.float32),
            shape((members, 4, LANES), jnp.float32),
        ),
        in_specs=[vmem, vmem, vmem],
        out_specs=(vmem, vmem),
        scratch_shapes=[pltpu.VMEM((32, LANES), jnp.float32)],
        name="residuals",
    )(read, data, cells)


def adjoint_kernel(
    grid_rows, own_rows, grid_planes, periods, moments, places, count, features, mass, field,
    gradient, d0, d1, d2, picked, total,
):
    first_plane, first_row, first_own = place(grid_rows, own_rows)
    blocks = moments.shape[0]
    window_rows = PLANES * WINDOW

    def add_chunk(chunk, fresh):
        feature = features[chunk]
        weight = row_weights(feature, 0, window_rows)
        depth = depth_picks(feature)
        depth = jnp.concatenate([depth, depth], axis=1)
        gathered = jnp.zeros((96, LANES), jnp.float32)
        for block in range(blocks):
            pieces = jnp.concatenate(parts_of(moments[block]), axis=0)
            gathered += dot_nt(pieces, picks(places, block, chunk))
        picked[...] = gathered[0:32] + gathered[32:64] + gathered[64:96]

        def one_field(number, carry):
            values = weight * picked[pl.ds(number, 1), :]
            high = values.astype(jnp.bfloat16)
            low = (values - high.astype(jnp.float32)).astype(jnp.bfloat16)
            placed = dot_nt(jnp.concatenate([high, low], axis=1), depth)
            if fresh:
                d0[number] = placed
            else:
                d0[number] += placed
            return carry

        lax.fori_loop(0, 4 * MOMENTS, one_field, 0)

    add_chunk(0, True)

    def one_chunk(chunk, carry):
        add_chunk(chunk, False)
        return carry

    lax.fori_loop(1, count[0], one_chunk, 0)

    def start(f, c, plane):
        return d0[2 * f + c, plane * WINDOW : (plane + 1) * WINDOW, :]

    def level_one(f, carry):
        def b(plane):
            return start(f, 0, plane), start(f, 1, plane), None

        for plane, here, curled in curl_curl(b, 1, 6, first_plane, grid_planes):
            m = mass[plane - 1]
            for c in range(2):
                mixed = CENTER * here[c] + start(f + 2, c, plane)
                d1[f, c, plane - 1] = (
                    (1.0 + MOMENTUM[1]) * here[c] - STEP[0] * (curled[c] + m * mixed)
                )
            d1[f, 2, plane - 1] = -STEP[0] * curled[2]
        return carry

    lax.fori_loop(0, 2 * (MOMENTS - 1), level_one, 0)

    def level_two(f, carry):
        def get(plane):
            return tuple(d1[f, c, plane - 1] for c in range(3))

        for plane, here, curled in curl_curl(get, 2, 5, first_plane, grid_planes):
            m = mass[plane - 1]
            for c in range(3):
                mixed = CENTER * here[c] + d1[f + 2, c, plane - 1]
                value = (1.0 + MOMENTUM[2]) * here[c] - STEP[1] * (curled[c] + m * mixed)
                if c < 2:
                    value = value - MOMENTUM[1] * start(f, c, plane)
                d2[f, c, plane - 2] = value
        return carry

    lax.fori_loop(0, 2 * (MOMENTS - 2), level_two, 0)

    total[...] = jnp.zeros(total.shape, jnp.float32)

    def level_three(f, carry):
        def get(plane):
            return tuple(d2[f, c, plane - 2] for c in range(3))

        for plane, here, curled in curl_curl(get, 3, 4, first_plane, grid_planes):
            m = mass[plane - 1]
            added = None
            for c in range(3):
                mixed = CENTER * here[c] + d2[f + 2, c, plane - 2]
                first = d1[f, c, plane - 1]
                last = (
                    (1.0 + MOMENTUM[3]) * here[c] - MOMENTUM[2] * first
                    - STEP[2] * (curled[c] + m * mixed)
                )
                value = STEP[1] * first + STEP[2] * here[c] + STEP[3] * last
                if c < 2:
                    value = value + STEP[0] * start(f, c, plane)
                term = value * field[f, c, plane - 3]
                added = term if added is None else added + term
            total[plane - 3] += added
        return carry

    lax.fori_loop(0, 2 * DEGREE, level_three, 0)
    offset = pl.multiple_of(first_own - first_row, 8)
    gradient[...] = total[:, pl.ds(offset, own_rows), :] * (-1.0 / periods)


def adjoint_solve(moments, station_parts, mass, field, grid_rows, members, grid_planes):
    vmem = pl.BlockSpec(memory_space=pltpu.VMEM)
    smem = pl.BlockSpec(memory_space=pltpu.SMEM)
    own_rows = grid_rows // members
    return pl.pallas_call(
        lambda *refs: adjoint_kernel(grid_rows, own_rows, grid_planes, members, *refs),
        out_shape=jax.ShapeDtypeStruct((2, own_rows, LANES), jnp.float32),
        in_specs=[vmem, vmem, smem, vmem, vmem, vmem],
        out_specs=vmem,
        scratch_shapes=[
            pltpu.VMEM((4 * MOMENTS, PLANES * WINDOW, LANES), jnp.float32),
            pltpu.VMEM((2 * (MOMENTS - 1), 3, PLANES - 2, WINDOW, LANES), jnp.float32),
            pltpu.VMEM((2 * (MOMENTS - 2), 3, PLANES - 4, WINDOW, LANES), jnp.float32),
            pltpu.VMEM((32, LANES), jnp.float32),
            pltpu.VMEM((2, WINDOW, LANES), jnp.float32),
        ],
        compiler_params=pltpu.CompilerParams(vmem_limit_bytes=VMEM_LIMIT),
        cost_estimate=pl.CostEstimate(flops=200_000_000, bytes_accessed=3_000_000, transcendentals=0),
        name="adjoint_solve",
    )(moments, *station_parts, mass, field.reshape(2 * DEGREE, 3, 2, WINDOW, LANES))


def shards(source, conductivity, period_shift, site_cells, site_weights, observed, data_weight):
    grid_rows = conductivity.shape[1]
    count = lax.axis_size("space")
    members = lax.axis_size("period")
    grid_planes = conductivity.shape[0] * count
    slab, up, down, up2, down2, data = pack(
        source, conductivity, period_shift, observed, data_weight, members
    )

    def moved(values, by):
        pairs = []
        for i in range(count):
            if 0 <= i + by < count:
                flip = 0 if (i + by) // 2 == i // 2 else 1
                pairs += [(i * members + t, (i + by) * members + (t ^ flip)) for t in range(members)]
        return lax.ppermute(values, ("space", "period"), pairs)

    below = moved(up, 1)
    above = moved(down, -1)
    below2 = moved(up2, 2)
    above2 = moved(down2, -2)
    data = lax.all_to_all(data, "period", 0, 0, tiled=True)
    station_parts = stations(site_cells, site_weights, grid_rows, members)
    field, sent, mass = forward_solve(
        slab, below, above, below2, above2, station_parts, grid_rows, members, grid_planes
    )
    read = lax.all_to_all(sent, "space", 0, 0, tiled=True)
    moments, owned = residuals(read, data, site_cells, grid_rows, members)
    moments = lax.all_to_all(moments, "space", 0, 0, tiled=True)
    moments, owned = lax.optimization_barrier((moments, owned))
    owned = lax.all_to_all(owned, "period", 0, 0, tiled=True)
    gradient = adjoint_solve(moments, station_parts, mass, field, grid_rows, members, grid_planes)
    return jnp.sum(owned, axis=0, keepdims=True), gradient


def solution(mesh):
    placed = (
        P(None, None, "space", None, None),
        P("space", None, None),
        P("period"),
        P(),
        P(),
        P("period", None, "space"),
        P("period", None, "space"),
    )
    return jax.shard_map(
        shards,
        mesh=mesh,
        in_specs=placed,
        out_specs=(P("period", None, "space"), P("space", "period", None)),
        check_vma=False,
    )
```

```python
import jax
import jax.numpy as jnp
from jax import lax
from jax.experimental import pallas as pl
from jax.experimental.pallas import tpu as pltpu
from jax.sharding import PartitionSpec as P

SWEEPS = 4
LOWER_BOUND = 0.05
UPPER_BOUND = 16.0

CENTER = 1.25
HALO = SWEEPS - 1
PLANES = 2 + 2 * HALO
WINDOW = 32
NARROW = 24
DEGREE = SWEEPS
MOMENTS = 2 * SWEEPS - 1
LANES = 128
VMEM_SMALL = 6 * 1024 * 1024
VMEM_LIMIT = 16 * 1024 * 1024


def chebyshev_steps(sweep_count):
    center = 0.5 * (UPPER_BOUND + LOWER_BOUND)
    spread = 0.5 * (UPPER_BOUND - LOWER_BOUND)
    step_sizes = []
    momenta = []
    step_size = 1.0 / center
    for number in range(sweep_count):
        if number == 0:
            momentum = 0.0
        elif number == 1:
            momentum = 0.5 * (spread * step_size) ** 2
        else:
            momentum = (0.5 * spread * step_size) ** 2
        if number > 0:
            step_size = 1.0 / (center - momentum / step_size)
        step_sizes.append(step_size)
        momenta.append(momentum)
    return (step_sizes, momenta)


STEP, MOMENTUM = chebyshev_steps(SWEEPS)


def window_row(member, grid_rows, own_rows):
    first = member * own_rows - (WINDOW - own_rows) // 2
    return pl.multiple_of(jnp.clip(first, 0, grid_rows - WINDOW), 8)


def narrow_row(member, grid_rows, own_rows):
    return jnp.clip(member * own_rows - (NARROW - own_rows) // 2, 0, grid_rows - NARROW)


def first_window_plane():
    return lax.axis_index("space") * 2 - HALO


def iota(shape, dim):
    return lax.broadcasted_iota(jnp.int32, shape, dim)


def parts_of(values):
    high = values.astype(jnp.bfloat16)
    rest = values - high.astype(jnp.float32)
    middle = rest.astype(jnp.bfloat16)
    low = (rest - middle.astype(jnp.float32)).astype(jnp.bfloat16)
    return high, middle, low


def dot_nt(left, right):
    return lax.dot_general(left, right, (((1,), (1,)), ((), ())), preferred_element_type=jnp.float32)


def dot_nn(left, right):
    return lax.dot_general(left, right, (((1,), (0,)), ((), ())), preferred_element_type=jnp.float32)


def next_z(v):
    return jnp.where(iota(v.shape, 1) == v.shape[1] - 1, 0.0, pltpu.roll(v, v.shape[1] - 1, 1))


def last_z(v):
    return jnp.where(iota(v.shape, 1) == 0, 0.0, pltpu.roll(v, 1, 1))


def next_y(v):
    return jnp.where(iota(v.shape, 0) == v.shape[0] - 1, 0.0, pltpu.roll(v, v.shape[0] - 1, 0))


def last_y(v):
    return jnp.where(iota(v.shape, 0) == 0, 0.0, pltpu.roll(v, 1, 0))


def curl_curl(get, first, last, first_plane, planes_in_grid):
    before = None
    here = get(first - 1)
    for plane in range(first - 1, last + 1):
        after = get(plane + 1)
        east, north, down = here
        c2 = next_z(east) - east
        if down is not None:
            c2 = c2 - (after[2] - down)
        c3 = (after[1] - north) - (next_y(east) - east)
        if plane < HALO and plane % 2 == 0:
            inside = jnp.where(first_plane + plane < 0, 0.0, 1.0)
            c2 = c2 * inside
            c3 = c3 * inside
        if plane >= first:
            c1 = north - next_z(north)
            if down is not None:
                c1 = c1 + (next_y(down) - down)
            a1 = (c3 - last_y(c3)) - (c2 - last_z(c2))
            a2 = (c1 - last_z(c1)) - (c3 - before[1])
            a3 = (c2 - before[0]) - (c1 - last_y(c1))
            if plane == HALO + 2:
                inside = jnp.where(first_plane + plane >= planes_in_grid, 0.0, 1.0)
                a1, a2, a3 = a1 * inside, a2 * inside, a3 * inside
            yield plane, here, (a1, a2, a3)
        before = (c2, c3)
        here = after


def pack_kernel(
    grid_rows, own_rows, source, conductivity, shift, observed, weight,
    slab, beside, far_a, far_b, data, sems,
):
    member = lax.axis_index("period")
    pair = (lax.axis_index("space") // 2) % 2
    copies = []
    rows = pl.ds(window_row(member, grid_rows, own_rows), WINDOW)
    for pol in range(2):
        copies.append((source.at[pol, :, :, rows, :], slab.at[pl.ds(3 * pol, 3)]))
    copies.append((conductivity.at[:, rows, :], slab.at[6]))
    rows = pl.ds(window_row(member + 1 - 2 * (member % 2), grid_rows, own_rows), WINDOW)
    for pol in range(2):
        copies.append((source.at[pol, :, :, rows, :], beside.at[pl.ds(3 * pol, 3)]))
        copies.append((source.at[pol, :, 1 - pair, rows, :], far_a.at[pl.ds(3 * pol, 3)]))
        copies.append((source.at[pol, :, pair, rows, :], far_b.at[pl.ds(3 * pol, 3)]))
    copies.append((conductivity.at[:, rows, :], beside.at[6]))
    started = [pltpu.make_async_copy(a, b, sems.at[i]) for i, (a, b) in enumerate(copies)]
    for copy in started:
        copy.start()
    for member in range(data.shape[0]):
        data[member, 0:4, :] = observed[0]
        data[member, 4:8, :] = weight[0]
        data[member, 8:16, :] = jnp.full((8, LANES), shift[0], jnp.float32)
    for copy in started:
        copy.wait()


def pack(source, conductivity, shift, observed, weight, members):
    grid_rows = source.shape[3]
    shape = jax.ShapeDtypeStruct
    hbm = pl.BlockSpec(memory_space=pl.ANY)
    vmem = pl.BlockSpec(memory_space=pltpu.VMEM)
    smem = pl.BlockSpec(memory_space=pltpu.SMEM)
    return pl.pallas_call(
        lambda *refs: pack_kernel(grid_rows, grid_rows // members, *refs),
        out_shape=(shape((7, 2, WINDOW, LANES), jnp.float32),) * 2
        + (shape((6, WINDOW, LANES), jnp.float32),) * 2
        + (shape((members, 16, LANES), jnp.float32),),
        in_specs=[hbm, hbm, smem, vmem, vmem],
        out_specs=(vmem,) * 5,
        scratch_shapes=[pltpu.SemaphoreType.DMA((10,))],
        compiler_params=pltpu.CompilerParams(vmem_limit_bytes=VMEM_SMALL),
        name="pack",
    )(source, conductivity, shift, observed, weight)


def stations_kernel(grid_rows, own_rows, cells, weights, places, count, features, marks, staged):
    member = lax.axis_index("period")
    first_own = member * own_rows
    first_row = window_row(member, grid_rows, own_rows)
    first_narrow = narrow_row(member, grid_rows, own_rows)
    plane_size = grid_rows * LANES
    cell = cells[...]
    x = cell // plane_size - first_window_plane()
    y = (cell // LANES) % grid_rows
    reached = (
        (x >= 0) & (x < PLANES)
        & (y >= first_own - HALO - 1) & (y < first_own + own_rows + HALO + 1)
    )
    row = jnp.where(reached, x * WINDOW + y - first_row, 0).astype(jnp.float32)
    narrow = jnp.where(reached, x * NARROW + y - first_narrow, 0).astype(jnp.float32)
    weight = jnp.where(reached, weights[...], 0.0)
    present = jnp.max(jnp.where(reached, 1.0, 0.0), axis=0, keepdims=True)
    blocks = cell.shape[1] // LANES
    staged[...] = jnp.zeros(staged.shape, jnp.float32)
    staged[0:4, :] = row
    staged[4:8, :] = (cell % LANES).astype(jnp.float32)
    staged[20:24, :] = narrow
    for number, part in enumerate(parts_of(weight)):
        staged[8 + 4 * number : 12 + 4 * number, :] = part.astype(jnp.float32)
    for block in range(blocks):
        marks[block : block + 1, :] = present[:, block * LANES : (block + 1) * LANES]
    mark = marks[...]
    square = (LANES, LANES)
    upto = jnp.where(iota(square, 0) <= iota(square, 1), 1.0, 0.0).astype(jnp.bfloat16)
    inner = dot_nn(mark.astype(jnp.bfloat16), upto)
    totals = dot_nn(mark.astype(jnp.bfloat16), jnp.ones(square, jnp.bfloat16))
    earlier = jnp.where(iota((blocks, blocks), 0) > iota((blocks, blocks), 1), 1.0, 0.0)
    offsets = dot_nn(earlier.astype(jnp.bfloat16), totals.astype(jnp.bfloat16))
    places[...] = jnp.where(mark > 0.0, inner + offsets - 1.0, -1.0).astype(jnp.int32)
    chunks = (jnp.sum(mark).astype(jnp.int32) + LANES - 1) // LANES
    count[0] = chunks

    def one_chunk(chunk, carry):
        gathered = jnp.zeros((staged.shape[0], LANES), jnp.float32)
        for block in range(blocks):
            feature = staged[:, block * LANES : (block + 1) * LANES].astype(jnp.bfloat16)
            gathered += dot_nt(feature, picks(places, block, chunk))
        features[chunk] = gathered
        return carry

    features[0] = jnp.zeros(features.shape[1:], jnp.float32)
    lax.fori_loop(0, chunks, one_chunk, 0)


def picks(places, block, chunk):
    wanted = places[block : block + 1, :] - chunk * LANES
    return jnp.where(iota((LANES, LANES), 0) == wanted, 1.0, 0.0).astype(jnp.bfloat16)


def stations(cells, weights, grid_rows, members):
    blocks = cells.shape[1] // LANES
    shape = jax.ShapeDtypeStruct
    vmem = pl.BlockSpec(memory_space=pltpu.VMEM)
    return pl.pallas_call(
        lambda *refs: stations_kernel(grid_rows, grid_rows // members, *refs),
        out_shape=(
            shape((blocks, LANES), jnp.int32),
            shape((1,), jnp.int32),
            shape((blocks, 32, LANES), jnp.float32),
        ),
        in_specs=[vmem, vmem],
        out_specs=(vmem, pl.BlockSpec(memory_space=pltpu.SMEM), vmem),
        scratch_shapes=[
            pltpu.VMEM((blocks, LANES), jnp.float32),
            pltpu.VMEM((32, cells.shape[1]), jnp.float32),
        ],
        compiler_params=pltpu.CompilerParams(vmem_limit_bytes=VMEM_LIMIT),
        cost_estimate=pl.CostEstimate(flops=10_000_000, bytes_accessed=200_000, transcendentals=0),
        name="stations",
    )(cells, weights)


def row_weights(feature, field, first, count):
    rows = (iota((count, LANES), 0) + first).astype(jnp.float32)
    total = jnp.zeros((count, LANES), jnp.float32)
    for q in range(4):
        weight = feature[8 + q : 9 + q] + feature[12 + q : 13 + q] + feature[16 + q : 17 + q]
        total += jnp.where(rows == feature[field + q : field + q + 1], weight, 0.0)
    return total


def depth_picks(feature):
    depth = iota((LANES, LANES), 0).astype(jnp.float32)
    return jnp.where(depth == feature[4:5], 1.0, 0.0).astype(jnp.bfloat16)


def forward_kernel(
    grid_rows, own_rows, grid_planes, slab, mate, beside, far_a, far_b, places, count, features,
    field, sent, mass, window, d1, d2,
):
    first_plane = first_window_plane()
    even = lax.axis_index("space") % 2 == 0
    lower = (lax.axis_index("space") // 2) % 2 == 0
    for plane in range(2):
        here, there = mate[:, plane], beside[:, plane]
        window[:, 1 + plane] = jnp.where(even, there, here)
        window[:, 3 + plane] = slab[:, plane]
        window[:, 5 + plane] = jnp.where(even, here, there)
    window[0:6, 0] = jnp.where(lower, far_b[...], far_a[...])
    window[0:6, PLANES - 1] = jnp.where(lower, far_a[...], far_b[...])
    mass[...] = window[6, 1 : PLANES - 1]

    def part(number, plane):
        return window[number, plane]

    for pol in range(2):
        def b(plane, pol=pol):
            return tuple(part(3 * pol + c, plane) for c in range(3))

        for plane, here, curled in curl_curl(b, 1, 6, first_plane, grid_planes):
            m = mass[plane - 1]
            for c in range(3):
                heavy = m * here[c]
                d1[0, pol, c, plane - 1] = (
                    (1.0 + MOMENTUM[1]) * here[c] - STEP[0] * (curled[c] + CENTER * heavy)
                )
                d1[1, pol, c, plane - 1] = -STEP[0] * heavy

        def level1(j, pol=pol):
            return lambda plane: tuple(d1[j, pol, c, plane - 1] for c in range(3))

        for j in range(2):
            for plane, here, curled in curl_curl(level1(j), 2, 5, first_plane, grid_planes):
                m = mass[plane - 1]
                for c in range(3):
                    mixed = CENTER * here[c]
                    if j == 1:
                        mixed = mixed + d1[0, pol, c, plane - 1]
                    value = (1.0 + MOMENTUM[2]) * here[c] - STEP[1] * (curled[c] + m * mixed)
                    if j == 0:
                        value = value - MOMENTUM[1] * part(3 * pol + c, plane)
                    d2[j, pol, c, plane - 2] = value
                    if j == 1:
                        d2[2, pol, c, plane - 2] = -STEP[1] * (m * here[c])

        def level2(j, pol=pol):
            return lambda plane: tuple(d2[j, pol, c, plane - 2] for c in range(3))

        for j in range(3):
            for plane, here, curled in curl_curl(level2(j), 3, 4, first_plane, grid_planes):
                m = mass[plane - 1]
                for c in range(3):
                    mixed = CENTER * here[c]
                    if j > 0:
                        mixed = mixed + d2[j - 1, pol, c, plane - 2]
                    last = (1.0 + MOMENTUM[3]) * here[c] - STEP[2] * (curled[c] + m * mixed)
                    value = STEP[2] * here[c]
                    if j < 2:
                        first = d1[j, pol, c, plane - 1]
                        last = last - MOMENTUM[2] * first
                        value = value + STEP[1] * first
                    if j == 0:
                        value = value + STEP[0] * part(3 * pol + c, plane)
                    field[j, pol, c, plane - 3] = value + STEP[3] * last
                    if j == 2:
                        field[3, pol, c, plane - 3] = -(STEP[3] * STEP[2]) * (m * here[c])

    members = sent.shape[0]
    sent[...] = jnp.zeros(sent.shape, jnp.float32)

    def one_chunk(chunk, carry):
        feature = features[chunk]
        weight = row_weights(feature, 0, HALO * WINDOW, 2 * WINDOW)
        depth = depth_picks(feature)
        rows = []
        for j in range(DEGREE):
            for pol in range(2):
                for c in range(2):
                    values = field[j, pol, c].reshape(2 * WINDOW, LANES)
                    at_depth = sum(dot_nn(piece, depth) for piece in parts_of(values))
                    rows.append(jnp.sum(at_depth * weight, axis=0, keepdims=True))
        read = jnp.concatenate(rows, axis=0)
        pieces = jnp.concatenate(parts_of(read), axis=0)
        for block in range(members):
            spread = dot_nn(pieces, picks(places, block, chunk))
            sent[block] += spread[0:16] + spread[16:32] + spread[32:48]
        return carry

    lax.fori_loop(0, count[0], one_chunk, 0)


def forward_solve(windows, station_parts, grid_rows, members, grid_planes):
    shape = jax.ShapeDtypeStruct
    vmem = pl.BlockSpec(memory_space=pltpu.VMEM)
    smem = pl.BlockSpec(memory_space=pltpu.SMEM)
    blocks = station_parts[0].shape[0]
    return pl.pallas_call(
        lambda *refs: forward_kernel(grid_rows, grid_rows // members, grid_planes, *refs),
        out_shape=(
            shape((DEGREE, 2, 3, 2, WINDOW, LANES), jnp.float32),
            shape((blocks, 4 * DEGREE, LANES), jnp.float32),
            shape((PLANES - 2, WINDOW, LANES), jnp.float32),
        ),
        in_specs=[vmem] * 6 + [smem, vmem],
        out_specs=(vmem, vmem, vmem),
        scratch_shapes=[
            pltpu.VMEM((7, PLANES, WINDOW, LANES), jnp.float32),
            pltpu.VMEM((2, 2, 3, PLANES - 2, WINDOW, LANES), jnp.float32),
            pltpu.VMEM((3, 2, 3, PLANES - 4, WINDOW, LANES), jnp.float32),
        ],
        compiler_params=pltpu.CompilerParams(vmem_limit_bytes=VMEM_LIMIT),
        cost_estimate=pl.CostEstimate(flops=50_000_000, bytes_accessed=3_000_000, transcendentals=0),
        name="forward_solve",
    )(*windows, *station_parts)


def residual_kernel(grid_rows, own_rows, read, data, cells, moments, owned, staged):
    members = data.shape[0]
    total = read[0]
    for member in range(1, read.shape[0]):
        total = total + read[member]
    coefficients = [total[4 * j : 4 * j + 4] for j in range(DEGREE)]
    first = pl.multiple_of(lax.axis_index("space") * LANES, LANES)
    cell = cells[:, pl.ds(first, LANES)]
    y = jnp.min((cell // LANES) % grid_rows, axis=0, keepdims=True)
    mine = (y // own_rows) == lax.axis_index("period")
    sums = [jnp.zeros((4, LANES), jnp.float32) for _ in range(MOMENTS)]
    for member in range(members):
        shift = data[member, 8:9, :]
        delta = shift - CENTER
        value = coefficients[DEGREE - 1]
        for j in range(DEGREE - 2, -1, -1):
            value = value * delta + coefficients[j]
        owned[member] = jnp.where(mine, value, 0.0)
        weight = data[member, 4:8, :]
        term = shift * (weight * weight * (value - data[member, 0:4, :]))
        for number in range(MOMENTS):
            sums[number] = sums[number] + term
            if number + 1 < MOMENTS:
                term = term * delta
    staged[...] = jnp.zeros(staged.shape, jnp.float32)
    for number in range(MOMENTS):
        staged[4 * number : 4 * number + 4, :] = sums[number]
    value = staged[...]
    for member in range(moments.shape[0]):
        moments[member] = value


def residuals(read, data, cells, grid_rows, members):
    shape = jax.ShapeDtypeStruct
    vmem = pl.BlockSpec(memory_space=pltpu.VMEM)
    return pl.pallas_call(
        lambda *refs: residual_kernel(grid_rows, grid_rows // members, *refs),
        out_shape=(
            shape((read.shape[0], 32, LANES), jnp.float32),
            shape((members, 4, LANES), jnp.float32),
        ),
        in_specs=[vmem, vmem, vmem],
        out_specs=(vmem, vmem),
        scratch_shapes=[pltpu.VMEM((32, LANES), jnp.float32)],
        compiler_params=pltpu.CompilerParams(vmem_limit_bytes=VMEM_SMALL),
        name="residuals",
    )(read, data, cells)


def adjoint_kernel(
    grid_rows, own_rows, grid_planes, periods, moments, places, count, features, mass, field,
    gradient, d0, d1, d2, picked, total,
):
    first_plane = first_window_plane()
    member = lax.axis_index("period")
    first_row = narrow_row(member, grid_rows, own_rows)
    inner = pl.ds(first_row - window_row(member, grid_rows, own_rows), NARROW)
    own = pl.ds(member * own_rows - first_row, own_rows)
    blocks = moments.shape[0]
    window_rows = PLANES * NARROW

    def add_chunk(chunk, fresh):
        feature = features[chunk]
        weight = row_weights(feature, 20, 0, window_rows)
        depth = depth_picks(feature)
        depth = jnp.concatenate([depth, depth], axis=1)
        gathered = jnp.zeros((96, LANES), jnp.float32)
        for block in range(blocks):
            pieces = jnp.concatenate(parts_of(moments[block]), axis=0)
            gathered += dot_nt(pieces, picks(places, block, chunk))
        picked[...] = gathered[0:32] + gathered[32:64] + gathered[64:96]

        def one_field(number, carry):
            values = weight * picked[pl.ds(number, 1), :]
            high = values.astype(jnp.bfloat16)
            low = (values - high.astype(jnp.float32)).astype(jnp.bfloat16)
            placed = dot_nt(jnp.concatenate([high, low], axis=1), depth)
            if fresh:
                d0[number] = placed
            else:
                d0[number] += placed
            return carry

        lax.fori_loop(0, 4 * MOMENTS, one_field, 0, unroll=MOMENTS)

    add_chunk(0, True)

    def one_chunk(chunk, carry):
        add_chunk(chunk, False)
        return carry

    lax.fori_loop(1, count[0], one_chunk, 0)

    def start(f, c, plane):
        return d0[2 * f + c, plane * NARROW : (plane + 1) * NARROW, :]

    def level_one(f, carry):
        def b(plane):
            return start(f, 0, plane), start(f, 1, plane), None

        for plane, here, curled in curl_curl(b, 1, 6, first_plane, grid_planes):
            m = mass[plane - 1, inner, :]
            for c in range(2):
                mixed = CENTER * here[c] + start(f + 2, c, plane)
                d1[f, c, plane - 1] = (
                    (1.0 + MOMENTUM[1]) * here[c] - STEP[0] * (curled[c] + m * mixed)
                )
            d1[f, 2, plane - 1] = -STEP[0] * curled[2]
        return carry

    lax.fori_loop(0, 2 * (MOMENTS - 1), level_one, 0)

    def level_two(f, carry):
        def get(plane):
            return tuple(d1[f, c, plane - 1] for c in range(3))

        for plane, here, curled in curl_curl(get, 2, 5, first_plane, grid_planes):
            m = mass[plane - 1, inner, :]
            for c in range(3):
                mixed = CENTER * here[c] + d1[f + 2, c, plane - 1]
                value = (1.0 + MOMENTUM[2]) * here[c] - STEP[1] * (curled[c] + m * mixed)
                if c < 2:
                    value = value - MOMENTUM[1] * start(f, c, plane)
                d2[f, c, plane - 2] = value
        return carry

    lax.fori_loop(0, 2 * (MOMENTS - 2), level_two, 0)

    total[...] = jnp.zeros(total.shape, jnp.float32)

    def level_three(f, carry):
        def get(plane):
            return tuple(d2[f, c, plane - 2] for c in range(3))

        for plane, here, curled in curl_curl(get, 3, 4, first_plane, grid_planes):
            m = mass[plane - 1, inner, :]
            added = None
            for c in range(3):
                mixed = CENTER * here[c] + d2[f + 2, c, plane - 2]
                first = d1[f, c, plane - 1]
                last = (
                    (1.0 + MOMENTUM[3]) * here[c] - MOMENTUM[2] * first
                    - STEP[2] * (curled[c] + m * mixed)
                )
                value = STEP[1] * first + STEP[2] * here[c] + STEP[3] * last
                if c < 2:
                    value = value + STEP[0] * start(f, c, plane)
                term = value * field[f, c, plane - 3, inner, :]
                added = term if added is None else added + term
            total[plane - 3] += added
        return carry

    lax.fori_loop(0, 2 * DEGREE, level_three, 0)
    gradient[...] = total[:, own, :] * (-1.0 / periods)


def adjoint_solve(moments, station_parts, mass, field, grid_rows, members, grid_planes):
    vmem = pl.BlockSpec(memory_space=pltpu.VMEM)
    smem = pl.BlockSpec(memory_space=pltpu.SMEM)
    own_rows = grid_rows // members
    return pl.pallas_call(
        lambda *refs: adjoint_kernel(grid_rows, own_rows, grid_planes, members, *refs),
        out_shape=jax.ShapeDtypeStruct((2, own_rows, LANES), jnp.float32),
        in_specs=[vmem, vmem, smem, vmem, vmem, vmem],
        out_specs=vmem,
        scratch_shapes=[
            pltpu.VMEM((4 * MOMENTS, PLANES * NARROW, LANES), jnp.float32),
            pltpu.VMEM((2 * (MOMENTS - 1), 3, PLANES - 2, NARROW, LANES), jnp.float32),
            pltpu.VMEM((2 * (MOMENTS - 2), 3, PLANES - 4, NARROW, LANES), jnp.float32),
            pltpu.VMEM((32, LANES), jnp.float32),
            pltpu.VMEM((2, NARROW, LANES), jnp.float32),
        ],
        compiler_params=pltpu.CompilerParams(vmem_limit_bytes=VMEM_LIMIT),
        cost_estimate=pl.CostEstimate(flops=200_000_000, bytes_accessed=3_000_000, transcendentals=0),
        name="adjoint_solve",
    )(moments, *station_parts, mass, field.reshape(2 * DEGREE, 3, 2, WINDOW, LANES))


def shards(source, conductivity, period_shift, site_cells, site_weights, observed, data_weight):
    grid_rows = conductivity.shape[1]
    count = lax.axis_size("space")
    members = lax.axis_size("period")
    grid_planes = conductivity.shape[0] * count
    slab, beside, far_a, far_b, data = pack(
        source, conductivity, period_shift, observed, data_weight, members
    )

    def swapped(values, partner):
        pairs = []
        for i in range(count):
            j = partner(i)
            flip = 0 if i // 2 == j // 2 else 1
            if 0 <= j < count:
                pairs += [(i * members + t, j * members + (t ^ flip)) for t in range(members)]
        return lax.ppermute(values, ("space", "period"), pairs)

    windows = (
        slab,
        swapped(slab, lambda i: i ^ 1),
        swapped(beside, lambda i: i + 1 if i % 2 else i - 1),
        swapped(far_a, lambda i: i ^ 2),
        swapped(far_b, lambda i: i + 2 if i & 2 else i - 2),
    )
    data = lax.all_to_all(data, "period", 0, 0, tiled=True)
    station_parts = stations(site_cells, site_weights, grid_rows, members)
    field, sent, mass = forward_solve(windows, station_parts, grid_rows, members, grid_planes)
    read = lax.all_to_all(sent, "space", 0, 0, tiled=True)
    moments, owned = residuals(read, data, site_cells, grid_rows, members)
    moments = lax.all_to_all(moments, "space", 0, 0, tiled=True)
    moments, owned = lax.optimization_barrier((moments, owned))
    owned = lax.all_to_all(owned, "period", 0, 0, tiled=True)
    gradient = adjoint_solve(moments, station_parts, mass, field, grid_rows, members, grid_planes)
    return jnp.sum(owned, axis=0, keepdims=True), gradient


def solution(mesh):
    placed = (
        P(None, None, "space", None, None),
        P("space", None, None),
        P("period"),
        P(),
        P(),
        P("period", None, "space"),
        P("period", None, "space"),
    )
    return jax.shard_map(
        shards,
        mesh=mesh,
        in_specs=placed,
        out_specs=(P("period", None, "space"), P("space", "period", None)),
        check_vma=False,
    )
```

```python
import jax
import jax.numpy as jnp
from jax import lax
from jax.experimental import pallas as pl
from jax.experimental.pallas import tpu as pltpu
from jax.sharding import PartitionSpec as P

SWEEPS = 4
LOWER_BOUND = 0.05
UPPER_BOUND = 16.0

CENTER = 1.25
HALO = SWEEPS - 1
PLANES = 2 + 2 * HALO
WINDOW = 32
NARROW = 24
DEGREE = SWEEPS
MOMENTS = 2 * SWEEPS - 1
LANES = 128
VMEM_SMALL = 6 * 1024 * 1024
VMEM_LIMIT = 16 * 1024 * 1024


def chebyshev_steps(sweep_count):
    center = 0.5 * (UPPER_BOUND + LOWER_BOUND)
    spread = 0.5 * (UPPER_BOUND - LOWER_BOUND)
    step_sizes = []
    momenta = []
    step_size = 1.0 / center
    for number in range(sweep_count):
        if number == 0:
            momentum = 0.0
        elif number == 1:
            momentum = 0.5 * (spread * step_size) ** 2
        else:
            momentum = (0.5 * spread * step_size) ** 2
        if number > 0:
            step_size = 1.0 / (center - momentum / step_size)
        step_sizes.append(step_size)
        momenta.append(momentum)
    return (step_sizes, momenta)


STEP, MOMENTUM = chebyshev_steps(SWEEPS)


def window_row(member, grid_rows, own_rows):
    first = member * own_rows - (WINDOW - own_rows) // 2
    return pl.multiple_of(jnp.clip(first, 0, grid_rows - WINDOW), 8)


def narrow_row(member, grid_rows, own_rows):
    return jnp.clip(member * own_rows - (NARROW - own_rows) // 2, 0, grid_rows - NARROW)


def first_window_plane():
    return lax.axis_index("space") * 2 - HALO


def iota(shape, dim):
    return lax.broadcasted_iota(jnp.int32, shape, dim)


def parts_of(values):
    high = values.astype(jnp.bfloat16)
    rest = values - high.astype(jnp.float32)
    middle = rest.astype(jnp.bfloat16)
    low = (rest - middle.astype(jnp.float32)).astype(jnp.bfloat16)
    return high, middle, low


def dot_nt(left, right):
    return lax.dot_general(left, right, (((1,), (1,)), ((), ())), preferred_element_type=jnp.float32)


def dot_nn(left, right):
    return lax.dot_general(left, right, (((1,), (0,)), ((), ())), preferred_element_type=jnp.float32)


def next_z(v):
    return jnp.where(iota(v.shape, 1) == v.shape[1] - 1, 0.0, pltpu.roll(v, v.shape[1] - 1, 1))


def last_z(v):
    return jnp.where(iota(v.shape, 1) == 0, 0.0, pltpu.roll(v, 1, 1))


def next_y(v):
    return jnp.where(iota(v.shape, 0) == v.shape[0] - 1, 0.0, pltpu.roll(v, v.shape[0] - 1, 0))


def last_y(v):
    return jnp.where(iota(v.shape, 0) == 0, 0.0, pltpu.roll(v, 1, 0))


def curl_curl(get, first, last, first_plane, planes_in_grid):
    before = None
    here = get(first - 1)
    for plane in range(first - 1, last + 1):
        after = get(plane + 1)
        east, north, down = here
        c2 = next_z(east) - east
        if down is not None:
            c2 = c2 - (after[2] - down)
        c3 = (after[1] - north) - (next_y(east) - east)
        if plane < HALO and plane % 2 == 0:
            inside = jnp.where(first_plane + plane < 0, 0.0, 1.0)
            c2 = c2 * inside
            c3 = c3 * inside
        if plane >= first:
            c1 = north - next_z(north)
            if down is not None:
                c1 = c1 + (next_y(down) - down)
            a1 = (c3 - last_y(c3)) - (c2 - last_z(c2))
            a2 = (c1 - last_z(c1)) - (c3 - before[1])
            a3 = (c2 - before[0]) - (c1 - last_y(c1))
            if plane == HALO + 2:
                inside = jnp.where(first_plane + plane >= planes_in_grid, 0.0, 1.0)
                a1, a2, a3 = a1 * inside, a2 * inside, a3 * inside
            yield plane, here, (a1, a2, a3)
        before = (c2, c3)
        here = after


def pack_kernel(
    grid_rows, own_rows, source, conductivity, shift, observed, weight,
    slab, beside, far_a, far_b, data, pairs, sems,
):
    member = lax.axis_index("period")
    pair = (lax.axis_index("space") // 2) % 2
    copies = [(observed.at[0], pairs.at[0]), (weight.at[0], pairs.at[1])]
    rows = pl.ds(window_row(member, grid_rows, own_rows), WINDOW)
    for pol in range(2):
        copies.append((source.at[pol, :, :, rows, :], slab.at[pl.ds(3 * pol, 3)]))
    copies.append((conductivity.at[:, rows, :], slab.at[6]))
    rows = pl.ds(window_row(member + 1 - 2 * (member % 2), grid_rows, own_rows), WINDOW)
    for pol in range(2):
        copies.append((source.at[pol, :, :, rows, :], beside.at[pl.ds(3 * pol, 3)]))
        copies.append((source.at[pol, :, 1 - pair, rows, :], far_a.at[pl.ds(3 * pol, 3)]))
        copies.append((source.at[pol, :, pair, rows, :], far_b.at[pl.ds(3 * pol, 3)]))
    copies.append((conductivity.at[:, rows, :], beside.at[6]))
    started = [pltpu.make_async_copy(a, b, sems.at[i]) for i, (a, b) in enumerate(copies)]
    for copy in started:
        copy.start()
    for copy in started:
        copy.wait()
    for member in range(data.shape[0]):
        data[member, 0:4, :] = pairs[0]
        data[member, 4:8, :] = pairs[1]
        data[member, 8:16, :] = jnp.full((8, LANES), shift[0], jnp.float32)


def pack(source, conductivity, shift, observed, weight, members):
    grid_rows = source.shape[3]
    shape = jax.ShapeDtypeStruct
    hbm = pl.BlockSpec(memory_space=pltpu.HBM)
    vmem = pl.BlockSpec(memory_space=pltpu.VMEM)
    smem = pl.BlockSpec(memory_space=pltpu.SMEM)
    return pl.pallas_call(
        lambda *refs: pack_kernel(grid_rows, grid_rows // members, *refs),
        out_shape=(shape((7, 2, WINDOW, LANES), jnp.float32),) * 2
        + (shape((6, WINDOW, LANES), jnp.float32),) * 2
        + (shape((members, 16, LANES), jnp.float32),),
        in_specs=[hbm, hbm, smem, hbm, hbm],
        out_specs=(vmem,) * 5,
        scratch_shapes=[pltpu.VMEM((2, 4, LANES), jnp.float32), pltpu.SemaphoreType.DMA((12,))],
        compiler_params=pltpu.CompilerParams(vmem_limit_bytes=62 * 1024 * 1024),
        name="pack",
    )(source, conductivity, shift, observed, weight)


def stations_kernel(grid_rows, own_rows, cells, weights, places, count, features, marks, staged):
    member = lax.axis_index("period")
    first_own = member * own_rows
    first_row = window_row(member, grid_rows, own_rows)
    first_narrow = narrow_row(member, grid_rows, own_rows)
    plane_size = grid_rows * LANES
    cell = cells[...]
    x = cell // plane_size - first_window_plane()
    y = (cell // LANES) % grid_rows
    reached = (
        (x >= 0) & (x < PLANES)
        & (y >= first_own - HALO - 1) & (y < first_own + own_rows + HALO + 1)
    )
    row = jnp.where(reached, x * WINDOW + y - first_row, 0).astype(jnp.float32)
    narrow = jnp.where(reached, x * NARROW + y - first_narrow, 0).astype(jnp.float32)
    weight = jnp.where(reached, weights[...], 0.0)
    present = jnp.max(jnp.where(reached, 1.0, 0.0), axis=0, keepdims=True)
    blocks = cell.shape[1] // LANES
    staged[...] = jnp.zeros(staged.shape, jnp.float32)
    staged[0:4, :] = row
    staged[4:8, :] = (cell % LANES).astype(jnp.float32)
    staged[20:24, :] = narrow
    for number, part in enumerate(parts_of(weight)):
        staged[8 + 4 * number : 12 + 4 * number, :] = part.astype(jnp.float32)
    for block in range(blocks):
        marks[block : block + 1, :] = present[:, block * LANES : (block + 1) * LANES]
    mark = marks[...]
    square = (LANES, LANES)
    upto = jnp.where(iota(square, 0) <= iota(square, 1), 1.0, 0.0).astype(jnp.bfloat16)
    inner = dot_nn(mark.astype(jnp.bfloat16), upto)
    totals = dot_nn(mark.astype(jnp.bfloat16), jnp.ones(square, jnp.bfloat16))
    earlier = jnp.where(iota((blocks, blocks), 0) > iota((blocks, blocks), 1), 1.0, 0.0)
    offsets = dot_nn(earlier.astype(jnp.bfloat16), totals.astype(jnp.bfloat16))
    places[...] = jnp.where(mark > 0.0, inner + offsets - 1.0, -1.0).astype(jnp.int32)
    chunks = (jnp.sum(mark).astype(jnp.int32) + LANES - 1) // LANES
    count[0] = chunks

    def one_chunk(chunk, carry):
        gathered = jnp.zeros((staged.shape[0], LANES), jnp.float32)
        for block in range(blocks):
            feature = staged[:, block * LANES : (block + 1) * LANES].astype(jnp.bfloat16)
            gathered += dot_nt(feature, picks(places, block, chunk))
        features[chunk] = gathered
        return carry

    features[0] = jnp.zeros(features.shape[1:], jnp.float32)
    lax.fori_loop(0, chunks, one_chunk, 0)


def picks(places, block, chunk):
    wanted = places[block : block + 1, :] - chunk * LANES
    return jnp.where(iota((LANES, LANES), 0) == wanted, 1.0, 0.0).astype(jnp.bfloat16)


def stations(cells, weights, grid_rows, members):
    blocks = cells.shape[1] // LANES
    shape = jax.ShapeDtypeStruct
    vmem = pl.BlockSpec(memory_space=pltpu.VMEM)
    return pl.pallas_call(
        lambda *refs: stations_kernel(grid_rows, grid_rows // members, *refs),
        out_shape=(
            shape((blocks, LANES), jnp.int32),
            shape((1,), jnp.int32),
            shape((blocks, 32, LANES), jnp.float32),
        ),
        in_specs=[vmem, vmem],
        out_specs=(vmem, pl.BlockSpec(memory_space=pltpu.SMEM), vmem),
        scratch_shapes=[
            pltpu.VMEM((blocks, LANES), jnp.float32),
            pltpu.VMEM((32, cells.shape[1]), jnp.float32),
        ],
        compiler_params=pltpu.CompilerParams(vmem_limit_bytes=VMEM_LIMIT),
        cost_estimate=pl.CostEstimate(flops=10_000_000, bytes_accessed=200_000, transcendentals=0),
        name="stations",
    )(cells, weights)


def row_weights(feature, field, first, count):
    rows = (iota((count, LANES), 0) + first).astype(jnp.float32)
    total = jnp.zeros((count, LANES), jnp.float32)
    for q in range(4):
        weight = feature[8 + q : 9 + q] + feature[12 + q : 13 + q] + feature[16 + q : 17 + q]
        total += jnp.where(rows == feature[field + q : field + q + 1], weight, 0.0)
    return total


def depth_picks(feature):
    depth = iota((LANES, LANES), 0).astype(jnp.float32)
    return jnp.where(depth == feature[4:5], 1.0, 0.0).astype(jnp.bfloat16)


def forward_kernel(
    grid_rows, own_rows, grid_planes, slab, mate, beside, far_a, far_b, places, count, features,
    field, sent, mass, window, d1, d2,
):
    first_plane = first_window_plane()
    even = lax.axis_index("space") % 2 == 0
    lower = (lax.axis_index("space") // 2) % 2 == 0
    for plane in range(2):
        here, there = mate[:, plane], beside[:, plane]
        window[:, 1 + plane] = jnp.where(even, there, here)
        window[:, 3 + plane] = slab[:, plane]
        window[:, 5 + plane] = jnp.where(even, here, there)
    window[0:6, 0] = jnp.where(lower, far_b[...], far_a[...])
    window[0:6, PLANES - 1] = jnp.where(lower, far_a[...], far_b[...])
    mass[...] = window[6, 1 : PLANES - 1]

    def part(number, plane):
        return window[number, plane]

    for pol in range(2):
        def b(plane, pol=pol):
            return tuple(part(3 * pol + c, plane) for c in range(3))

        for plane, here, curled in curl_curl(b, 1, 6, first_plane, grid_planes):
            m = mass[plane - 1]
            for c in range(3):
                heavy = m * here[c]
                d1[0, pol, c, plane - 1] = (
                    (1.0 + MOMENTUM[1]) * here[c] - STEP[0] * (curled[c] + CENTER * heavy)
                )
                d1[1, pol, c, plane - 1] = -STEP[0] * heavy

        def level1(j, pol=pol):
            return lambda plane: tuple(d1[j, pol, c, plane - 1] for c in range(3))

        for j in range(2):
            for plane, here, curled in curl_curl(level1(j), 2, 5, first_plane, grid_planes):
                m = mass[plane - 1]
                for c in range(3):
                    mixed = CENTER * here[c]
                    if j == 1:
                        mixed = mixed + d1[0, pol, c, plane - 1]
                    value = (1.0 + MOMENTUM[2]) * here[c] - STEP[1] * (curled[c] + m * mixed)
                    if j == 0:
                        value = value - MOMENTUM[1] * part(3 * pol + c, plane)
                    d2[j, pol, c, plane - 2] = value
                    if j == 1:
                        d2[2, pol, c, plane - 2] = -STEP[1] * (m * here[c])

        def level2(j, pol=pol):
            return lambda plane: tuple(d2[j, pol, c, plane - 2] for c in range(3))

        for j in range(3):
            for plane, here, curled in curl_curl(level2(j), 3, 4, first_plane, grid_planes):
                m = mass[plane - 1]
                for c in range(3):
                    mixed = CENTER * here[c]
                    if j > 0:
                        mixed = mixed + d2[j - 1, pol, c, plane - 2]
                    last = (1.0 + MOMENTUM[3]) * here[c] - STEP[2] * (curled[c] + m * mixed)
                    value = STEP[2] * here[c]
                    if j < 2:
                        first = d1[j, pol, c, plane - 1]
                        last = last - MOMENTUM[2] * first
                        value = value + STEP[1] * first
                    if j == 0:
                        value = value + STEP[0] * part(3 * pol + c, plane)
                    field[j, pol, c, plane - 3] = value + STEP[3] * last
                    if j == 2:
                        field[3, pol, c, plane - 3] = -(STEP[3] * STEP[2]) * (m * here[c])

    members = sent.shape[0]
    sent[...] = jnp.zeros(sent.shape, jnp.float32)

    def one_chunk(chunk, carry):
        feature = features[chunk]
        weight = row_weights(feature, 0, HALO * WINDOW, 2 * WINDOW)
        depth = depth_picks(feature)
        rows = []
        for j in range(DEGREE):
            for pol in range(2):
                for c in range(2):
                    values = field[j, pol, c].reshape(2 * WINDOW, LANES)
                    at_depth = sum(dot_nn(piece, depth) for piece in parts_of(values))
                    rows.append(jnp.sum(at_depth * weight, axis=0, keepdims=True))
        read = jnp.concatenate(rows, axis=0)
        pieces = jnp.concatenate(parts_of(read), axis=0)
        for block in range(members):
            spread = dot_nn(pieces, picks(places, block, chunk))
            sent[block] += spread[0:16] + spread[16:32] + spread[32:48]
        return carry

    lax.fori_loop(0, count[0], one_chunk, 0)


def forward_solve(windows, station_parts, grid_rows, members, grid_planes):
    shape = jax.ShapeDtypeStruct
    vmem = pl.BlockSpec(memory_space=pltpu.VMEM)
    smem = pl.BlockSpec(memory_space=pltpu.SMEM)
    blocks = station_parts[0].shape[0]
    return pl.pallas_call(
        lambda *refs: forward_kernel(grid_rows, grid_rows // members, grid_planes, *refs),
        out_shape=(
            shape((DEGREE, 2, 3, 2, WINDOW, LANES), jnp.float32),
            shape((blocks, 4 * DEGREE, LANES), jnp.float32),
            shape((PLANES - 2, WINDOW, LANES), jnp.float32),
        ),
        in_specs=[vmem] * 6 + [smem, vmem],
        out_specs=(vmem, vmem, vmem),
        scratch_shapes=[
            pltpu.VMEM((7, PLANES, WINDOW, LANES), jnp.float32),
            pltpu.VMEM((2, 2, 3, PLANES - 2, WINDOW, LANES), jnp.float32),
            pltpu.VMEM((3, 2, 3, PLANES - 4, WINDOW, LANES), jnp.float32),
        ],
        compiler_params=pltpu.CompilerParams(vmem_limit_bytes=VMEM_LIMIT),
        cost_estimate=pl.CostEstimate(flops=20_000_000_000, bytes_accessed=3_000_000, transcendentals=0),
        name="forward_solve",
    )(*windows, *station_parts)


def residual_kernel(grid_rows, own_rows, read, data, cells, moments, owned, staged):
    members = data.shape[0]
    total = read[0]
    for member in range(1, read.shape[0]):
        total = total + read[member]
    coefficients = [total[4 * j : 4 * j + 4] for j in range(DEGREE)]
    first = pl.multiple_of(lax.axis_index("space") * LANES, LANES)
    cell = cells[:, pl.ds(first, LANES)]
    y = jnp.min((cell // LANES) % grid_rows, axis=0, keepdims=True)
    mine = (y // own_rows) == lax.axis_index("period")
    sums = [jnp.zeros((4, LANES), jnp.float32) for _ in range(MOMENTS)]
    for member in range(members):
        shift = data[member, 8:9, :]
        delta = shift - CENTER
        value = coefficients[DEGREE - 1]
        for j in range(DEGREE - 2, -1, -1):
            value = value * delta + coefficients[j]
        owned[member] = jnp.where(mine, value, 0.0)
        weight = data[member, 4:8, :]
        term = shift * (weight * weight * (value - data[member, 0:4, :]))
        for number in range(MOMENTS):
            sums[number] = sums[number] + term
            if number + 1 < MOMENTS:
                term = term * delta
    staged[...] = jnp.zeros(staged.shape, jnp.float32)
    for number in range(MOMENTS):
        staged[4 * number : 4 * number + 4, :] = sums[number]
    value = staged[...]
    for member in range(moments.shape[0]):
        moments[member] = value


def residuals(read, data, cells, grid_rows, members):
    shape = jax.ShapeDtypeStruct
    vmem = pl.BlockSpec(memory_space=pltpu.VMEM)
    return pl.pallas_call(
        lambda *refs: residual_kernel(grid_rows, grid_rows // members, *refs),
        out_shape=(
            shape((read.shape[0], 32, LANES), jnp.float32),
            shape((members, 4, LANES), jnp.float32),
        ),
        in_specs=[vmem, vmem, vmem],
        out_specs=(vmem, vmem),
        scratch_shapes=[pltpu.VMEM((32, LANES), jnp.float32)],
        compiler_params=pltpu.CompilerParams(vmem_limit_bytes=VMEM_SMALL),
        name="residuals",
    )(read, data, cells)


def adjoint_kernel(
    grid_rows, own_rows, grid_planes, periods, moments, places, count, features, mass, field,
    gradient, d0, d1, d2, picked, total,
):
    first_plane = first_window_plane()
    member = lax.axis_index("period")
    first_row = narrow_row(member, grid_rows, own_rows)
    inner = pl.ds(first_row - window_row(member, grid_rows, own_rows), NARROW)
    own = pl.ds(member * own_rows - first_row, own_rows)
    blocks = moments.shape[0]
    window_rows = PLANES * NARROW

    def add_chunk(chunk, fresh):
        feature = features[chunk]
        weight = row_weights(feature, 20, 0, window_rows)
        depth = depth_picks(feature)
        depth = jnp.concatenate([depth, depth], axis=1)
        gathered = jnp.zeros((96, LANES), jnp.float32)
        for block in range(blocks):
            pieces = jnp.concatenate(parts_of(moments[block]), axis=0)
            gathered += dot_nt(pieces, picks(places, block, chunk))
        picked[...] = gathered[0:32] + gathered[32:64] + gathered[64:96]

        def one_field(number, carry):
            values = weight * picked[pl.ds(number, 1), :]
            high = values.astype(jnp.bfloat16)
            low = (values - high.astype(jnp.float32)).astype(jnp.bfloat16)
            placed = dot_nt(jnp.concatenate([high, low], axis=1), depth)
            if fresh:
                d0[number] = placed
            else:
                d0[number] += placed
            return carry

        lax.fori_loop(0, 4 * MOMENTS, one_field, 0, unroll=MOMENTS)

    add_chunk(0, True)

    def one_chunk(chunk, carry):
        add_chunk(chunk, False)
        return carry

    lax.fori_loop(1, count[0], one_chunk, 0)

    def start(f, c, plane):
        return d0[2 * f + c, plane * NARROW : (plane + 1) * NARROW, :]

    def level_one(f, carry):
        def b(plane):
            return start(f, 0, plane), start(f, 1, plane), None

        for plane, here, curled in curl_curl(b, 1, 6, first_plane, grid_planes):
            m = mass[plane - 1, inner, :]
            for c in range(2):
                mixed = CENTER * here[c] + start(f + 2, c, plane)
                d1[f, c, plane - 1] = (
                    (1.0 + MOMENTUM[1]) * here[c] - STEP[0] * (curled[c] + m * mixed)
                )
            d1[f, 2, plane - 1] = -STEP[0] * curled[2]
        return carry

    lax.fori_loop(0, 2 * (MOMENTS - 1), level_one, 0)

    def level_two(f, carry):
        def get(plane):
            return tuple(d1[f, c, plane - 1] for c in range(3))

        for plane, here, curled in curl_curl(get, 2, 5, first_plane, grid_planes):
            m = mass[plane - 1, inner, :]
            for c in range(3):
                mixed = CENTER * here[c] + d1[f + 2, c, plane - 1]
                value = (1.0 + MOMENTUM[2]) * here[c] - STEP[1] * (curled[c] + m * mixed)
                if c < 2:
                    value = value - MOMENTUM[1] * start(f, c, plane)
                d2[f, c, plane - 2] = value
        return carry

    lax.fori_loop(0, 2 * (MOMENTS - 2), level_two, 0)

    total[...] = jnp.zeros(total.shape, jnp.float32)

    def level_three(f, carry):
        def get(plane):
            return tuple(d2[f, c, plane - 2] for c in range(3))

        for plane, here, curled in curl_curl(get, 3, 4, first_plane, grid_planes):
            m = mass[plane - 1, inner, :]
            added = None
            for c in range(3):
                mixed = CENTER * here[c] + d2[f + 2, c, plane - 2]
                first = d1[f, c, plane - 1]
                last = (
                    (1.0 + MOMENTUM[3]) * here[c] - MOMENTUM[2] * first
                    - STEP[2] * (curled[c] + m * mixed)
                )
                value = STEP[1] * first + STEP[2] * here[c] + STEP[3] * last
                if c < 2:
                    value = value + STEP[0] * start(f, c, plane)
                term = value * field[f, c, plane - 3, inner, :]
                added = term if added is None else added + term
            total[plane - 3] += added
        return carry

    lax.fori_loop(0, 2 * DEGREE, level_three, 0)
    gradient[...] = total[:, own, :] * (-1.0 / periods)


def adjoint_solve(moments, station_parts, mass, field, grid_rows, members, grid_planes):
    vmem = pl.BlockSpec(memory_space=pltpu.VMEM)
    smem = pl.BlockSpec(memory_space=pltpu.SMEM)
    own_rows = grid_rows // members
    return pl.pallas_call(
        lambda *refs: adjoint_kernel(grid_rows, own_rows, grid_planes, members, *refs),
        out_shape=jax.ShapeDtypeStruct((2, own_rows, LANES), jnp.float32),
        in_specs=[vmem, vmem, smem, vmem, vmem, vmem],
        out_specs=vmem,
        scratch_shapes=[
            pltpu.VMEM((4 * MOMENTS, PLANES * NARROW, LANES), jnp.float32),
            pltpu.VMEM((2 * (MOMENTS - 1), 3, PLANES - 2, NARROW, LANES), jnp.float32),
            pltpu.VMEM((2 * (MOMENTS - 2), 3, PLANES - 4, NARROW, LANES), jnp.float32),
            pltpu.VMEM((32, LANES), jnp.float32),
            pltpu.VMEM((2, NARROW, LANES), jnp.float32),
        ],
        compiler_params=pltpu.CompilerParams(vmem_limit_bytes=VMEM_LIMIT),
        cost_estimate=pl.CostEstimate(flops=200_000_000, bytes_accessed=3_000_000, transcendentals=0),
        name="adjoint_solve",
    )(moments, *station_parts, mass, field.reshape(2 * DEGREE, 3, 2, WINDOW, LANES))


def shards(source, conductivity, period_shift, site_cells, site_weights, observed, data_weight):
    grid_rows = conductivity.shape[1]
    count = lax.axis_size("space")
    members = lax.axis_size("period")
    grid_planes = conductivity.shape[0] * count
    slab, beside, far_a, far_b, data = pack(
        source, conductivity, period_shift, observed, data_weight, members
    )

    def swapped(values, partner):
        pairs = []
        for i in range(count):
            j = partner(i)
            flip = 0 if i // 2 == j // 2 else 1
            if 0 <= j < count:
                pairs += [(i * members + t, j * members + (t ^ flip)) for t in range(members)]
        return lax.ppermute(values, ("space", "period"), pairs)

    windows = (
        slab,
        swapped(slab, lambda i: i ^ 1),
        swapped(beside, lambda i: i + 1 if i % 2 else i - 1),
        swapped(far_a, lambda i: i ^ 2),
        swapped(far_b, lambda i: i + 2 if i & 2 else i - 2),
    )
    mate, data = lax.optimization_barrier((windows[1], data))
    windows = (windows[0], mate, *windows[2:])
    data = lax.all_to_all(data, "period", 0, 0, tiled=True)
    station_parts = stations(site_cells, site_weights, grid_rows, members)
    field, sent, mass = forward_solve(windows, station_parts, grid_rows, members, grid_planes)
    sent, data = lax.optimization_barrier((sent, data))
    read = lax.all_to_all(sent, "space", 0, 0, tiled=True)
    moments, owned = residuals(read, data, site_cells, grid_rows, members)
    moments = lax.all_to_all(moments, "space", 0, 0, tiled=True)
    moments, owned = lax.optimization_barrier((moments, owned))
    owned = lax.all_to_all(owned, "period", 0, 0, tiled=True)
    gradient = adjoint_solve(moments, station_parts, mass, field, grid_rows, members, grid_planes)
    return jnp.sum(owned, axis=0, keepdims=True), gradient


def solution(mesh):
    placed = (
        P(None, None, "space", None, None),
        P("space", None, None),
        P("period"),
        P(),
        P(),
        P("period", None, "space"),
        P("period", None, "space"),
    )
    return jax.shard_map(
        shards,
        mesh=mesh,
        in_specs=placed,
        out_specs=(P("period", None, "space"), P("space", "period", None)),
        check_vma=False,
    )
```

```python
import jax
import jax.numpy as jnp
from jax import lax
from jax.experimental import pallas as pl
from jax.experimental.pallas import tpu as pltpu
from jax.sharding import PartitionSpec as P

SWEEPS = 4
LOWER_BOUND = 0.05
UPPER_BOUND = 16.0

CENTER = 1.25
HALO = SWEEPS - 1
PLANES = 2 + 2 * HALO
WINDOW = 32
NARROW = 24
DEGREE = SWEEPS
MOMENTS = 2 * SWEEPS - 1
LANES = 128
VMEM_SMALL = 6 * 1024 * 1024
VMEM_LIMIT = 16 * 1024 * 1024


def chebyshev_steps(sweep_count):
    center = 0.5 * (UPPER_BOUND + LOWER_BOUND)
    spread = 0.5 * (UPPER_BOUND - LOWER_BOUND)
    step_sizes = []
    momenta = []
    step_size = 1.0 / center
    for number in range(sweep_count):
        if number == 0:
            momentum = 0.0
        elif number == 1:
            momentum = 0.5 * (spread * step_size) ** 2
        else:
            momentum = (0.5 * spread * step_size) ** 2
        if number > 0:
            step_size = 1.0 / (center - momentum / step_size)
        step_sizes.append(step_size)
        momenta.append(momentum)
    return (step_sizes, momenta)


STEP, MOMENTUM = chebyshev_steps(SWEEPS)


def window_row(member, grid_rows, own_rows):
    first = member * own_rows - (WINDOW - own_rows) // 2
    return pl.multiple_of(jnp.clip(first, 0, grid_rows - WINDOW), 8)


def narrow_row(member, grid_rows, own_rows):
    return jnp.clip(member * own_rows - (NARROW - own_rows) // 2, 0, grid_rows - NARROW)


def first_window_plane():
    return lax.axis_index("space") * 2 - HALO


def iota(shape, dim):
    return lax.broadcasted_iota(jnp.int32, shape, dim)


def parts_of(values):
    high = values.astype(jnp.bfloat16)
    rest = values - high.astype(jnp.float32)
    middle = rest.astype(jnp.bfloat16)
    low = (rest - middle.astype(jnp.float32)).astype(jnp.bfloat16)
    return high, middle, low


def dot_nt(left, right):
    return lax.dot_general(left, right, (((1,), (1,)), ((), ())), preferred_element_type=jnp.float32)


def dot_nn(left, right):
    return lax.dot_general(left, right, (((1,), (0,)), ((), ())), preferred_element_type=jnp.float32)


def next_z(v):
    return jnp.where(iota(v.shape, 1) == v.shape[1] - 1, 0.0, pltpu.roll(v, v.shape[1] - 1, 1))


def last_z(v):
    return jnp.where(iota(v.shape, 1) == 0, 0.0, pltpu.roll(v, 1, 1))


def next_y(v):
    return jnp.where(iota(v.shape, 0) == v.shape[0] - 1, 0.0, pltpu.roll(v, v.shape[0] - 1, 0))


def last_y(v):
    return jnp.where(iota(v.shape, 0) == 0, 0.0, pltpu.roll(v, 1, 0))


def curl_curl(get, first, last, first_plane, planes_in_grid):
    before = None
    here = get(first - 1)
    for plane in range(first - 1, last + 1):
        after = get(plane + 1)
        east, north, down = here
        c2 = next_z(east) - east
        if down is not None:
            c2 = c2 - (after[2] - down)
        c3 = (after[1] - north) - (next_y(east) - east)
        if plane < HALO and plane % 2 == 0:
            inside = jnp.where(first_plane + plane < 0, 0.0, 1.0)
            c2 = c2 * inside
            c3 = c3 * inside
        if plane >= first:
            c1 = north - next_z(north)
            if down is not None:
                c1 = c1 + (next_y(down) - down)
            a1 = (c3 - last_y(c3)) - (c2 - last_z(c2))
            a2 = (c1 - last_z(c1)) - (c3 - before[1])
            a3 = (c2 - before[0]) - (c1 - last_y(c1))
            if plane == HALO + 2:
                inside = jnp.where(first_plane + plane >= planes_in_grid, 0.0, 1.0)
                a1, a2, a3 = a1 * inside, a2 * inside, a3 * inside
            yield plane, here, (a1, a2, a3)
        before = (c2, c3)
        here = after


def pack_kernel(
    grid_rows, own_rows, source, conductivity, shift, observed, weight,
    slab, beside, far_a, far_b, data, pairs, sems,
):
    member = lax.axis_index("period")
    pair = (lax.axis_index("space") // 2) % 2
    copies = [(observed.at[0], pairs.at[0]), (weight.at[0], pairs.at[1])]
    rows = pl.ds(window_row(member, grid_rows, own_rows), WINDOW)
    for pol in range(2):
        copies.append((source.at[pol, :, :, rows, :], slab.at[pl.ds(3 * pol, 3)]))
    copies.append((conductivity.at[:, rows, :], slab.at[6]))
    rows = pl.ds(window_row(member + 1 - 2 * (member % 2), grid_rows, own_rows), WINDOW)
    for pol in range(2):
        copies.append((source.at[pol, :, :, rows, :], beside.at[pl.ds(3 * pol, 3)]))
        copies.append((source.at[pol, :, 1 - pair, rows, :], far_a.at[pl.ds(3 * pol, 3)]))
        copies.append((source.at[pol, :, pair, rows, :], far_b.at[pl.ds(3 * pol, 3)]))
    copies.append((conductivity.at[:, rows, :], beside.at[6]))
    started = [pltpu.make_async_copy(a, b, sems.at[i]) for i, (a, b) in enumerate(copies)]
    for copy in started:
        copy.start()
    for copy in started:
        copy.wait()
    for member in range(data.shape[0]):
        data[member, 0:4, :] = pairs[0]
        data[member, 4:8, :] = pairs[1]
        data[member, 8:16, :] = jnp.full((8, LANES), shift[0], jnp.float32)


def pack(source, conductivity, shift, observed, weight, members):
    grid_rows = source.shape[3]
    shape = jax.ShapeDtypeStruct
    hbm = pl.BlockSpec(memory_space=pltpu.HBM)
    vmem = pl.BlockSpec(memory_space=pltpu.VMEM)
    smem = pl.BlockSpec(memory_space=pltpu.SMEM)
    return pl.pallas_call(
        lambda *refs: pack_kernel(grid_rows, grid_rows // members, *refs),
        out_shape=(shape((7, 2, WINDOW, LANES), jnp.float32),) * 2
        + (shape((6, WINDOW, LANES), jnp.float32),) * 2
        + (shape((members, 16, LANES), jnp.float32),),
        in_specs=[hbm, hbm, smem, hbm, hbm],
        out_specs=(vmem,) * 5,
        scratch_shapes=[pltpu.VMEM((2, 4, LANES), jnp.float32), pltpu.SemaphoreType.DMA((12,))],
        compiler_params=pltpu.CompilerParams(vmem_limit_bytes=VMEM_SMALL),
        name="pack",
    )(
        *(pltpu.with_memory_space_constraint(v, pltpu.HBM) for v in (source, conductivity)),
        shift,
        *(pltpu.with_memory_space_constraint(v, pltpu.HBM) for v in (observed, weight)),
    )


def stations_kernel(grid_rows, own_rows, cells, weights, places, count, features, marks, staged):
    member = lax.axis_index("period")
    first_own = member * own_rows
    first_row = window_row(member, grid_rows, own_rows)
    first_narrow = narrow_row(member, grid_rows, own_rows)
    plane_size = grid_rows * LANES
    cell = cells[...]
    x = cell // plane_size - first_window_plane()
    y = (cell // LANES) % grid_rows
    reached = (
        (x >= 0) & (x < PLANES)
        & (y >= first_own - HALO - 1) & (y < first_own + own_rows + HALO + 1)
    )
    row = jnp.where(reached, x * WINDOW + y - first_row, 0).astype(jnp.float32)
    narrow = jnp.where(reached, x * NARROW + y - first_narrow, 0).astype(jnp.float32)
    weight = jnp.where(reached, weights[...], 0.0)
    present = jnp.max(jnp.where(reached, 1.0, 0.0), axis=0, keepdims=True)
    blocks = cell.shape[1] // LANES
    staged[...] = jnp.zeros(staged.shape, jnp.float32)
    staged[0:4, :] = row
    staged[4:8, :] = (cell % LANES).astype(jnp.float32)
    staged[20:24, :] = narrow
    for number, part in enumerate(parts_of(weight)):
        staged[8 + 4 * number : 12 + 4 * number, :] = part.astype(jnp.float32)
    for block in range(blocks):
        marks[block : block + 1, :] = present[:, block * LANES : (block + 1) * LANES]
    mark = marks[...]
    square = (LANES, LANES)
    upto = jnp.where(iota(square, 0) <= iota(square, 1), 1.0, 0.0).astype(jnp.bfloat16)
    inner = dot_nn(mark.astype(jnp.bfloat16), upto)
    totals = dot_nn(mark.astype(jnp.bfloat16), jnp.ones(square, jnp.bfloat16))
    earlier = jnp.where(iota((blocks, blocks), 0) > iota((blocks, blocks), 1), 1.0, 0.0)
    offsets = dot_nn(earlier.astype(jnp.bfloat16), totals.astype(jnp.bfloat16))
    places[...] = jnp.where(mark > 0.0, inner + offsets - 1.0, -1.0).astype(jnp.int32)
    chunks = (jnp.sum(mark).astype(jnp.int32) + LANES - 1) // LANES
    count[0] = chunks

    def one_chunk(chunk, carry):
        gathered = jnp.zeros((staged.shape[0], LANES), jnp.float32)
        for block in range(blocks):
            feature = staged[:, block * LANES : (block + 1) * LANES].astype(jnp.bfloat16)
            gathered += dot_nt(feature, picks(places, block, chunk))
        features[chunk] = gathered
        return carry

    features[0] = jnp.zeros(features.shape[1:], jnp.float32)
    lax.fori_loop(0, chunks, one_chunk, 0)


def picks(places, block, chunk):
    wanted = places[block : block + 1, :] - chunk * LANES
    return jnp.where(iota((LANES, LANES), 0) == wanted, 1.0, 0.0).astype(jnp.bfloat16)


def stations(cells, weights, grid_rows, members):
    blocks = cells.shape[1] // LANES
    shape = jax.ShapeDtypeStruct
    vmem = pl.BlockSpec(memory_space=pltpu.VMEM)
    return pl.pallas_call(
        lambda *refs: stations_kernel(grid_rows, grid_rows // members, *refs),
        out_shape=(
            shape((blocks, LANES), jnp.int32),
            shape((1,), jnp.int32),
            shape((blocks, 32, LANES), jnp.float32),
        ),
        in_specs=[vmem, vmem],
        out_specs=(vmem, pl.BlockSpec(memory_space=pltpu.SMEM), vmem),
        scratch_shapes=[
            pltpu.VMEM((blocks, LANES), jnp.float32),
            pltpu.VMEM((32, cells.shape[1]), jnp.float32),
        ],
        compiler_params=pltpu.CompilerParams(vmem_limit_bytes=VMEM_LIMIT),
        cost_estimate=pl.CostEstimate(flops=10_000_000, bytes_accessed=200_000, transcendentals=0),
        name="stations",
    )(cells, weights)


def row_weights(feature, field, first, count):
    rows = (iota((count, LANES), 0) + first).astype(jnp.float32)
    total = jnp.zeros((count, LANES), jnp.float32)
    for q in range(4):
        weight = feature[8 + q : 9 + q] + feature[12 + q : 13 + q] + feature[16 + q : 17 + q]
        total += jnp.where(rows == feature[field + q : field + q + 1], weight, 0.0)
    return total


def depth_picks(feature):
    depth = iota((LANES, LANES), 0).astype(jnp.float32)
    return jnp.where(depth == feature[4:5], 1.0, 0.0).astype(jnp.bfloat16)


def forward_kernel(
    grid_rows, own_rows, grid_planes, slab, mate, beside, far_a, far_b, places, count, features,
    field, sent, mass, window, d1, d2,
):
    first_plane = first_window_plane()
    even = lax.axis_index("space") % 2 == 0
    lower = (lax.axis_index("space") // 2) % 2 == 0
    for plane in range(2):
        here, there = mate[:, plane], beside[:, plane]
        window[:, 1 + plane] = jnp.where(even, there, here)
        window[:, 3 + plane] = slab[:, plane]
        window[:, 5 + plane] = jnp.where(even, here, there)
    window[0:6, 0] = jnp.where(lower, far_b[...], far_a[...])
    window[0:6, PLANES - 1] = jnp.where(lower, far_a[...], far_b[...])
    mass[...] = window[6, 1 : PLANES - 1]

    def part(number, plane):
        return window[number, plane]

    for pol in range(2):
        def b(plane, pol=pol):
            return tuple(part(3 * pol + c, plane) for c in range(3))

        for plane, here, curled in curl_curl(b, 1, 6, first_plane, grid_planes):
            m = mass[plane - 1]
            for c in range(3):
                heavy = m * here[c]
                d1[0, pol, c, plane - 1] = (
                    (1.0 + MOMENTUM[1]) * here[c] - STEP[0] * (curled[c] + CENTER * heavy)
                )
                d1[1, pol, c, plane - 1] = -STEP[0] * heavy

        def level1(j, pol=pol):
            return lambda plane: tuple(d1[j, pol, c, plane - 1] for c in range(3))

        for j in range(2):
            for plane, here, curled in curl_curl(level1(j), 2, 5, first_plane, grid_planes):
                m = mass[plane - 1]
                for c in range(3):
                    mixed = CENTER * here[c]
                    if j == 1:
                        mixed = mixed + d1[0, pol, c, plane - 1]
                    value = (1.0 + MOMENTUM[2]) * here[c] - STEP[1] * (curled[c] + m * mixed)
                    if j == 0:
                        value = value - MOMENTUM[1] * part(3 * pol + c, plane)
                    d2[j, pol, c, plane - 2] = value
                    if j == 1:
                        d2[2, pol, c, plane - 2] = -STEP[1] * (m * here[c])

        def level2(j, pol=pol):
            return lambda plane: tuple(d2[j, pol, c, plane - 2] for c in range(3))

        for j in range(3):
            for plane, here, curled in curl_curl(level2(j), 3, 4, first_plane, grid_planes):
                m = mass[plane - 1]
                for c in range(3):
                    mixed = CENTER * here[c]
                    if j > 0:
                        mixed = mixed + d2[j - 1, pol, c, plane - 2]
                    last = (1.0 + MOMENTUM[3]) * here[c] - STEP[2] * (curled[c] + m * mixed)
                    value = STEP[2] * here[c]
                    if j < 2:
                        first = d1[j, pol, c, plane - 1]
                        last = last - MOMENTUM[2] * first
                        value = value + STEP[1] * first
                    if j == 0:
                        value = value + STEP[0] * part(3 * pol + c, plane)
                    field[j, pol, c, plane - 3] = value + STEP[3] * last
                    if j == 2:
                        field[3, pol, c, plane - 3] = -(STEP[3] * STEP[2]) * (m * here[c])

    members = sent.shape[0]
    sent[...] = jnp.zeros(sent.shape, jnp.float32)

    def one_chunk(chunk, carry):
        feature = features[chunk]
        weight = row_weights(feature, 0, HALO * WINDOW, 2 * WINDOW)
        depth = depth_picks(feature)
        rows = []
        for j in range(DEGREE):
            for pol in range(2):
                for c in range(2):
                    values = field[j, pol, c].reshape(2 * WINDOW, LANES)
                    at_depth = sum(dot_nn(piece, depth) for piece in parts_of(values))
                    rows.append(jnp.sum(at_depth * weight, axis=0, keepdims=True))
        read = jnp.concatenate(rows, axis=0)
        pieces = jnp.concatenate(parts_of(read), axis=0)
        for block in range(members):
            spread = dot_nn(pieces, picks(places, block, chunk))
            sent[block] += spread[0:16] + spread[16:32] + spread[32:48]
        return carry

    lax.fori_loop(0, count[0], one_chunk, 0)


def forward_solve(windows, station_parts, grid_rows, members, grid_planes):
    shape = jax.ShapeDtypeStruct
    vmem = pl.BlockSpec(memory_space=pltpu.VMEM)
    smem = pl.BlockSpec(memory_space=pltpu.SMEM)
    blocks = station_parts[0].shape[0]
    return pl.pallas_call(
        lambda *refs: forward_kernel(grid_rows, grid_rows // members, grid_planes, *refs),
        out_shape=(
            shape((DEGREE, 2, 3, 2, WINDOW, LANES), jnp.float32),
            shape((blocks, 4 * DEGREE, LANES), jnp.float32),
            shape((PLANES - 2, WINDOW, LANES), jnp.float32),
        ),
        in_specs=[vmem] * 6 + [smem, vmem],
        out_specs=(vmem, vmem, vmem),
        scratch_shapes=[
            pltpu.VMEM((7, PLANES, WINDOW, LANES), jnp.float32),
            pltpu.VMEM((2, 2, 3, PLANES - 2, WINDOW, LANES), jnp.float32),
            pltpu.VMEM((3, 2, 3, PLANES - 4, WINDOW, LANES), jnp.float32),
        ],
        compiler_params=pltpu.CompilerParams(vmem_limit_bytes=VMEM_LIMIT),
        cost_estimate=pl.CostEstimate(flops=20_000_000_000, bytes_accessed=3_000_000, transcendentals=0),
        name="forward_solve",
    )(*windows, *station_parts)


def residual_kernel(grid_rows, own_rows, read, data, cells, moments, owned, staged):
    members = data.shape[0]
    total = read[0]
    for member in range(1, read.shape[0]):
        total = total + read[member]
    coefficients = [total[4 * j : 4 * j + 4] for j in range(DEGREE)]
    first = pl.multiple_of(lax.axis_index("space") * LANES, LANES)
    cell = cells[:, pl.ds(first, LANES)]
    y = jnp.min((cell // LANES) % grid_rows, axis=0, keepdims=True)
    mine = (y // own_rows) == lax.axis_index("period")
    sums = [jnp.zeros((4, LANES), jnp.float32) for _ in range(MOMENTS)]
    for member in range(members):
        shift = data[member, 8:9, :]
        delta = shift - CENTER
        value = coefficients[DEGREE - 1]
        for j in range(DEGREE - 2, -1, -1):
            value = value * delta + coefficients[j]
        owned[member] = jnp.where(mine, value, 0.0)
        weight = data[member, 4:8, :]
        term = shift * (weight * weight * (value - data[member, 0:4, :]))
        for number in range(MOMENTS):
            sums[number] = sums[number] + term
            if number + 1 < MOMENTS:
                term = term * delta
    staged[...] = jnp.zeros(staged.shape, jnp.float32)
    for number in range(MOMENTS):
        staged[4 * number : 4 * number + 4, :] = sums[number]
    value = staged[...]
    for member in range(moments.shape[0]):
        moments[member] = value


def residuals(read, data, cells, grid_rows, members):
    shape = jax.ShapeDtypeStruct
    vmem = pl.BlockSpec(memory_space=pltpu.VMEM)
    return pl.pallas_call(
        lambda *refs: residual_kernel(grid_rows, grid_rows // members, *refs),
        out_shape=(
            shape((read.shape[0], 32, LANES), jnp.float32),
            shape((members, 4, LANES), jnp.float32),
        ),
        in_specs=[vmem, vmem, vmem],
        out_specs=(vmem, vmem),
        scratch_shapes=[pltpu.VMEM((32, LANES), jnp.float32)],
        compiler_params=pltpu.CompilerParams(vmem_limit_bytes=VMEM_SMALL),
        name="residuals",
    )(read, data, cells)


def adjoint_kernel(
    grid_rows, own_rows, grid_planes, periods, moments, places, count, features, mass, field,
    gradient, d0, d1, d2, picked, total,
):
    first_plane = first_window_plane()
    member = lax.axis_index("period")
    first_row = narrow_row(member, grid_rows, own_rows)
    inner = pl.ds(first_row - window_row(member, grid_rows, own_rows), NARROW)
    own = pl.ds(member * own_rows - first_row, own_rows)
    blocks = moments.shape[0]
    window_rows = PLANES * NARROW

    def add_chunk(chunk, fresh):
        feature = features[chunk]
        weight = row_weights(feature, 20, 0, window_rows)
        depth = depth_picks(feature)
        depth = jnp.concatenate([depth, depth], axis=1)
        gathered = jnp.zeros((96, LANES), jnp.float32)
        for block in range(blocks):
            pieces = jnp.concatenate(parts_of(moments[block]), axis=0)
            gathered += dot_nt(pieces, picks(places, block, chunk))
        picked[...] = gathered[0:32] + gathered[32:64] + gathered[64:96]

        def one_field(number, carry):
            values = weight * picked[pl.ds(number, 1), :]
            high = values.astype(jnp.bfloat16)
            low = (values - high.astype(jnp.float32)).astype(jnp.bfloat16)
            placed = dot_nt(jnp.concatenate([high, low], axis=1), depth)
            if fresh:
                d0[number] = placed
            else:
                d0[number] += placed
            return carry

        lax.fori_loop(0, 4 * MOMENTS, one_field, 0, unroll=MOMENTS)

    add_chunk(0, True)

    def one_chunk(chunk, carry):
        add_chunk(chunk, False)
        return carry

    lax.fori_loop(1, count[0], one_chunk, 0)

    def start(f, c, plane):
        return d0[2 * f + c, plane * NARROW : (plane + 1) * NARROW, :]

    def level_one(f, carry):
        def b(plane):
            return start(f, 0, plane), start(f, 1, plane), None

        for plane, here, curled in curl_curl(b, 1, 6, first_plane, grid_planes):
            m = mass[plane - 1, inner, :]
            for c in range(2):
                mixed = CENTER * here[c] + start(f + 2, c, plane)
                d1[f, c, plane - 1] = (
                    (1.0 + MOMENTUM[1]) * here[c] - STEP[0] * (curled[c] + m * mixed)
                )
            d1[f, 2, plane - 1] = -STEP[0] * curled[2]
        return carry

    lax.fori_loop(0, 2 * (MOMENTS - 1), level_one, 0)

    def level_two(f, carry):
        def get(plane):
            return tuple(d1[f, c, plane - 1] for c in range(3))

        for plane, here, curled in curl_curl(get, 2, 5, first_plane, grid_planes):
            m = mass[plane - 1, inner, :]
            for c in range(3):
                mixed = CENTER * here[c] + d1[f + 2, c, plane - 1]
                value = (1.0 + MOMENTUM[2]) * here[c] - STEP[1] * (curled[c] + m * mixed)
                if c < 2:
                    value = value - MOMENTUM[1] * start(f, c, plane)
                d2[f, c, plane - 2] = value
        return carry

    lax.fori_loop(0, 2 * (MOMENTS - 2), level_two, 0)

    total[...] = jnp.zeros(total.shape, jnp.float32)

    def level_three(f, carry):
        def get(plane):
            return tuple(d2[f, c, plane - 2] for c in range(3))

        for plane, here, curled in curl_curl(get, 3, 4, first_plane, grid_planes):
            m = mass[plane - 1, inner, :]
            added = None
            for c in range(3):
                mixed = CENTER * here[c] + d2[f + 2, c, plane - 2]
                first = d1[f, c, plane - 1]
                last = (
                    (1.0 + MOMENTUM[3]) * here[c] - MOMENTUM[2] * first
                    - STEP[2] * (curled[c] + m * mixed)
                )
                value = STEP[1] * first + STEP[2] * here[c] + STEP[3] * last
                if c < 2:
                    value = value + STEP[0] * start(f, c, plane)
                term = value * field[f, c, plane - 3, inner, :]
                added = term if added is None else added + term
            total[plane - 3] += added
        return carry

    lax.fori_loop(0, 2 * DEGREE, level_three, 0)
    gradient[...] = total[:, own, :] * (-1.0 / periods)


def adjoint_solve(moments, station_parts, mass, field, grid_rows, members, grid_planes):
    vmem = pl.BlockSpec(memory_space=pltpu.VMEM)
    smem = pl.BlockSpec(memory_space=pltpu.SMEM)
    own_rows = grid_rows // members
    return pl.pallas_call(
        lambda *refs: adjoint_kernel(grid_rows, own_rows, grid_planes, members, *refs),
        out_shape=jax.ShapeDtypeStruct((2, own_rows, LANES), jnp.float32),
        in_specs=[vmem, vmem, smem, vmem, vmem, vmem],
        out_specs=vmem,
        scratch_shapes=[
            pltpu.VMEM((4 * MOMENTS, PLANES * NARROW, LANES), jnp.float32),
            pltpu.VMEM((2 * (MOMENTS - 1), 3, PLANES - 2, NARROW, LANES), jnp.float32),
            pltpu.VMEM((2 * (MOMENTS - 2), 3, PLANES - 4, NARROW, LANES), jnp.float32),
            pltpu.VMEM((32, LANES), jnp.float32),
            pltpu.VMEM((2, NARROW, LANES), jnp.float32),
        ],
        compiler_params=pltpu.CompilerParams(vmem_limit_bytes=VMEM_LIMIT),
        cost_estimate=pl.CostEstimate(flops=200_000_000, bytes_accessed=3_000_000, transcendentals=0),
        name="adjoint_solve",
    )(moments, *station_parts, mass, field.reshape(2 * DEGREE, 3, 2, WINDOW, LANES))


def shards(source, conductivity, period_shift, site_cells, site_weights, observed, data_weight):
    grid_rows = conductivity.shape[1]
    count = lax.axis_size("space")
    members = lax.axis_size("period")
    grid_planes = conductivity.shape[0] * count
    slab, beside, far_a, far_b, data = pack(
        source, conductivity, period_shift, observed, data_weight, members
    )

    def swapped(values, partner):
        pairs = []
        for i in range(count):
            j = partner(i)
            flip = 0 if i // 2 == j // 2 else 1
            if 0 <= j < count:
                pairs += [(i * members + t, j * members + (t ^ flip)) for t in range(members)]
        return lax.ppermute(values, ("space", "period"), pairs)

    windows = (
        slab,
        swapped(slab, lambda i: i ^ 1),
        swapped(beside, lambda i: i + 1 if i % 2 else i - 1),
        swapped(far_a, lambda i: i ^ 2),
        swapped(far_b, lambda i: i + 2 if i & 2 else i - 2),
    )
    mate, data, late_cells = lax.optimization_barrier((windows[1], data, site_cells))
    windows = (windows[0], mate, *windows[2:])
    data = lax.all_to_all(data, "period", 0, 0, tiled=True)
    station_parts = stations(late_cells, site_weights, grid_rows, members)
    field, sent, mass = forward_solve(windows, station_parts, grid_rows, members, grid_planes)
    sent, data = lax.optimization_barrier((sent, data))
    read = lax.all_to_all(sent, "space", 0, 0, tiled=True)
    moments, owned = residuals(read, data, site_cells, grid_rows, members)
    moments = lax.all_to_all(moments, "space", 0, 0, tiled=True)
    moments, owned = lax.optimization_barrier((moments, owned))
    owned = lax.all_to_all(owned, "period", 0, 0, tiled=True)
    gradient = adjoint_solve(moments, station_parts, mass, field, grid_rows, members, grid_planes)
    return jnp.sum(owned, axis=0, keepdims=True), gradient


def solution(mesh):
    placed = (
        P(None, None, "space", None, None),
        P("space", None, None),
        P("period"),
        P(),
        P(),
        P("period", None, "space"),
        P("period", None, "space"),
    )
    return jax.shard_map(
        shards,
        mesh=mesh,
        in_specs=placed,
        out_specs=(P("period", None, "space"), P("space", "period", None)),
        check_vma=False,
    )
```

```python
import jax
import jax.numpy as jnp
from jax import lax
from jax.experimental import pallas as pl
from jax.experimental.pallas import tpu as pltpu
from jax.sharding import PartitionSpec as P

SWEEPS = 4
LOWER_BOUND = 0.05
UPPER_BOUND = 16.0

CENTER = 1.25
HALO = SWEEPS - 1
PLANES = 2 + 2 * HALO
WINDOW = 32
NARROW = 24
DEGREE = SWEEPS
MOMENTS = 2 * SWEEPS - 1
LANES = 128
VMEM_SMALL = 6 * 1024 * 1024
VMEM_LIMIT = 16 * 1024 * 1024


def chebyshev_steps(sweep_count):
    center = 0.5 * (UPPER_BOUND + LOWER_BOUND)
    spread = 0.5 * (UPPER_BOUND - LOWER_BOUND)
    step_sizes = []
    momenta = []
    step_size = 1.0 / center
    for number in range(sweep_count):
        if number == 0:
            momentum = 0.0
        elif number == 1:
            momentum = 0.5 * (spread * step_size) ** 2
        else:
            momentum = (0.5 * spread * step_size) ** 2
        if number > 0:
            step_size = 1.0 / (center - momentum / step_size)
        step_sizes.append(step_size)
        momenta.append(momentum)
    return (step_sizes, momenta)


STEP, MOMENTUM = chebyshev_steps(SWEEPS)


def window_row(member, grid_rows, own_rows):
    first = member * own_rows - (WINDOW - own_rows) // 2
    return pl.multiple_of(jnp.clip(first, 0, grid_rows - WINDOW), 8)


def narrow_row(member, grid_rows, own_rows):
    return jnp.clip(member * own_rows - (NARROW - own_rows) // 2, 0, grid_rows - NARROW)


def first_window_plane():
    return lax.axis_index("space") * 2 - HALO


def iota(shape, dim):
    return lax.broadcasted_iota(jnp.int32, shape, dim)


def parts_of(values):
    high = values.astype(jnp.bfloat16)
    rest = values - high.astype(jnp.float32)
    middle = rest.astype(jnp.bfloat16)
    low = (rest - middle.astype(jnp.float32)).astype(jnp.bfloat16)
    return high, middle, low


def dot_nt(left, right):
    return lax.dot_general(left, right, (((1,), (1,)), ((), ())), preferred_element_type=jnp.float32)


def dot_nn(left, right):
    return lax.dot_general(left, right, (((1,), (0,)), ((), ())), preferred_element_type=jnp.float32)


def next_z(v):
    return jnp.where(iota(v.shape, 1) == v.shape[1] - 1, 0.0, pltpu.roll(v, v.shape[1] - 1, 1))


def last_z(v):
    return jnp.where(iota(v.shape, 1) == 0, 0.0, pltpu.roll(v, 1, 1))


def next_y(v):
    return jnp.where(iota(v.shape, 0) == v.shape[0] - 1, 0.0, pltpu.roll(v, v.shape[0] - 1, 0))


def last_y(v):
    return jnp.where(iota(v.shape, 0) == 0, 0.0, pltpu.roll(v, 1, 0))


def curl_curl(get, first, last, first_plane, planes_in_grid, along_z=None):
    before = None
    here = get(first - 1)
    for plane in range(first - 1, last + 1):
        after = get(plane + 1)
        east, north, down = here
        c2 = along_z(plane, 0) if along_z else next_z(east) - east
        if down is not None:
            c2 = c2 - (after[2] - down)
        c3 = (after[1] - north) - (next_y(east) - east)
        if plane < HALO and plane % 2 == 0:
            inside = jnp.where(first_plane + plane < 0, 0.0, 1.0)
            c2 = c2 * inside
            c3 = c3 * inside
        if plane >= first:
            c1 = -along_z(plane, 1) if along_z else north - next_z(north)
            if down is not None:
                c1 = c1 + (next_y(down) - down)
            a1 = (c3 - last_y(c3)) - (c2 - last_z(c2))
            a2 = (c1 - last_z(c1)) - (c3 - before[1])
            a3 = (c2 - before[0]) - (c1 - last_y(c1))
            if plane == HALO + 2:
                inside = jnp.where(first_plane + plane >= planes_in_grid, 0.0, 1.0)
                a1, a2, a3 = a1 * inside, a2 * inside, a3 * inside
            yield plane, here, (a1, a2, a3)
        before = (c2, c3)
        here = after


def pack_kernel(
    grid_rows, own_rows, source, conductivity, shift, observed, weight,
    slab, beside, far_a, far_b, data, pairs, sems,
):
    member = lax.axis_index("period")
    pair = (lax.axis_index("space") // 2) % 2
    copies = [(observed.at[0], pairs.at[0]), (weight.at[0], pairs.at[1])]
    rows = pl.ds(window_row(member, grid_rows, own_rows), WINDOW)
    for pol in range(2):
        copies.append((source.at[pol, :, :, rows, :], slab.at[pl.ds(3 * pol, 3)]))
    copies.append((conductivity.at[:, rows, :], slab.at[6]))
    rows = pl.ds(window_row(member + 1 - 2 * (member % 2), grid_rows, own_rows), WINDOW)
    for pol in range(2):
        copies.append((source.at[pol, :, :, rows, :], beside.at[pl.ds(3 * pol, 3)]))
        copies.append((source.at[pol, :, 1 - pair, rows, :], far_a.at[pl.ds(3 * pol, 3)]))
        copies.append((source.at[pol, :, pair, rows, :], far_b.at[pl.ds(3 * pol, 3)]))
    copies.append((conductivity.at[:, rows, :], beside.at[6]))
    started = [pltpu.make_async_copy(a, b, sems.at[i]) for i, (a, b) in enumerate(copies)]
    for copy in started:
        copy.start()
    for copy in started:
        copy.wait()
    for member in range(data.shape[0]):
        data[member, 0:4, :] = pairs[0]
        data[member, 4:8, :] = pairs[1]
        data[member, 8:16, :] = jnp.full((8, LANES), shift[0], jnp.float32)


def pack(source, conductivity, shift, observed, weight, members):
    grid_rows = source.shape[3]
    shape = jax.ShapeDtypeStruct
    hbm = pl.BlockSpec(memory_space=pltpu.HBM)
    vmem = pl.BlockSpec(memory_space=pltpu.VMEM)
    smem = pl.BlockSpec(memory_space=pltpu.SMEM)
    return pl.pallas_call(
        lambda *refs: pack_kernel(grid_rows, grid_rows // members, *refs),
        out_shape=(shape((7, 2, WINDOW, LANES), jnp.float32),) * 2
        + (shape((6, WINDOW, LANES), jnp.float32),) * 2
        + (shape((members, 16, LANES), jnp.float32),),
        in_specs=[hbm, hbm, smem, hbm, hbm],
        out_specs=(vmem,) * 5,
        scratch_shapes=[pltpu.VMEM((2, 4, LANES), jnp.float32), pltpu.SemaphoreType.DMA((12,))],
        compiler_params=pltpu.CompilerParams(vmem_limit_bytes=VMEM_SMALL),
        name="pack",
    )(
        *(pltpu.with_memory_space_constraint(v, pltpu.HBM) for v in (source, conductivity)),
        shift,
        *(pltpu.with_memory_space_constraint(v, pltpu.HBM) for v in (observed, weight)),
    )


def stations_kernel(grid_rows, own_rows, cells, weights, places, count, features, marks, staged):
    member = lax.axis_index("period")
    first_own = member * own_rows
    first_row = window_row(member, grid_rows, own_rows)
    first_narrow = narrow_row(member, grid_rows, own_rows)
    plane_size = grid_rows * LANES
    cell = cells[...]
    x = cell // plane_size - first_window_plane()
    y = (cell // LANES) % grid_rows
    reached = (
        (x >= 0) & (x < PLANES)
        & (y >= first_own - HALO - 1) & (y < first_own + own_rows + HALO + 1)
    )
    row = jnp.where(reached, x * WINDOW + y - first_row, 0).astype(jnp.float32)
    narrow = jnp.where(reached, x * NARROW + y - first_narrow, 0).astype(jnp.float32)
    weight = jnp.where(reached, weights[...], 0.0)
    present = jnp.max(jnp.where(reached, 1.0, 0.0), axis=0, keepdims=True)
    blocks = cell.shape[1] // LANES
    staged[...] = jnp.zeros(staged.shape, jnp.float32)
    staged[0:4, :] = row
    staged[4:8, :] = (cell % LANES).astype(jnp.float32)
    staged[20:24, :] = narrow
    for number, part in enumerate(parts_of(weight)):
        staged[8 + 4 * number : 12 + 4 * number, :] = part.astype(jnp.float32)
    for block in range(blocks):
        marks[block : block + 1, :] = present[:, block * LANES : (block + 1) * LANES]
    mark = marks[...]
    square = (LANES, LANES)
    upto = jnp.where(iota(square, 0) <= iota(square, 1), 1.0, 0.0).astype(jnp.bfloat16)
    inner = dot_nn(mark.astype(jnp.bfloat16), upto)
    totals = dot_nn(mark.astype(jnp.bfloat16), jnp.ones(square, jnp.bfloat16))
    earlier = jnp.where(iota((blocks, blocks), 0) > iota((blocks, blocks), 1), 1.0, 0.0)
    offsets = dot_nn(earlier.astype(jnp.bfloat16), totals.astype(jnp.bfloat16))
    places[...] = jnp.where(mark > 0.0, inner + offsets - 1.0, -1.0).astype(jnp.int32)
    chunks = (jnp.sum(mark).astype(jnp.int32) + LANES - 1) // LANES
    count[0] = chunks

    def one_chunk(chunk, carry):
        gathered = jnp.zeros((staged.shape[0], LANES), jnp.float32)
        for block in range(blocks):
            feature = staged[:, block * LANES : (block + 1) * LANES].astype(jnp.bfloat16)
            gathered += dot_nt(feature, picks(places, block, chunk))
        features[chunk] = gathered
        return carry

    features[0] = jnp.zeros(features.shape[1:], jnp.float32)
    lax.fori_loop(0, chunks, one_chunk, 0)


def picks(places, block, chunk):
    wanted = places[block : block + 1, :] - chunk * LANES
    return jnp.where(iota((LANES, LANES), 0) == wanted, 1.0, 0.0).astype(jnp.bfloat16)


def stations(cells, weights, grid_rows, members):
    blocks = cells.shape[1] // LANES
    shape = jax.ShapeDtypeStruct
    vmem = pl.BlockSpec(memory_space=pltpu.VMEM)
    return pl.pallas_call(
        lambda *refs: stations_kernel(grid_rows, grid_rows // members, *refs),
        out_shape=(
            shape((blocks, LANES), jnp.int32),
            shape((1,), jnp.int32),
            shape((blocks, 32, LANES), jnp.float32),
        ),
        in_specs=[vmem, vmem],
        out_specs=(vmem, pl.BlockSpec(memory_space=pltpu.SMEM), vmem),
        scratch_shapes=[
            pltpu.VMEM((blocks, LANES), jnp.float32),
            pltpu.VMEM((32, cells.shape[1]), jnp.float32),
        ],
        compiler_params=pltpu.CompilerParams(vmem_limit_bytes=VMEM_LIMIT),
        cost_estimate=pl.CostEstimate(flops=10_000_000, bytes_accessed=200_000, transcendentals=0),
        name="stations",
    )(cells, weights)


def row_weights(feature, field, first, count):
    rows = (iota((count, LANES), 0) + first).astype(jnp.float32)
    total = jnp.zeros((count, LANES), jnp.float32)
    for q in range(4):
        weight = feature[8 + q : 9 + q] + feature[12 + q : 13 + q] + feature[16 + q : 17 + q]
        total += jnp.where(rows == feature[field + q : field + q + 1], weight, 0.0)
    return total


def depth_picks(feature):
    depth = iota((LANES, LANES), 0).astype(jnp.float32)
    return jnp.where(depth == feature[4:5], 1.0, 0.0).astype(jnp.bfloat16)


def depth_picks_and_differences(feature):
    depth = iota((LANES, LANES), 0).astype(jnp.float32)
    here = jnp.where(depth == feature[4:5], 1.0, 0.0)
    change = jnp.where(depth + 1.0 == feature[4:5], 1.0, 0.0) - here
    return jnp.concatenate([here, change], axis=0).astype(jnp.bfloat16)


def forward_kernel(
    grid_rows, own_rows, grid_planes, slab, mate, beside, far_a, far_b, places, count, features,
    field, sent, mass, window, d1, d2,
):
    first_plane = first_window_plane()
    even = lax.axis_index("space") % 2 == 0
    lower = (lax.axis_index("space") // 2) % 2 == 0
    for plane in range(2):
        here, there = mate[:, plane], beside[:, plane]
        window[:, 1 + plane] = jnp.where(even, there, here)
        window[:, 3 + plane] = slab[:, plane]
        window[:, 5 + plane] = jnp.where(even, here, there)
    window[0:6, 0] = jnp.where(lower, far_b[...], far_a[...])
    window[0:6, PLANES - 1] = jnp.where(lower, far_a[...], far_b[...])
    mass[...] = window[6, 1 : PLANES - 1]

    def part(number, plane):
        return window[number, plane]

    for pol in range(2):
        def b(plane, pol=pol):
            return tuple(part(3 * pol + c, plane) for c in range(3))

        for plane, here, curled in curl_curl(b, 1, 6, first_plane, grid_planes):
            m = mass[plane - 1]
            for c in range(3):
                heavy = m * here[c]
                d1[0, pol, c, plane - 1] = (
                    (1.0 + MOMENTUM[1]) * here[c] - STEP[0] * (curled[c] + CENTER * heavy)
                )
                d1[1, pol, c, plane - 1] = -STEP[0] * heavy

        def level1(j, pol=pol):
            return lambda plane: tuple(d1[j, pol, c, plane - 1] for c in range(3))

        for j in range(2):
            for plane, here, curled in curl_curl(level1(j), 2, 5, first_plane, grid_planes):
                m = mass[plane - 1]
                for c in range(3):
                    mixed = CENTER * here[c]
                    if j == 1:
                        mixed = mixed + d1[0, pol, c, plane - 1]
                    value = (1.0 + MOMENTUM[2]) * here[c] - STEP[1] * (curled[c] + m * mixed)
                    if j == 0:
                        value = value - MOMENTUM[1] * part(3 * pol + c, plane)
                    d2[j, pol, c, plane - 2] = value
                    if j == 1:
                        d2[2, pol, c, plane - 2] = -STEP[1] * (m * here[c])

        def level2(j, pol=pol):
            return lambda plane: tuple(d2[j, pol, c, plane - 2] for c in range(3))

        for j in range(3):
            for plane, here, curled in curl_curl(level2(j), 3, 4, first_plane, grid_planes):
                m = mass[plane - 1]
                for c in range(3):
                    mixed = CENTER * here[c]
                    if j > 0:
                        mixed = mixed + d2[j - 1, pol, c, plane - 2]
                    last = (1.0 + MOMENTUM[3]) * here[c] - STEP[2] * (curled[c] + m * mixed)
                    value = STEP[2] * here[c]
                    if j < 2:
                        first = d1[j, pol, c, plane - 1]
                        last = last - MOMENTUM[2] * first
                        value = value + STEP[1] * first
                    if j == 0:
                        value = value + STEP[0] * part(3 * pol + c, plane)
                    field[j, pol, c, plane - 3] = value + STEP[3] * last
                    if j == 2:
                        field[3, pol, c, plane - 3] = -(STEP[3] * STEP[2]) * (m * here[c])

    members = sent.shape[0]
    sent[...] = jnp.zeros(sent.shape, jnp.float32)

    def one_chunk(chunk, carry):
        feature = features[chunk]
        weight = row_weights(feature, 0, HALO * WINDOW, 2 * WINDOW)
        depth = depth_picks(feature)
        rows = []
        for j in range(DEGREE):
            for pol in range(2):
                for c in range(2):
                    values = field[j, pol, c].reshape(2 * WINDOW, LANES)
                    at_depth = sum(dot_nn(piece, depth) for piece in parts_of(values))
                    rows.append(jnp.sum(at_depth * weight, axis=0, keepdims=True))
        read = jnp.concatenate(rows, axis=0)
        pieces = jnp.concatenate(parts_of(read), axis=0)
        for block in range(members):
            spread = dot_nn(pieces, picks(places, block, chunk))
            sent[block] += spread[0:16] + spread[16:32] + spread[32:48]
        return carry

    lax.fori_loop(0, count[0], one_chunk, 0)


def forward_solve(windows, station_parts, grid_rows, members, grid_planes):
    shape = jax.ShapeDtypeStruct
    vmem = pl.BlockSpec(memory_space=pltpu.VMEM)
    smem = pl.BlockSpec(memory_space=pltpu.SMEM)
    blocks = station_parts[0].shape[0]
    return pl.pallas_call(
        lambda *refs: forward_kernel(grid_rows, grid_rows // members, grid_planes, *refs),
        out_shape=(
            shape((DEGREE, 2, 3, 2, WINDOW, LANES), jnp.float32),
            shape((blocks, 4 * DEGREE, LANES), jnp.float32),
            shape((PLANES - 2, WINDOW, LANES), jnp.float32),
        ),
        in_specs=[vmem] * 6 + [smem, vmem],
        out_specs=(vmem, vmem, vmem),
        scratch_shapes=[
            pltpu.VMEM((7, PLANES, WINDOW, LANES), jnp.float32),
            pltpu.VMEM((2, 2, 3, PLANES - 2, WINDOW, LANES), jnp.float32),
            pltpu.VMEM((3, 2, 3, PLANES - 4, WINDOW, LANES), jnp.float32),
        ],
        compiler_params=pltpu.CompilerParams(vmem_limit_bytes=VMEM_LIMIT),
        cost_estimate=pl.CostEstimate(flops=20_000_000_000, bytes_accessed=3_000_000, transcendentals=0),
        name="forward_solve",
    )(*windows, *station_parts)


def residual_kernel(grid_rows, own_rows, read, data, cells, moments, owned, staged):
    members = data.shape[0]
    total = read[0]
    for member in range(1, read.shape[0]):
        total = total + read[member]
    coefficients = [total[4 * j : 4 * j + 4] for j in range(DEGREE)]
    first = pl.multiple_of(lax.axis_index("space") * LANES, LANES)
    cell = cells[:, pl.ds(first, LANES)]
    y = jnp.min((cell // LANES) % grid_rows, axis=0, keepdims=True)
    mine = (y // own_rows) == lax.axis_index("period")
    sums = [jnp.zeros((4, LANES), jnp.float32) for _ in range(MOMENTS)]
    for member in range(members):
        shift = data[member, 8:9, :]
        delta = shift - CENTER
        value = coefficients[DEGREE - 1]
        for j in range(DEGREE - 2, -1, -1):
            value = value * delta + coefficients[j]
        owned[member] = jnp.where(mine, value, 0.0)
        weight = data[member, 4:8, :]
        term = shift * (weight * weight * (value - data[member, 0:4, :]))
        for number in range(MOMENTS):
            sums[number] = sums[number] + term
            if number + 1 < MOMENTS:
                term = term * delta
    staged[...] = jnp.zeros(staged.shape, jnp.float32)
    for number in range(MOMENTS):
        staged[4 * number : 4 * number + 4, :] = sums[number]
    value = staged[...]
    for member in range(moments.shape[0]):
        moments[member] = value


def residuals(read, data, cells, grid_rows, members):
    shape = jax.ShapeDtypeStruct
    vmem = pl.BlockSpec(memory_space=pltpu.VMEM)
    return pl.pallas_call(
        lambda *refs: residual_kernel(grid_rows, grid_rows // members, *refs),
        out_shape=(
            shape((read.shape[0], 32, LANES), jnp.float32),
            shape((members, 4, LANES), jnp.float32),
        ),
        in_specs=[vmem, vmem, vmem],
        out_specs=(vmem, vmem),
        scratch_shapes=[pltpu.VMEM((32, LANES), jnp.float32)],
        compiler_params=pltpu.CompilerParams(vmem_limit_bytes=VMEM_SMALL),
        name="residuals",
    )(read, data, cells)


def adjoint_kernel(
    grid_rows, own_rows, grid_planes, periods, moments, places, count, features, mass, field,
    gradient, d0, slope, d1, d2, picked, total,
):
    first_plane = first_window_plane()
    member = lax.axis_index("period")
    first_row = narrow_row(member, grid_rows, own_rows)
    inner = pl.ds(first_row - window_row(member, grid_rows, own_rows), NARROW)
    own = pl.ds(member * own_rows - first_row, own_rows)
    blocks = moments.shape[0]
    window_rows = PLANES * NARROW

    def add_chunk(chunk, fresh):
        feature = features[chunk]
        weight = row_weights(feature, 20, 0, window_rows)
        depth = depth_picks_and_differences(feature)
        depth = jnp.concatenate([depth, depth], axis=1)
        gathered = jnp.zeros((96, LANES), jnp.float32)
        for block in range(blocks):
            pieces = jnp.concatenate(parts_of(moments[block]), axis=0)
            gathered += dot_nt(pieces, picks(places, block, chunk))
        picked[...] = gathered[0:32] + gathered[32:64] + gathered[64:96]

        def one_field(number, carry):
            values = weight * picked[pl.ds(number, 1), :]
            high = values.astype(jnp.bfloat16)
            low = (values - high.astype(jnp.float32)).astype(jnp.bfloat16)
            placed = dot_nt(jnp.concatenate([high, low], axis=1), depth)
            if fresh:
                d0[number] = placed[:, :LANES]
                slope[number] = placed[:, LANES:]
            else:
                d0[number] += placed[:, :LANES]
                slope[number] += placed[:, LANES:]
            return carry

        lax.fori_loop(0, 4 * MOMENTS, one_field, 0, unroll=2 * MOMENTS)

    add_chunk(0, True)

    def one_chunk(chunk, carry):
        add_chunk(chunk, False)
        return carry

    lax.fori_loop(1, count[0], one_chunk, 0)

    def start(f, c, plane):
        return d0[2 * f + c, plane * NARROW : (plane + 1) * NARROW, :]

    def level_one(f, carry):
        def b(plane):
            return start(f, 0, plane), start(f, 1, plane), None

        def along_z(plane, c):
            return slope[2 * f + c, plane * NARROW : (plane + 1) * NARROW, :]

        for plane, here, curled in curl_curl(b, 1, 6, first_plane, grid_planes, along_z):
            m = mass[plane - 1, inner, :]
            for c in range(2):
                mixed = CENTER * here[c] + start(f + 2, c, plane)
                d1[f, c, plane - 1] = (
                    (1.0 + MOMENTUM[1]) * here[c] - STEP[0] * (curled[c] + m * mixed)
                )
            d1[f, 2, plane - 1] = -STEP[0] * curled[2]
        return carry

    lax.fori_loop(0, 2 * (MOMENTS - 1), level_one, 0, unroll=4)

    def level_two(f, carry):
        def get(plane):
            return tuple(d1[f, c, plane - 1] for c in range(3))

        for plane, here, curled in curl_curl(get, 2, 5, first_plane, grid_planes):
            m = mass[plane - 1, inner, :]
            for c in range(3):
                mixed = CENTER * here[c] + d1[f + 2, c, plane - 1]
                value = (1.0 + MOMENTUM[2]) * here[c] - STEP[1] * (curled[c] + m * mixed)
                if c < 2:
                    value = value - MOMENTUM[1] * start(f, c, plane)
                d2[f, c, plane - 2] = value
        return carry

    lax.fori_loop(0, 2 * (MOMENTS - 2), level_two, 0, unroll=2)

    total[...] = jnp.zeros(total.shape, jnp.float32)

    def level_three(f, carry):
        def get(plane):
            return tuple(d2[f, c, plane - 2] for c in range(3))

        for plane, here, curled in curl_curl(get, 3, 4, first_plane, grid_planes):
            m = mass[plane - 1, inner, :]
            added = None
            for c in range(3):
                mixed = CENTER * here[c] + d2[f + 2, c, plane - 2]
                first = d1[f, c, plane - 1]
                last = (
                    (1.0 + MOMENTUM[3]) * here[c] - MOMENTUM[2] * first
                    - STEP[2] * (curled[c] + m * mixed)
                )
                value = STEP[1] * first + STEP[2] * here[c] + STEP[3] * last
                if c < 2:
                    value = value + STEP[0] * start(f, c, plane)
                term = value * field[f, c, plane - 3, inner, :]
                added = term if added is None else added + term
            total[plane - 3] += added
        return carry

    lax.fori_loop(0, 2 * DEGREE, level_three, 0, unroll=8)
    gradient[...] = total[:, own, :] * (-1.0 / periods)


def adjoint_solve(moments, station_parts, mass, field, grid_rows, members, grid_planes):
    vmem = pl.BlockSpec(memory_space=pltpu.VMEM)
    smem = pl.BlockSpec(memory_space=pltpu.SMEM)
    own_rows = grid_rows // members
    return pl.pallas_call(
        lambda *refs: adjoint_kernel(grid_rows, own_rows, grid_planes, members, *refs),
        out_shape=jax.ShapeDtypeStruct((2, own_rows, LANES), jnp.float32),
        in_specs=[vmem, vmem, smem, vmem, vmem, vmem],
        out_specs=vmem,
        scratch_shapes=[
            pltpu.VMEM((4 * MOMENTS, PLANES * NARROW, LANES), jnp.float32),
            pltpu.VMEM((4 * MOMENTS, PLANES * NARROW, LANES), jnp.float32),
            pltpu.VMEM((2 * (MOMENTS - 1), 3, PLANES - 2, NARROW, LANES), jnp.float32),
            pltpu.VMEM((2 * (MOMENTS - 2), 3, PLANES - 4, NARROW, LANES), jnp.float32),
            pltpu.VMEM((32, LANES), jnp.float32),
            pltpu.VMEM((2, NARROW, LANES), jnp.float32),
        ],
        compiler_params=pltpu.CompilerParams(vmem_limit_bytes=VMEM_LIMIT),
        cost_estimate=pl.CostEstimate(flops=200_000_000, bytes_accessed=3_000_000, transcendentals=0),
        name="adjoint_solve",
    )(moments, *station_parts, mass, field.reshape(2 * DEGREE, 3, 2, WINDOW, LANES))


def shards(source, conductivity, period_shift, site_cells, site_weights, observed, data_weight):
    grid_rows = conductivity.shape[1]
    count = lax.axis_size("space")
    members = lax.axis_size("period")
    grid_planes = conductivity.shape[0] * count
    slab, beside, far_a, far_b, data = pack(
        source, conductivity, period_shift, observed, data_weight, members
    )

    def swapped(values, partner):
        pairs = []
        for i in range(count):
            j = partner(i)
            flip = 0 if i // 2 == j // 2 else 1
            if 0 <= j < count:
                pairs += [(i * members + t, j * members + (t ^ flip)) for t in range(members)]
        return lax.ppermute(values, ("space", "period"), pairs)

    windows = (
        slab,
        swapped(slab, lambda i: i ^ 1),
        swapped(beside, lambda i: i + 1 if i % 2 else i - 1),
        swapped(far_a, lambda i: i ^ 2),
        swapped(far_b, lambda i: i + 2 if i & 2 else i - 2),
    )
    mate, data, late_cells = lax.optimization_barrier((windows[1], data, site_cells))
    windows = (windows[0], mate, *windows[2:])
    data = lax.all_to_all(data, "period", 0, 0, tiled=True)
    station_parts = stations(late_cells, site_weights, grid_rows, members)
    field, sent, mass = forward_solve(windows, station_parts, grid_rows, members, grid_planes)
    sent, data = lax.optimization_barrier((sent, data))
    read = lax.all_to_all(sent, "space", 0, 0, tiled=True)
    moments, owned = residuals(read, data, site_cells, grid_rows, members)
    moments = lax.all_to_all(moments, "space", 0, 0, tiled=True)
    moments, owned = lax.optimization_barrier((moments, owned))
    owned = lax.all_to_all(owned, "period", 0, 0, tiled=True)
    gradient = adjoint_solve(moments, station_parts, mass, field, grid_rows, members, grid_planes)
    return jnp.sum(owned, axis=0, keepdims=True), gradient


def solution(mesh):
    placed = (
        P(None, None, "space", None, None),
        P("space", None, None),
        P("period"),
        P(),
        P(),
        P("period", None, "space"),
        P("period", None, "space"),
    )
    return jax.shard_map(
        shards,
        mesh=mesh,
        in_specs=placed,
        out_specs=(P("period", None, "space"), P("space", "period", None)),
        check_vma=False,
    )
```

```python
import jax
import jax.numpy as jnp
from jax import lax
from jax.experimental import pallas as pl
from jax.experimental.pallas import tpu as pltpu
from jax.sharding import PartitionSpec as P

SWEEPS = 4
LOWER_BOUND = 0.05
UPPER_BOUND = 16.0

CENTER = 1.25
HALO = SWEEPS - 1
PLANES = 2 + 2 * HALO
WINDOW = 32
NARROW = 24
DEGREE = SWEEPS
MOMENTS = 2 * SWEEPS - 1
LANES = 128
VMEM_SMALL = 6 * 1024 * 1024
VMEM_LIMIT = 16 * 1024 * 1024


def chebyshev_steps(sweep_count):
    center = 0.5 * (UPPER_BOUND + LOWER_BOUND)
    spread = 0.5 * (UPPER_BOUND - LOWER_BOUND)
    step_sizes = []
    momenta = []
    step_size = 1.0 / center
    for number in range(sweep_count):
        if number == 0:
            momentum = 0.0
        elif number == 1:
            momentum = 0.5 * (spread * step_size) ** 2
        else:
            momentum = (0.5 * spread * step_size) ** 2
        if number > 0:
            step_size = 1.0 / (center - momentum / step_size)
        step_sizes.append(step_size)
        momenta.append(momentum)
    return (step_sizes, momenta)


STEP, MOMENTUM = chebyshev_steps(SWEEPS)


def window_row(member, grid_rows, own_rows):
    first = member * own_rows - (WINDOW - own_rows) // 2
    return pl.multiple_of(jnp.clip(first, 0, grid_rows - WINDOW), 8)


def narrow_row(member, grid_rows, own_rows):
    return jnp.clip(member * own_rows - (NARROW - own_rows) // 2, 0, grid_rows - NARROW)


def first_window_plane():
    return lax.axis_index("space") * 2 - HALO


def iota(shape, dim):
    return lax.broadcasted_iota(jnp.int32, shape, dim)


def parts_of(values):
    high = values.astype(jnp.bfloat16)
    rest = values - high.astype(jnp.float32)
    middle = rest.astype(jnp.bfloat16)
    low = (rest - middle.astype(jnp.float32)).astype(jnp.bfloat16)
    return high, middle, low


def dot_nt(left, right):
    return lax.dot_general(left, right, (((1,), (1,)), ((), ())), preferred_element_type=jnp.float32)


def dot_nn(left, right):
    return lax.dot_general(left, right, (((1,), (0,)), ((), ())), preferred_element_type=jnp.float32)


def next_z(v):
    return jnp.where(iota(v.shape, 1) == v.shape[1] - 1, 0.0, pltpu.roll(v, v.shape[1] - 1, 1))


def last_z(v):
    return jnp.where(iota(v.shape, 1) == 0, 0.0, pltpu.roll(v, 1, 1))


def next_y(v):
    return jnp.where(iota(v.shape, 0) == v.shape[0] - 1, 0.0, pltpu.roll(v, v.shape[0] - 1, 0))


def last_y(v):
    return jnp.where(iota(v.shape, 0) == 0, 0.0, pltpu.roll(v, 1, 0))


def curl_curl(get, first, last, first_plane, planes_in_grid, along_z=None):
    before = None
    here = get(first - 1)
    for plane in range(first - 1, last + 1):
        after = get(plane + 1)
        east, north, down = here
        c2 = along_z(plane, 0) if along_z else next_z(east) - east
        if down is not None:
            c2 = c2 - (after[2] - down)
        c3 = (after[1] - north) - (next_y(east) - east)
        if plane < HALO and plane % 2 == 0:
            inside = jnp.where(first_plane + plane < 0, 0.0, 1.0)
            c2 = c2 * inside
            c3 = c3 * inside
        if plane >= first:
            c1 = -along_z(plane, 1) if along_z else north - next_z(north)
            if down is not None:
                c1 = c1 + (next_y(down) - down)
            a1 = (c3 - last_y(c3)) - (c2 - last_z(c2))
            a2 = (c1 - last_z(c1)) - (c3 - before[1])
            a3 = (c2 - before[0]) - (c1 - last_y(c1))
            if plane == HALO + 2:
                inside = jnp.where(first_plane + plane >= planes_in_grid, 0.0, 1.0)
                a1, a2, a3 = a1 * inside, a2 * inside, a3 * inside
            yield plane, here, (a1, a2, a3)
        before = (c2, c3)
        here = after


def pack_kernel(
    grid_rows, own_rows, source, conductivity, shift, observed, weight,
    slab, beside, far, data, pairs, sems,
):
    member = lax.axis_index("period")
    odd = lax.axis_index("space") % 2
    copies = [(observed.at[0], pairs.at[0]), (weight.at[0], pairs.at[1])]
    rows = pl.ds(window_row(member, grid_rows, own_rows), WINDOW)
    for pol in range(2):
        copies.append((source.at[pol, :, :, rows, :], slab.at[pl.ds(3 * pol, 3)]))
    copies.append((conductivity.at[:, rows, :], slab.at[6]))
    rows = pl.ds(window_row(member + 1 - 2 * (member % 2), grid_rows, own_rows), WINDOW)
    for pol in range(2):
        copies.append((source.at[pol, :, :, rows, :], beside.at[pl.ds(3 * pol, 3)]))
        copies.append((source.at[pol, :, 1 - odd, rows, :], far.at[pl.ds(3 * pol, 3)]))
    copies.append((conductivity.at[:, rows, :], beside.at[6]))
    started = [pltpu.make_async_copy(a, b, sems.at[i]) for i, (a, b) in enumerate(copies)]
    for copy in started:
        copy.start()
    for copy in started:
        copy.wait()
    for member in range(data.shape[0]):
        data[member, 0:4, :] = pairs[0]
        data[member, 4:8, :] = pairs[1]
        data[member, 8:16, :] = jnp.full((8, LANES), shift[0], jnp.float32)


def pack(source, conductivity, shift, observed, weight, members):
    grid_rows = source.shape[3]
    shape = jax.ShapeDtypeStruct
    hbm = pl.BlockSpec(memory_space=pltpu.HBM)
    vmem = pl.BlockSpec(memory_space=pltpu.VMEM)
    smem = pl.BlockSpec(memory_space=pltpu.SMEM)
    return pl.pallas_call(
        lambda *refs: pack_kernel(grid_rows, grid_rows // members, *refs),
        out_shape=(shape((7, 2, WINDOW, LANES), jnp.float32),) * 2
        + (shape((6, WINDOW, LANES), jnp.float32),)
        + (shape((members, 16, LANES), jnp.float32),),
        in_specs=[hbm, hbm, smem, hbm, hbm],
        out_specs=(vmem,) * 4,
        scratch_shapes=[pltpu.VMEM((2, 4, LANES), jnp.float32), pltpu.SemaphoreType.DMA((10,))],
        compiler_params=pltpu.CompilerParams(vmem_limit_bytes=VMEM_SMALL),
        name="pack",
    )(
        *(pltpu.with_memory_space_constraint(v, pltpu.HBM) for v in (source, conductivity)),
        shift,
        *(pltpu.with_memory_space_constraint(v, pltpu.HBM) for v in (observed, weight)),
    )


def stations_kernel(grid_rows, own_rows, cells, weights, places, count, features, marks, staged):
    member = lax.axis_index("period")
    first_own = member * own_rows
    first_row = window_row(member, grid_rows, own_rows)
    first_narrow = narrow_row(member, grid_rows, own_rows)
    plane_size = grid_rows * LANES
    cell = cells[...]
    x = cell // plane_size - first_window_plane()
    y = (cell // LANES) % grid_rows
    reached = (
        (x >= 0) & (x < PLANES)
        & (y >= first_own - HALO - 1) & (y < first_own + own_rows + HALO + 1)
    )
    row = jnp.where(reached, x * WINDOW + y - first_row, 0).astype(jnp.float32)
    narrow = jnp.where(reached, x * NARROW + y - first_narrow, 0).astype(jnp.float32)
    weight = jnp.where(reached, weights[...], 0.0)
    present = jnp.max(jnp.where(reached, 1.0, 0.0), axis=0, keepdims=True)
    blocks = cell.shape[1] // LANES
    staged[...] = jnp.zeros(staged.shape, jnp.float32)
    staged[0:4, :] = row
    staged[4:8, :] = (cell % LANES).astype(jnp.float32)
    staged[20:24, :] = narrow
    for number, part in enumerate(parts_of(weight)):
        staged[8 + 4 * number : 12 + 4 * number, :] = part.astype(jnp.float32)
    for block in range(blocks):
        marks[block : block + 1, :] = present[:, block * LANES : (block + 1) * LANES]
    mark = marks[...]
    square = (LANES, LANES)
    upto = jnp.where(iota(square, 0) <= iota(square, 1), 1.0, 0.0).astype(jnp.bfloat16)
    inner = dot_nn(mark.astype(jnp.bfloat16), upto)
    totals = dot_nn(mark.astype(jnp.bfloat16), jnp.ones(square, jnp.bfloat16))
    earlier = jnp.where(iota((blocks, blocks), 0) > iota((blocks, blocks), 1), 1.0, 0.0)
    offsets = dot_nn(earlier.astype(jnp.bfloat16), totals.astype(jnp.bfloat16))
    places[...] = jnp.where(mark > 0.0, inner + offsets - 1.0, -1.0).astype(jnp.int32)
    chunks = (jnp.sum(mark).astype(jnp.int32) + LANES - 1) // LANES
    count[0] = chunks

    def one_chunk(chunk, carry):
        gathered = jnp.zeros((staged.shape[0], LANES), jnp.float32)
        for block in range(blocks):
            feature = staged[:, block * LANES : (block + 1) * LANES].astype(jnp.bfloat16)
            gathered += dot_nt(feature, picks(places, block, chunk))
        features[chunk] = gathered
        return carry

    features[0] = jnp.zeros(features.shape[1:], jnp.float32)
    lax.fori_loop(0, chunks, one_chunk, 0)


def picks(places, block, chunk):
    wanted = places[block : block + 1, :] - chunk * LANES
    return jnp.where(iota((LANES, LANES), 0) == wanted, 1.0, 0.0).astype(jnp.bfloat16)


def stations(cells, weights, grid_rows, members):
    blocks = cells.shape[1] // LANES
    shape = jax.ShapeDtypeStruct
    vmem = pl.BlockSpec(memory_space=pltpu.VMEM)
    return pl.pallas_call(
        lambda *refs: stations_kernel(grid_rows, grid_rows // members, *refs),
        out_shape=(
            shape((blocks, LANES), jnp.int32),
            shape((1,), jnp.int32),
            shape((blocks, 32, LANES), jnp.float32),
        ),
        in_specs=[vmem, vmem],
        out_specs=(vmem, pl.BlockSpec(memory_space=pltpu.SMEM), vmem),
        scratch_shapes=[
            pltpu.VMEM((blocks, LANES), jnp.float32),
            pltpu.VMEM((32, cells.shape[1]), jnp.float32),
        ],
        compiler_params=pltpu.CompilerParams(vmem_limit_bytes=VMEM_LIMIT),
        cost_estimate=pl.CostEstimate(flops=10_000_000, bytes_accessed=200_000, transcendentals=0),
        name="stations",
    )(cells, weights)


def row_weights(feature, field, first, count):
    rows = (iota((count, LANES), 0) + first).astype(jnp.float32)
    total = jnp.zeros((count, LANES), jnp.float32)
    for q in range(4):
        weight = feature[8 + q : 9 + q] + feature[12 + q : 13 + q] + feature[16 + q : 17 + q]
        total += jnp.where(rows == feature[field + q : field + q + 1], weight, 0.0)
    return total


def depth_picks(feature):
    depth = iota((LANES, LANES), 0).astype(jnp.float32)
    return jnp.where(depth == feature[4:5], 1.0, 0.0).astype(jnp.bfloat16)


def depth_picks_and_differences(feature):
    depth = iota((LANES, LANES), 0).astype(jnp.float32)
    here = jnp.where(depth == feature[4:5], 1.0, 0.0)
    change = jnp.where(depth + 1.0 == feature[4:5], 1.0, 0.0) - here
    return jnp.concatenate([here, change], axis=0).astype(jnp.bfloat16)


def forward_kernel(
    grid_rows, own_rows, grid_planes, slab, mate, beside, far, relay, places, count, features,
    field, sent, mass, window, d1, d2,
):
    first_plane = first_window_plane()
    even = lax.axis_index("space") % 2 == 0
    for plane in range(2):
        here, there = mate[:, plane], beside[:, plane]
        window[:, 1 + plane] = jnp.where(even, there, here)
        window[:, 3 + plane] = slab[:, plane]
        window[:, 5 + plane] = jnp.where(even, here, there)
    window[0:6, 0] = jnp.where(even, far[...], relay[0:6, 1])
    window[0:6, PLANES - 1] = jnp.where(even, relay[0:6, 0], far[...])
    mass[...] = window[6, 1 : PLANES - 1]

    def part(number, plane):
        return window[number, plane]

    for pol in range(2):
        def b(plane, pol=pol):
            return tuple(part(3 * pol + c, plane) for c in range(3))

        for plane, here, curled in curl_curl(b, 1, 6, first_plane, grid_planes):
            m = mass[plane - 1]
            for c in range(3):
                heavy = m * here[c]
                d1[0, pol, c, plane - 1] = (
                    (1.0 + MOMENTUM[1]) * here[c] - STEP[0] * (curled[c] + CENTER * heavy)
                )
                d1[1, pol, c, plane - 1] = -STEP[0] * heavy

        def level1(j, pol=pol):
            return lambda plane: tuple(d1[j, pol, c, plane - 1] for c in range(3))

        for j in range(2):
            for plane, here, curled in curl_curl(level1(j), 2, 5, first_plane, grid_planes):
                m = mass[plane - 1]
                for c in range(3):
                    mixed = CENTER * here[c]
                    if j == 1:
                        mixed = mixed + d1[0, pol, c, plane - 1]
                    value = (1.0 + MOMENTUM[2]) * here[c] - STEP[1] * (curled[c] + m * mixed)
                    if j == 0:
                        value = value - MOMENTUM[1] * part(3 * pol + c, plane)
                    d2[j, pol, c, plane - 2] = value
                    if j == 1:
                        d2[2, pol, c, plane - 2] = -STEP[1] * (m * here[c])

        def level2(j, pol=pol):
            return lambda plane: tuple(d2[j, pol, c, plane - 2] for c in range(3))

        for j in range(3):
            for plane, here, curled in curl_curl(level2(j), 3, 4, first_plane, grid_planes):
                m = mass[plane - 1]
                for c in range(3):
                    mixed = CENTER * here[c]
                    if j > 0:
                        mixed = mixed + d2[j - 1, pol, c, plane - 2]
                    last = (1.0 + MOMENTUM[3]) * here[c] - STEP[2] * (curled[c] + m * mixed)
                    value = STEP[2] * here[c]
                    if j < 2:
                        first = d1[j, pol, c, plane - 1]
                        last = last - MOMENTUM[2] * first
                        value = value + STEP[1] * first
                    if j == 0:
                        value = value + STEP[0] * part(3 * pol + c, plane)
                    field[j, pol, c, plane - 3] = value + STEP[3] * last
                    if j == 2:
                        field[3, pol, c, plane - 3] = -(STEP[3] * STEP[2]) * (m * here[c])

    members = sent.shape[0]
    sent[...] = jnp.zeros(sent.shape, jnp.float32)

    def one_chunk(chunk, carry):
        feature = features[chunk]
        weight = row_weights(feature, 0, HALO * WINDOW, 2 * WINDOW)
        depth = depth_picks(feature)
        rows = []
        for j in range(DEGREE):
            for pol in range(2):
                for c in range(2):
                    values = field[j, pol, c].reshape(2 * WINDOW, LANES)
                    at_depth = sum(dot_nn(piece, depth) for piece in parts_of(values))
                    rows.append(jnp.sum(at_depth * weight, axis=0, keepdims=True))
        read = jnp.concatenate(rows, axis=0)
        pieces = jnp.concatenate(parts_of(read), axis=0)
        for block in range(members):
            spread = dot_nn(pieces, picks(places, block, chunk))
            sent[block] += spread[0:16] + spread[16:32] + spread[32:48]
        return carry

    lax.fori_loop(0, count[0], one_chunk, 0)


def forward_solve(windows, station_parts, grid_rows, members, grid_planes):
    shape = jax.ShapeDtypeStruct
    vmem = pl.BlockSpec(memory_space=pltpu.VMEM)
    smem = pl.BlockSpec(memory_space=pltpu.SMEM)
    blocks = station_parts[0].shape[0]
    return pl.pallas_call(
        lambda *refs: forward_kernel(grid_rows, grid_rows // members, grid_planes, *refs),
        out_shape=(
            shape((DEGREE, 2, 3, 2, WINDOW, LANES), jnp.float32),
            shape((blocks, 4 * DEGREE, LANES), jnp.float32),
            shape((PLANES - 2, WINDOW, LANES), jnp.float32),
        ),
        in_specs=[vmem] * 6 + [smem, vmem],
        out_specs=(vmem, vmem, vmem),
        scratch_shapes=[
            pltpu.VMEM((7, PLANES, WINDOW, LANES), jnp.float32),
            pltpu.VMEM((2, 2, 3, PLANES - 2, WINDOW, LANES), jnp.float32),
            pltpu.VMEM((3, 2, 3, PLANES - 4, WINDOW, LANES), jnp.float32),
        ],
        compiler_params=pltpu.CompilerParams(vmem_limit_bytes=VMEM_LIMIT),
        cost_estimate=pl.CostEstimate(flops=20_000_000_000, bytes_accessed=3_000_000, transcendentals=0),
        name="forward_solve",
    )(*windows, *station_parts)


def residual_kernel(grid_rows, own_rows, read, data, cells, moments, owned, staged):
    members = data.shape[0]
    total = read[0]
    for member in range(1, read.shape[0]):
        total = total + read[member]
    coefficients = [total[4 * j : 4 * j + 4] for j in range(DEGREE)]
    first = pl.multiple_of(lax.axis_index("space") * LANES, LANES)
    cell = cells[:, pl.ds(first, LANES)]
    y = jnp.min((cell // LANES) % grid_rows, axis=0, keepdims=True)
    mine = (y // own_rows) == lax.axis_index("period")
    sums = [jnp.zeros((4, LANES), jnp.float32) for _ in range(MOMENTS)]
    for member in range(members):
        shift = data[member, 8:9, :]
        delta = shift - CENTER
        value = coefficients[DEGREE - 1]
        for j in range(DEGREE - 2, -1, -1):
            value = value * delta + coefficients[j]
        owned[member] = jnp.where(mine, value, 0.0)
        weight = data[member, 4:8, :]
        term = shift * (weight * weight * (value - data[member, 0:4, :]))
        for number in range(MOMENTS):
            sums[number] = sums[number] + term
            if number + 1 < MOMENTS:
                term = term * delta
    staged[...] = jnp.zeros(staged.shape, jnp.float32)
    for number in range(MOMENTS):
        staged[4 * number : 4 * number + 4, :] = sums[number]
    value = staged[...]
    for member in range(moments.shape[0]):
        moments[member] = value


def residuals(read, data, cells, grid_rows, members):
    shape = jax.ShapeDtypeStruct
    vmem = pl.BlockSpec(memory_space=pltpu.VMEM)
    return pl.pallas_call(
        lambda *refs: residual_kernel(grid_rows, grid_rows // members, *refs),
        out_shape=(
            shape((read.shape[0], 32, LANES), jnp.float32),
            shape((members, 4, LANES), jnp.float32),
        ),
        in_specs=[vmem, vmem, vmem],
        out_specs=(vmem, vmem),
        scratch_shapes=[pltpu.VMEM((32, LANES), jnp.float32)],
        compiler_params=pltpu.CompilerParams(vmem_limit_bytes=VMEM_SMALL),
        name="residuals",
    )(read, data, cells)


def adjoint_kernel(
    grid_rows, own_rows, grid_planes, periods, moments, places, count, features, mass, field,
    gradient, d0, slope, d1, d2, picked, total,
):
    first_plane = first_window_plane()
    member = lax.axis_index("period")
    first_row = narrow_row(member, grid_rows, own_rows)
    inner = pl.ds(first_row - window_row(member, grid_rows, own_rows), NARROW)
    own = pl.ds(member * own_rows - first_row, own_rows)
    blocks = moments.shape[0]
    window_rows = PLANES * NARROW

    def add_chunk(chunk, fresh):
        feature = features[chunk]
        weight = row_weights(feature, 20, 0, window_rows)
        depth = depth_picks_and_differences(feature)
        depth = jnp.concatenate([depth, depth], axis=1)
        gathered = jnp.zeros((96, LANES), jnp.float32)
        for block in range(blocks):
            pieces = jnp.concatenate(parts_of(moments[block]), axis=0)
            gathered += dot_nt(pieces, picks(places, block, chunk))
        picked[...] = gathered[0:32] + gathered[32:64] + gathered[64:96]

        def one_field(number, carry):
            values = weight * picked[pl.ds(number, 1), :]
            high = values.astype(jnp.bfloat16)
            low = (values - high.astype(jnp.float32)).astype(jnp.bfloat16)
            placed = dot_nt(jnp.concatenate([high, low], axis=1), depth)
            if fresh:
                d0[number] = placed[:, :LANES]
                slope[number] = placed[:, LANES:]
            else:
                d0[number] += placed[:, :LANES]
                slope[number] += placed[:, LANES:]
            return carry

        lax.fori_loop(0, 4 * MOMENTS, one_field, 0, unroll=2 * MOMENTS)

    add_chunk(0, True)

    def one_chunk(chunk, carry):
        add_chunk(chunk, False)
        return carry

    lax.fori_loop(1, count[0], one_chunk, 0)

    def start(f, c, plane):
        return d0[2 * f + c, plane * NARROW : (plane + 1) * NARROW, :]

    def level_one(f, carry):
        def b(plane):
            return start(f, 0, plane), start(f, 1, plane), None

        def along_z(plane, c):
            return slope[2 * f + c, plane * NARROW : (plane + 1) * NARROW, :]

        for plane, here, curled in curl_curl(b, 1, 6, first_plane, grid_planes, along_z):
            m = mass[plane - 1, inner, :]
            for c in range(2):
                mixed = CENTER * here[c] + start(f + 2, c, plane)
                d1[f, c, plane - 1] = (
                    (1.0 + MOMENTUM[1]) * here[c] - STEP[0] * (curled[c] + m * mixed)
                )
            d1[f, 2, plane - 1] = -STEP[0] * curled[2]
        return carry

    lax.fori_loop(0, 2 * (MOMENTS - 1), level_one, 0, unroll=4)

    def level_two(f, carry):
        def get(plane):
            return tuple(d1[f, c, plane - 1] for c in range(3))

        for plane, here, curled in curl_curl(get, 2, 5, first_plane, grid_planes):
            m = mass[plane - 1, inner, :]
            for c in range(3):
                mixed = CENTER * here[c] + d1[f + 2, c, plane - 1]
                value = (1.0 + MOMENTUM[2]) * here[c] - STEP[1] * (curled[c] + m * mixed)
                if c < 2:
                    value = value - MOMENTUM[1] * start(f, c, plane)
                d2[f, c, plane - 2] = value
        return carry

    lax.fori_loop(0, 2 * (MOMENTS - 2), level_two, 0, unroll=2)

    total[...] = jnp.zeros(total.shape, jnp.float32)

    def level_three(f, carry):
        def get(plane):
            return tuple(d2[f, c, plane - 2] for c in range(3))

        for plane, here, curled in curl_curl(get, 3, 4, first_plane, grid_planes):
            m = mass[plane - 1, inner, :]
            added = None
            for c in range(3):
                mixed = CENTER * here[c] + d2[f + 2, c, plane - 2]
                first = d1[f, c, plane - 1]
                last = (
                    (1.0 + MOMENTUM[3]) * here[c] - MOMENTUM[2] * first
                    - STEP[2] * (curled[c] + m * mixed)
                )
                value = STEP[1] * first + STEP[2] * here[c] + STEP[3] * last
                if c < 2:
                    value = value + STEP[0] * start(f, c, plane)
                term = value * field[f, c, plane - 3, inner, :]
                added = term if added is None else added + term
            total[plane - 3] += added
        return carry

    lax.fori_loop(0, 2 * DEGREE, level_three, 0, unroll=8)
    gradient[...] = total[:, own, :] * (-1.0 / periods)


def adjoint_solve(moments, station_parts, mass, field, grid_rows, members, grid_planes):
    vmem = pl.BlockSpec(memory_space=pltpu.VMEM)
    smem = pl.BlockSpec(memory_space=pltpu.SMEM)
    own_rows = grid_rows // members
    return pl.pallas_call(
        lambda *refs: adjoint_kernel(grid_rows, own_rows, grid_planes, members, *refs),
        out_shape=jax.ShapeDtypeStruct((2, own_rows, LANES), jnp.float32),
        in_specs=[vmem, vmem, smem, vmem, vmem, vmem],
        out_specs=vmem,
        scratch_shapes=[
            pltpu.VMEM((4 * MOMENTS, PLANES * NARROW, LANES), jnp.float32),
            pltpu.VMEM((4 * MOMENTS, PLANES * NARROW, LANES), jnp.float32),
            pltpu.VMEM((2 * (MOMENTS - 1), 3, PLANES - 2, NARROW, LANES), jnp.float32),
            pltpu.VMEM((2 * (MOMENTS - 2), 3, PLANES - 4, NARROW, LANES), jnp.float32),
            pltpu.VMEM((32, LANES), jnp.float32),
            pltpu.VMEM((2, NARROW, LANES), jnp.float32),
        ],
        compiler_params=pltpu.CompilerParams(vmem_limit_bytes=VMEM_LIMIT),
        cost_estimate=pl.CostEstimate(flops=200_000_000, bytes_accessed=3_000_000, transcendentals=0),
        name="adjoint_solve",
    )(moments, *station_parts, mass, field.reshape(2 * DEGREE, 3, 2, WINDOW, LANES))


def shards(source, conductivity, period_shift, site_cells, site_weights, observed, data_weight):
    grid_rows = conductivity.shape[1]
    count = lax.axis_size("space")
    members = lax.axis_size("period")
    grid_planes = conductivity.shape[0] * count
    slab, beside, far, data = pack(
        source, conductivity, period_shift, observed, data_weight, members
    )

    def swapped(values, partner):
        pairs = []
        for i in range(count):
            j = partner(i)
            flip = 0 if i // 2 == j // 2 else 1
            if 0 <= j < count:
                pairs += [(i * members + t, j * members + (t ^ flip)) for t in range(members)]
        return lax.ppermute(values, ("space", "period"), pairs)

    mate = swapped(slab, lambda i: i ^ 1)
    beside = swapped(beside, lambda i: i + 1 if i % 2 else i - 1)
    far = swapped(far, lambda i: i - 2 if i % 2 else i + 2)
    mate, data, late_cells = lax.optimization_barrier((mate, data, site_cells))
    data = lax.all_to_all(data, "period", 0, 0, tiled=True)
    places, *lists = stations(late_cells, site_weights, grid_rows, members)
    beside, far, places = lax.optimization_barrier((beside, far, places))
    station_parts = (places, *lists)
    windows = (slab, mate, beside, far, swapped(beside, lambda i: i ^ 1))
    field, sent, mass = forward_solve(windows, station_parts, grid_rows, members, grid_planes)
    sent, data = lax.optimization_barrier((sent, data))
    read = lax.all_to_all(sent, "space", 0, 0, tiled=True)
    moments, owned = residuals(read, data, site_cells, grid_rows, members)
    moments = lax.all_to_all(moments, "space", 0, 0, tiled=True)
    moments, owned = lax.optimization_barrier((moments, owned))
    owned = lax.all_to_all(owned, "period", 0, 0, tiled=True)
    gradient = adjoint_solve(moments, station_parts, mass, field, grid_rows, members, grid_planes)
    return jnp.sum(owned, axis=0, keepdims=True), gradient


def solution(mesh):
    placed = (
        P(None, None, "space", None, None),
        P("space", None, None),
        P("period"),
        P(),
        P(),
        P("period", None, "space"),
        P("period", None, "space"),
    )
    return jax.shard_map(
        shards,
        mesh=mesh,
        in_specs=placed,
        out_specs=(P("period", None, "space"), P("space", "period", None)),
        check_vma=False,
    )
```

```python
import jax
import jax.numpy as jnp
from jax import lax
from jax.experimental import pallas as pl
from jax.experimental.pallas import tpu as pltpu
from jax.sharding import PartitionSpec as P

SWEEPS = 4
LOWER_BOUND = 0.05
UPPER_BOUND = 16.0

CENTER = 1.25
HALO = SWEEPS - 1
PLANES = 2 + 2 * HALO
WINDOW = 32
NARROW = 24
DEGREE = SWEEPS
MOMENTS = 2 * SWEEPS - 1
LANES = 128
VMEM_SMALL = 6 * 1024 * 1024
VMEM_LIMIT = 16 * 1024 * 1024


def chebyshev_steps(sweep_count):
    center = 0.5 * (UPPER_BOUND + LOWER_BOUND)
    spread = 0.5 * (UPPER_BOUND - LOWER_BOUND)
    step_sizes = []
    momenta = []
    step_size = 1.0 / center
    for number in range(sweep_count):
        if number == 0:
            momentum = 0.0
        elif number == 1:
            momentum = 0.5 * (spread * step_size) ** 2
        else:
            momentum = (0.5 * spread * step_size) ** 2
        if number > 0:
            step_size = 1.0 / (center - momentum / step_size)
        step_sizes.append(step_size)
        momenta.append(momentum)
    return (step_sizes, momenta)


STEP, MOMENTUM = chebyshev_steps(SWEEPS)


def window_row(member, grid_rows, own_rows):
    first = member * own_rows - (WINDOW - own_rows) // 2
    return pl.multiple_of(jnp.clip(first, 0, grid_rows - WINDOW), 8)


def narrow_row(member, grid_rows, own_rows):
    return jnp.clip(member * own_rows - (NARROW - own_rows) // 2, 0, grid_rows - NARROW)


def first_window_plane():
    return lax.axis_index("space") * 2 - HALO


def iota(shape, dim):
    return lax.broadcasted_iota(jnp.int32, shape, dim)


def parts_of(values):
    high = values.astype(jnp.bfloat16)
    rest = values - high.astype(jnp.float32)
    middle = rest.astype(jnp.bfloat16)
    low = (rest - middle.astype(jnp.float32)).astype(jnp.bfloat16)
    return high, middle, low


def dot_nt(left, right):
    return lax.dot_general(left, right, (((1,), (1,)), ((), ())), preferred_element_type=jnp.float32)


def dot_nn(left, right):
    return lax.dot_general(left, right, (((1,), (0,)), ((), ())), preferred_element_type=jnp.float32)


def next_z(v):
    return jnp.where(iota(v.shape, 1) == v.shape[1] - 1, 0.0, pltpu.roll(v, v.shape[1] - 1, 1))


def last_z(v):
    return jnp.where(iota(v.shape, 1) == 0, 0.0, pltpu.roll(v, 1, 1))


def next_y(v):
    return jnp.where(iota(v.shape, 0) == v.shape[0] - 1, 0.0, pltpu.roll(v, v.shape[0] - 1, 0))


def last_y(v):
    return jnp.where(iota(v.shape, 0) == 0, 0.0, pltpu.roll(v, 1, 0))


def curl_curl(get, first, last, first_plane, planes_in_grid, along_z=None):
    before = None
    here = get(first - 1)
    for plane in range(first - 1, last + 1):
        after = get(plane + 1)
        east, north, down = here
        c2 = along_z(plane, 0) if along_z else next_z(east) - east
        if down is not None:
            c2 = c2 - (after[2] - down)
        c3 = (after[1] - north) - (next_y(east) - east)
        if plane < HALO and plane % 2 == 0:
            inside = jnp.where(first_plane + plane < 0, 0.0, 1.0)
            c2 = c2 * inside
            c3 = c3 * inside
        if plane >= first:
            c1 = -along_z(plane, 1) if along_z else north - next_z(north)
            if down is not None:
                c1 = c1 + (next_y(down) - down)
            a1 = (c3 - last_y(c3)) - (c2 - last_z(c2))
            a2 = (c1 - last_z(c1)) - (c3 - before[1])
            a3 = (c2 - before[0]) - (c1 - last_y(c1))
            if plane == HALO + 2:
                inside = jnp.where(first_plane + plane >= planes_in_grid, 0.0, 1.0)
                a1, a2, a3 = a1 * inside, a2 * inside, a3 * inside
            yield plane, here, (a1, a2, a3)
        before = (c2, c3)
        here = after


def pack_kernel(
    grid_rows, own_rows, source, conductivity, shift, observed, weight,
    slab, beside, data, pairs, sems,
):
    member = lax.axis_index("period")
    odd = lax.axis_index("space") % 2
    copies = [(observed.at[0], pairs.at[0]), (weight.at[0], pairs.at[1])]
    rows = pl.ds(window_row(member, grid_rows, own_rows), WINDOW)
    for pol in range(2):
        copies.append((source.at[pol, :, :, rows, :], slab.at[pl.ds(3 * pol, 3)]))
    copies.append((conductivity.at[:, rows, :], slab.at[6]))
    rows = pl.ds(window_row(member + 1 - 2 * (member % 2), grid_rows, own_rows), WINDOW)
    for pol in range(2):
        copies.append((source.at[pol, :, :, rows, :], beside.at[pl.ds(3 * pol, 3)]))
        for c in range(3):
            number = 3 * pol + c
            copies.append((source.at[pol, c, 1 - odd, rows, :], slab.at[7 + number // 2, number % 2]))
    copies.append((conductivity.at[:, rows, :], beside.at[6]))
    started = [pltpu.make_async_copy(a, b, sems.at[i]) for i, (a, b) in enumerate(copies)]
    for copy in started:
        copy.start()
    for copy in started:
        copy.wait()
    for member in range(data.shape[0]):
        data[member, 0:4, :] = pairs[0]
        data[member, 4:8, :] = pairs[1]
        data[member, 8:16, :] = jnp.full((8, LANES), shift[0], jnp.float32)


def pack(source, conductivity, shift, observed, weight, members):
    grid_rows = source.shape[3]
    shape = jax.ShapeDtypeStruct
    hbm = pl.BlockSpec(memory_space=pltpu.HBM)
    vmem = pl.BlockSpec(memory_space=pltpu.VMEM)
    smem = pl.BlockSpec(memory_space=pltpu.SMEM)
    return pl.pallas_call(
        lambda *refs: pack_kernel(grid_rows, grid_rows // members, *refs),
        out_shape=(
            shape((10, 2, WINDOW, LANES), jnp.float32),
            shape((7, 2, WINDOW, LANES), jnp.float32),
        )
        + (shape((members, 16, LANES), jnp.float32),),
        in_specs=[hbm, hbm, smem, hbm, hbm],
        out_specs=(vmem,) * 3,
        scratch_shapes=[pltpu.VMEM((2, 4, LANES), jnp.float32), pltpu.SemaphoreType.DMA((14,))],
        compiler_params=pltpu.CompilerParams(vmem_limit_bytes=VMEM_SMALL),
        name="pack",
    )(
        *(pltpu.with_memory_space_constraint(v, pltpu.HBM) for v in (source, conductivity)),
        shift,
        *(pltpu.with_memory_space_constraint(v, pltpu.HBM) for v in (observed, weight)),
    )


def extend_kernel(beside, mate, payload):
    payload[0:7] = beside[...]
    payload[7:10] = mate[7:10]


def extend(beside, mate):
    vmem = pl.BlockSpec(memory_space=pltpu.VMEM)
    return pl.pallas_call(
        extend_kernel,
        out_shape=jax.ShapeDtypeStruct((10, 2, WINDOW, LANES), jnp.float32),
        in_specs=[vmem, vmem],
        out_specs=vmem,
        compiler_params=pltpu.CompilerParams(vmem_limit_bytes=VMEM_SMALL),
        name="extend",
    )(beside, mate)


def stations_kernel(grid_rows, own_rows, cells, weights, places, count, features, marks, staged):
    member = lax.axis_index("period")
    first_own = member * own_rows
    first_row = window_row(member, grid_rows, own_rows)
    first_narrow = narrow_row(member, grid_rows, own_rows)
    plane_size = grid_rows * LANES
    cell = cells[...]
    x = cell // plane_size - first_window_plane()
    y = (cell // LANES) % grid_rows
    reached = (
        (x >= 0) & (x < PLANES)
        & (y >= first_own - HALO - 1) & (y < first_own + own_rows + HALO + 1)
    )
    row = jnp.where(reached, x * WINDOW + y - first_row, 0).astype(jnp.float32)
    narrow = jnp.where(reached, x * NARROW + y - first_narrow, 0).astype(jnp.float32)
    weight = jnp.where(reached, weights[...], 0.0)
    present = jnp.max(jnp.where(reached, 1.0, 0.0), axis=0, keepdims=True)
    blocks = cell.shape[1] // LANES
    staged[...] = jnp.zeros(staged.shape, jnp.float32)
    staged[0:4, :] = row
    staged[4:8, :] = (cell % LANES).astype(jnp.float32)
    staged[20:24, :] = narrow
    for number, part in enumerate(parts_of(weight)):
        staged[8 + 4 * number : 12 + 4 * number, :] = part.astype(jnp.float32)
    for block in range(blocks):
        marks[block : block + 1, :] = present[:, block * LANES : (block + 1) * LANES]
    mark = marks[...]
    square = (LANES, LANES)
    upto = jnp.where(iota(square, 0) <= iota(square, 1), 1.0, 0.0).astype(jnp.bfloat16)
    inner = dot_nn(mark.astype(jnp.bfloat16), upto)
    totals = dot_nn(mark.astype(jnp.bfloat16), jnp.ones(square, jnp.bfloat16))
    earlier = jnp.where(iota((blocks, blocks), 0) > iota((blocks, blocks), 1), 1.0, 0.0)
    offsets = dot_nn(earlier.astype(jnp.bfloat16), totals.astype(jnp.bfloat16))
    places[...] = jnp.where(mark > 0.0, inner + offsets - 1.0, -1.0).astype(jnp.int32)
    chunks = (jnp.sum(mark).astype(jnp.int32) + LANES - 1) // LANES
    count[0] = chunks

    def one_chunk(chunk, carry):
        gathered = jnp.zeros((staged.shape[0], LANES), jnp.float32)
        for block in range(blocks):
            feature = staged[:, block * LANES : (block + 1) * LANES].astype(jnp.bfloat16)
            gathered += dot_nt(feature, picks(places, block, chunk))
        features[chunk] = gathered
        return carry

    features[0] = jnp.zeros(features.shape[1:], jnp.float32)
    lax.fori_loop(0, chunks, one_chunk, 0)


def picks(places, block, chunk):
    wanted = places[block : block + 1, :] - chunk * LANES
    return jnp.where(iota((LANES, LANES), 0) == wanted, 1.0, 0.0).astype(jnp.bfloat16)


def stations(cells, weights, grid_rows, members):
    blocks = cells.shape[1] // LANES
    shape = jax.ShapeDtypeStruct
    vmem = pl.BlockSpec(memory_space=pltpu.VMEM)
    return pl.pallas_call(
        lambda *refs: stations_kernel(grid_rows, grid_rows // members, *refs),
        out_shape=(
            shape((blocks, LANES), jnp.int32),
            shape((1,), jnp.int32),
            shape((blocks, 32, LANES), jnp.float32),
        ),
        in_specs=[vmem, vmem],
        out_specs=(vmem, pl.BlockSpec(memory_space=pltpu.SMEM), vmem),
        scratch_shapes=[
            pltpu.VMEM((blocks, LANES), jnp.float32),
            pltpu.VMEM((32, cells.shape[1]), jnp.float32),
        ],
        compiler_params=pltpu.CompilerParams(vmem_limit_bytes=VMEM_LIMIT),
        cost_estimate=pl.CostEstimate(flops=10_000_000, bytes_accessed=200_000, transcendentals=0),
        name="stations",
    )(cells, weights)


def row_weights(feature, field, first, count):
    rows = (iota((count, LANES), 0) + first).astype(jnp.float32)
    total = jnp.zeros((count, LANES), jnp.float32)
    for q in range(4):
        weight = feature[8 + q : 9 + q] + feature[12 + q : 13 + q] + feature[16 + q : 17 + q]
        total += jnp.where(rows == feature[field + q : field + q + 1], weight, 0.0)
    return total


def depth_picks(feature):
    depth = iota((LANES, LANES), 0).astype(jnp.float32)
    return jnp.where(depth == feature[4:5], 1.0, 0.0).astype(jnp.bfloat16)


def depth_picks_and_differences(feature):
    depth = iota((LANES, LANES), 0).astype(jnp.float32)
    here = jnp.where(depth == feature[4:5], 1.0, 0.0)
    change = jnp.where(depth + 1.0 == feature[4:5], 1.0, 0.0) - here
    return jnp.concatenate([here, change], axis=0).astype(jnp.bfloat16)


def forward_kernel(
    grid_rows, own_rows, grid_planes, slab, mate, beside, relay, places, count, features,
    field, sent, mass, window, d1, d2,
):
    first_plane = first_window_plane()
    even = lax.axis_index("space") % 2 == 0
    for plane in range(2):
        here, there = mate[0:7, plane], beside[0:7, plane]
        window[:, 1 + plane] = jnp.where(even, there, here)
        window[:, 3 + plane] = slab[0:7, plane]
        window[:, 5 + plane] = jnp.where(even, here, there)
    far = beside[7:10].reshape(6, WINDOW, LANES)
    window[0:6, 0] = jnp.where(even, far, relay[0:6, 1])
    window[0:6, PLANES - 1] = jnp.where(even, relay[0:6, 0], far)
    mass[...] = window[6, 1 : PLANES - 1]

    def part(number, plane):
        return window[number, plane]

    for pol in range(2):
        def b(plane, pol=pol):
            return tuple(part(3 * pol + c, plane) for c in range(3))

        for plane, here, curled in curl_curl(b, 1, 6, first_plane, grid_planes):
            m = mass[plane - 1]
            for c in range(3):
                heavy = m * here[c]
                d1[0, pol, c, plane - 1] = (
                    (1.0 + MOMENTUM[1]) * here[c] - STEP[0] * (curled[c] + CENTER * heavy)
                )
                d1[1, pol, c, plane - 1] = -STEP[0] * heavy

        def level1(j, pol=pol):
            return lambda plane: tuple(d1[j, pol, c, plane - 1] for c in range(3))

        for j in range(2):
            for plane, here, curled in curl_curl(level1(j), 2, 5, first_plane, grid_planes):
                m = mass[plane - 1]
                for c in range(3):
                    mixed = CENTER * here[c]
                    if j == 1:
                        mixed = mixed + d1[0, pol, c, plane - 1]
                    value = (1.0 + MOMENTUM[2]) * here[c] - STEP[1] * (curled[c] + m * mixed)
                    if j == 0:
                        value = value - MOMENTUM[1] * part(3 * pol + c, plane)
                    d2[j, pol, c, plane - 2] = value
                    if j == 1:
                        d2[2, pol, c, plane - 2] = -STEP[1] * (m * here[c])

        def level2(j, pol=pol):
            return lambda plane: tuple(d2[j, pol, c, plane - 2] for c in range(3))

        for j in range(3):
            for plane, here, curled in curl_curl(level2(j), 3, 4, first_plane, grid_planes):
                m = mass[plane - 1]
                for c in range(3):
                    mixed = CENTER * here[c]
                    if j > 0:
                        mixed = mixed + d2[j - 1, pol, c, plane - 2]
                    last = (1.0 + MOMENTUM[3]) * here[c] - STEP[2] * (curled[c] + m * mixed)
                    value = STEP[2] * here[c]
                    if j < 2:
                        first = d1[j, pol, c, plane - 1]
                        last = last - MOMENTUM[2] * first
                        value = value + STEP[1] * first
                    if j == 0:
                        value = value + STEP[0] * part(3 * pol + c, plane)
                    field[j, pol, c, plane - 3] = value + STEP[3] * last
                    if j == 2:
                        field[3, pol, c, plane - 3] = -(STEP[3] * STEP[2]) * (m * here[c])

    members = sent.shape[0]
    sent[...] = jnp.zeros(sent.shape, jnp.float32)

    def one_chunk(chunk, carry):
        feature = features[chunk]
        weight = row_weights(feature, 0, HALO * WINDOW, 2 * WINDOW)
        depth = depth_picks(feature)
        rows = []
        stacked = jnp.concatenate([depth] * 3, axis=0)
        for j in range(DEGREE):
            values = field[j, :, 0:2].reshape(8 * WINDOW, LANES)
            at_depth = dot_nn(jnp.concatenate(parts_of(values), axis=1), stacked)
            for number in range(4):
                part = at_depth[2 * WINDOW * number : 2 * WINDOW * (number + 1)]
                rows.append(jnp.sum(part * weight, axis=0, keepdims=True))
        read = jnp.concatenate(rows, axis=0)
        pieces = jnp.concatenate(parts_of(read), axis=0)
        for block in range(members):
            spread = dot_nn(pieces, picks(places, block, chunk))
            sent[block] += spread[0:16] + spread[16:32] + spread[32:48]
        return carry

    lax.fori_loop(0, count[0], one_chunk, 0)


def forward_solve(windows, station_parts, grid_rows, members, grid_planes):
    shape = jax.ShapeDtypeStruct
    vmem = pl.BlockSpec(memory_space=pltpu.VMEM)
    smem = pl.BlockSpec(memory_space=pltpu.SMEM)
    blocks = station_parts[0].shape[0]
    return pl.pallas_call(
        lambda *refs: forward_kernel(grid_rows, grid_rows // members, grid_planes, *refs),
        out_shape=(
            shape((DEGREE, 2, 3, 2, WINDOW, LANES), jnp.float32),
            shape((blocks, 4 * DEGREE, LANES), jnp.float32),
            shape((PLANES - 2, WINDOW, LANES), jnp.float32),
        ),
        in_specs=[vmem] * 5 + [smem, vmem],
        out_specs=(vmem, vmem, vmem),
        scratch_shapes=[
            pltpu.VMEM((7, PLANES, WINDOW, LANES), jnp.float32),
            pltpu.VMEM((2, 2, 3, PLANES - 2, WINDOW, LANES), jnp.float32),
            pltpu.VMEM((3, 2, 3, PLANES - 4, WINDOW, LANES), jnp.float32),
        ],
        compiler_params=pltpu.CompilerParams(vmem_limit_bytes=VMEM_LIMIT),
        cost_estimate=pl.CostEstimate(flops=20_000_000_000, bytes_accessed=3_000_000, transcendentals=0),
        name="forward_solve",
    )(*windows, *station_parts)


def residual_kernel(grid_rows, own_rows, read, data, cells, moments, owned, staged):
    members = data.shape[0]
    total = read[0]
    for member in range(1, read.shape[0]):
        total = total + read[member]
    coefficients = [total[4 * j : 4 * j + 4] for j in range(DEGREE)]
    first = pl.multiple_of(lax.axis_index("space") * LANES, LANES)
    cell = cells[:, pl.ds(first, LANES)]
    y = jnp.min((cell // LANES) % grid_rows, axis=0, keepdims=True)
    mine = (y // own_rows) == lax.axis_index("period")
    sums = [jnp.zeros((4, LANES), jnp.float32) for _ in range(MOMENTS)]
    for member in range(members):
        shift = data[member, 8:9, :]
        delta = shift - CENTER
        value = coefficients[DEGREE - 1]
        for j in range(DEGREE - 2, -1, -1):
            value = value * delta + coefficients[j]
        owned[member] = jnp.where(mine, value, 0.0)
        weight = data[member, 4:8, :]
        term = shift * (weight * weight * (value - data[member, 0:4, :]))
        for number in range(MOMENTS):
            sums[number] = sums[number] + term
            if number + 1 < MOMENTS:
                term = term * delta
    staged[...] = jnp.zeros(staged.shape, jnp.float32)
    for number in range(MOMENTS):
        staged[4 * number : 4 * number + 4, :] = sums[number]
    value = staged[...]
    for member in range(moments.shape[0]):
        moments[member] = value


def residuals(read, data, cells, grid_rows, members):
    shape = jax.ShapeDtypeStruct
    vmem = pl.BlockSpec(memory_space=pltpu.VMEM)
    return pl.pallas_call(
        lambda *refs: residual_kernel(grid_rows, grid_rows // members, *refs),
        out_shape=(
            shape((read.shape[0], 32, LANES), jnp.float32),
            shape((members, 4, LANES), jnp.float32),
        ),
        in_specs=[vmem, vmem, vmem],
        out_specs=(vmem, vmem),
        scratch_shapes=[pltpu.VMEM((32, LANES), jnp.float32)],
        compiler_params=pltpu.CompilerParams(vmem_limit_bytes=VMEM_SMALL),
        name="residuals",
    )(read, data, cells)


def adjoint_kernel(
    grid_rows, own_rows, grid_planes, periods, moments, places, count, features, mass, field,
    gradient, d0, slope, d1, d2, picked, total,
):
    first_plane = first_window_plane()
    member = lax.axis_index("period")
    first_row = narrow_row(member, grid_rows, own_rows)
    inner = pl.ds(first_row - window_row(member, grid_rows, own_rows), NARROW)
    own = pl.ds(member * own_rows - first_row, own_rows)
    blocks = moments.shape[0]
    window_rows = PLANES * NARROW

    def add_chunk(chunk, fresh):
        feature = features[chunk]
        weight = row_weights(feature, 20, 0, window_rows)
        depth = depth_picks_and_differences(feature)
        depth = jnp.concatenate([depth, depth], axis=1)
        gathered = jnp.zeros((96, LANES), jnp.float32)
        for block in range(blocks):
            pieces = jnp.concatenate(parts_of(moments[block]), axis=0)
            gathered += dot_nt(pieces, picks(places, block, chunk))
        picked[...] = gathered[0:32] + gathered[32:64] + gathered[64:96]

        def one_field(number, carry):
            values = weight * picked[pl.ds(number, 1), :]
            high = values.astype(jnp.bfloat16)
            low = (values - high.astype(jnp.float32)).astype(jnp.bfloat16)
            placed = dot_nt(jnp.concatenate([high, low], axis=1), depth)
            if fresh:
                d0[number] = placed[:, :LANES]
                slope[number] = placed[:, LANES:]
            else:
                d0[number] += placed[:, :LANES]
                slope[number] += placed[:, LANES:]
            return carry

        lax.fori_loop(0, 4 * MOMENTS, one_field, 0, unroll=2 * MOMENTS)

    add_chunk(0, True)

    def one_chunk(chunk, carry):
        add_chunk(chunk, False)
        return carry

    lax.fori_loop(1, count[0], one_chunk, 0)

    def start(f, c, plane):
        return d0[2 * f + c, plane * NARROW : (plane + 1) * NARROW, :]

    def level_one(f, carry):
        def b(plane):
            return start(f, 0, plane), start(f, 1, plane), None

        def along_z(plane, c):
            return slope[2 * f + c, plane * NARROW : (plane + 1) * NARROW, :]

        for plane, here, curled in curl_curl(b, 1, 6, first_plane, grid_planes, along_z):
            m = mass[plane - 1, inner, :]
            for c in range(2):
                mixed = CENTER * here[c] + start(f + 2, c, plane)
                d1[f, c, plane - 1] = (
                    (1.0 + MOMENTUM[1]) * here[c] - STEP[0] * (curled[c] + m * mixed)
                )
            d1[f, 2, plane - 1] = -STEP[0] * curled[2]
        return carry

    lax.fori_loop(0, 2 * (MOMENTS - 1), level_one, 0, unroll=4)

    def level_two(f, carry):
        def get(plane):
            return tuple(d1[f, c, plane - 1] for c in range(3))

        for plane, here, curled in curl_curl(get, 2, 5, first_plane, grid_planes):
            m = mass[plane - 1, inner, :]
            for c in range(3):
                mixed = CENTER * here[c] + d1[f + 2, c, plane - 1]
                value = (1.0 + MOMENTUM[2]) * here[c] - STEP[1] * (curled[c] + m * mixed)
                if c < 2:
                    value = value - MOMENTUM[1] * start(f, c, plane)
                d2[f, c, plane - 2] = value
        return carry

    lax.fori_loop(0, 2 * (MOMENTS - 2), level_two, 0, unroll=2)

    total[...] = jnp.zeros(total.shape, jnp.float32)

    def level_three(f, carry):
        def get(plane):
            return tuple(d2[f, c, plane - 2] for c in range(3))

        for plane, here, curled in curl_curl(get, 3, 4, first_plane, grid_planes):
            m = mass[plane - 1, inner, :]
            added = None
            for c in range(3):
                mixed = CENTER * here[c] + d2[f + 2, c, plane - 2]
                first = d1[f, c, plane - 1]
                last = (
                    (1.0 + MOMENTUM[3]) * here[c] - MOMENTUM[2] * first
                    - STEP[2] * (curled[c] + m * mixed)
                )
                value = STEP[1] * first + STEP[2] * here[c] + STEP[3] * last
                if c < 2:
                    value = value + STEP[0] * start(f, c, plane)
                term = value * field[f, c, plane - 3, inner, :]
                added = term if added is None else added + term
            total[plane - 3] += added
        return carry

    lax.fori_loop(0, 2 * DEGREE, level_three, 0, unroll=8)
    gradient[...] = total[:, own, :] * (-1.0 / periods)


def adjoint_solve(moments, station_parts, mass, field, grid_rows, members, grid_planes):
    vmem = pl.BlockSpec(memory_space=pltpu.VMEM)
    smem = pl.BlockSpec(memory_space=pltpu.SMEM)
    own_rows = grid_rows // members
    return pl.pallas_call(
        lambda *refs: adjoint_kernel(grid_rows, own_rows, grid_planes, members, *refs),
        out_shape=jax.ShapeDtypeStruct((2, own_rows, LANES), jnp.float32),
        in_specs=[vmem, vmem, smem, vmem, vmem, vmem],
        out_specs=vmem,
        scratch_shapes=[
            pltpu.VMEM((4 * MOMENTS, PLANES * NARROW, LANES), jnp.float32),
            pltpu.VMEM((4 * MOMENTS, PLANES * NARROW, LANES), jnp.float32),
            pltpu.VMEM((2 * (MOMENTS - 1), 3, PLANES - 2, NARROW, LANES), jnp.float32),
            pltpu.VMEM((2 * (MOMENTS - 2), 3, PLANES - 4, NARROW, LANES), jnp.float32),
            pltpu.VMEM((32, LANES), jnp.float32),
            pltpu.VMEM((2, NARROW, LANES), jnp.float32),
        ],
        compiler_params=pltpu.CompilerParams(vmem_limit_bytes=VMEM_LIMIT),
        cost_estimate=pl.CostEstimate(flops=200_000_000, bytes_accessed=3_000_000, transcendentals=0),
        name="adjoint_solve",
    )(moments, *station_parts, mass, field.reshape(2 * DEGREE, 3, 2, WINDOW, LANES))


def shards(source, conductivity, period_shift, site_cells, site_weights, observed, data_weight):
    grid_rows = conductivity.shape[1]
    count = lax.axis_size("space")
    members = lax.axis_size("period")
    grid_planes = conductivity.shape[0] * count
    slab, beside, data = pack(
        source, conductivity, period_shift, observed, data_weight, members
    )

    def swapped(values, partner):
        pairs = []
        for i in range(count):
            j = partner(i)
            flip = 0 if i // 2 == j // 2 else 1
            if 0 <= j < count:
                pairs += [(i * members + t, j * members + (t ^ flip)) for t in range(members)]
        return lax.ppermute(values, ("space", "period"), pairs)

    mate = swapped(slab, lambda i: i ^ 1)
    payload, data, late_cells = lax.optimization_barrier((extend(beside, mate), data, site_cells))
    beside = swapped(payload, lambda i: i + 1 if i % 2 else i - 1)
    places, *lists = stations(late_cells, site_weights, grid_rows, members)
    data = lax.all_to_all(data, "period", 0, 0, tiled=True)
    beside, data, places = lax.optimization_barrier((beside, data, places))
    station_parts = (places, *lists)
    windows = (slab, mate, beside, swapped(beside, lambda i: i ^ 1))
    field, sent, mass = forward_solve(windows, station_parts, grid_rows, members, grid_planes)
    sent, data = lax.optimization_barrier((sent, data))
    read = lax.all_to_all(sent, "space", 0, 0, tiled=True)
    moments, owned = residuals(read, data, site_cells, grid_rows, members)
    moments = lax.all_to_all(moments, "space", 0, 0, tiled=True)
    moments, owned = lax.optimization_barrier((moments, owned))
    owned = lax.all_to_all(owned, "period", 0, 0, tiled=True)
    gradient = adjoint_solve(moments, station_parts, mass, field, grid_rows, members, grid_planes)
    return jnp.sum(owned, axis=0, keepdims=True), gradient


def solution(mesh):
    placed = (
        P(None, None, "space", None, None),
        P("space", None, None),
        P("period"),
        P(),
        P(),
        P("period", None, "space"),
        P("period", None, "space"),
    )
    return jax.shard_map(
        shards,
        mesh=mesh,
        in_specs=placed,
        out_specs=(P("period", None, "space"), P("space", "period", None)),
        check_vma=False,
    )
```

```python
import jax
import jax.numpy as jnp
from jax import lax
from jax.experimental import pallas as pl
from jax.experimental.pallas import tpu as pltpu
from jax.sharding import PartitionSpec as P

SWEEPS = 4
LOWER_BOUND = 0.05
UPPER_BOUND = 16.0

CENTER = 1.25
HALO = SWEEPS - 1
PLANES = 2 + 2 * HALO
WINDOW = 32
NARROW = 24
DEGREE = SWEEPS
MOMENTS = 2 * SWEEPS - 1
LANES = 128
VMEM_SMALL = 6 * 1024 * 1024
VMEM_LIMIT = 16 * 1024 * 1024


def chebyshev_steps(sweep_count):
    center = 0.5 * (UPPER_BOUND + LOWER_BOUND)
    spread = 0.5 * (UPPER_BOUND - LOWER_BOUND)
    step_sizes = []
    momenta = []
    step_size = 1.0 / center
    for number in range(sweep_count):
        if number == 0:
            momentum = 0.0
        elif number == 1:
            momentum = 0.5 * (spread * step_size) ** 2
        else:
            momentum = (0.5 * spread * step_size) ** 2
        if number > 0:
            step_size = 1.0 / (center - momentum / step_size)
        step_sizes.append(step_size)
        momenta.append(momentum)
    return (step_sizes, momenta)


STEP, MOMENTUM = chebyshev_steps(SWEEPS)


def window_row(member, grid_rows, own_rows):
    first = member * own_rows - (WINDOW - own_rows) // 2
    return pl.multiple_of(jnp.clip(first, 0, grid_rows - WINDOW), 8)


def narrow_row(member, grid_rows, own_rows):
    return jnp.clip(member * own_rows - (NARROW - own_rows) // 2, 0, grid_rows - NARROW)


def first_window_plane():
    return lax.axis_index("space") * 2 - HALO


def iota(shape, dim):
    return lax.broadcasted_iota(jnp.int32, shape, dim)


def parts_of(values):
    high = values.astype(jnp.bfloat16)
    rest = values - high.astype(jnp.float32)
    middle = rest.astype(jnp.bfloat16)
    low = (rest - middle.astype(jnp.float32)).astype(jnp.bfloat16)
    return high, middle, low


def dot_nt(left, right):
    return lax.dot_general(left, right, (((1,), (1,)), ((), ())), preferred_element_type=jnp.float32)


def dot_nn(left, right):
    return lax.dot_general(left, right, (((1,), (0,)), ((), ())), preferred_element_type=jnp.float32)


def next_z(v):
    return jnp.where(iota(v.shape, 1) == v.shape[1] - 1, 0.0, pltpu.roll(v, v.shape[1] - 1, 1))


def last_z(v):
    return jnp.where(iota(v.shape, 1) == 0, 0.0, pltpu.roll(v, 1, 1))


def next_y(v):
    return jnp.where(iota(v.shape, 0) == v.shape[0] - 1, 0.0, pltpu.roll(v, v.shape[0] - 1, 0))


def last_y(v):
    return jnp.where(iota(v.shape, 0) == 0, 0.0, pltpu.roll(v, 1, 0))


def curl_curl(get, first, last, first_plane, planes_in_grid, along_z=None):
    before = None
    here = get(first - 1)
    for plane in range(first - 1, last + 1):
        after = get(plane + 1)
        east, north, down = here
        c2 = along_z(plane, 0) if along_z else next_z(east) - east
        if down is not None:
            c2 = c2 - (after[2] - down)
        c3 = (after[1] - north) - (next_y(east) - east)
        if plane < HALO and plane % 2 == 0:
            inside = jnp.where(first_plane + plane < 0, 0.0, 1.0)
            c2 = c2 * inside
            c3 = c3 * inside
        if plane >= first:
            c1 = -along_z(plane, 1) if along_z else north - next_z(north)
            if down is not None:
                c1 = c1 + (next_y(down) - down)
            a1 = (c3 - last_y(c3)) - (c2 - last_z(c2))
            a2 = (c1 - last_z(c1)) - (c3 - before[1])
            a3 = (c2 - before[0]) - (c1 - last_y(c1))
            if plane == HALO + 2:
                inside = jnp.where(first_plane + plane >= planes_in_grid, 0.0, 1.0)
                a1, a2, a3 = a1 * inside, a2 * inside, a3 * inside
            yield plane, here, (a1, a2, a3)
        before = (c2, c3)
        here = after


def pack_kernel(
    grid_rows, own_rows, source, conductivity, shift, observed, weight,
    slab, beside, far_a, far_b, data, pairs, sems,
):
    member = lax.axis_index("period")
    pair = (lax.axis_index("space") // 2) % 2
    copies = [(observed.at[0], pairs.at[0]), (weight.at[0], pairs.at[1])]
    rows = pl.ds(window_row(member, grid_rows, own_rows), WINDOW)
    for pol in range(2):
        copies.append((source.at[pol, :, :, rows, :], slab.at[pl.ds(3 * pol, 3)]))
    copies.append((conductivity.at[:, rows, :], slab.at[6]))
    rows = pl.ds(window_row(member + 1 - 2 * (member % 2), grid_rows, own_rows), WINDOW)
    for pol in range(2):
        copies.append((source.at[pol, :, :, rows, :], beside.at[pl.ds(3 * pol, 3)]))
        copies.append((source.at[pol, :, 1 - pair, rows, :], far_a.at[pl.ds(3 * pol, 3)]))
        copies.append((source.at[pol, :, pair, rows, :], far_b.at[pl.ds(3 * pol, 3)]))
    copies.append((conductivity.at[:, rows, :], beside.at[6]))
    started = [pltpu.make_async_copy(a, b, sems.at[i]) for i, (a, b) in enumerate(copies)]
    for copy in started:
        copy.start()
    for copy in started[:2]:
        copy.wait()
    for member in range(data.shape[0]):
        data[member, 0:4, :] = pairs[0]
        data[member, 4:8, :] = pairs[1]
        data[member, 8:16, :] = jnp.full((8, LANES), shift[0], jnp.float32)
    for copy in started[2:]:
        copy.wait()


def pack(source, conductivity, shift, observed, weight, members):
    grid_rows = source.shape[3]
    shape = jax.ShapeDtypeStruct
    hbm = pl.BlockSpec(memory_space=pltpu.HBM)
    vmem = pl.BlockSpec(memory_space=pltpu.VMEM)
    smem = pl.BlockSpec(memory_space=pltpu.SMEM)
    return pl.pallas_call(
        lambda *refs: pack_kernel(grid_rows, grid_rows // members, *refs),
        out_shape=(shape((7, 2, WINDOW, LANES), jnp.float32),) * 2
        + (shape((6, WINDOW, LANES), jnp.float32),) * 2
        + (shape((members, 16, LANES), jnp.float32),),
        in_specs=[hbm, hbm, smem, hbm, hbm],
        out_specs=(vmem,) * 5,
        scratch_shapes=[pltpu.VMEM((2, 4, LANES), jnp.float32), pltpu.SemaphoreType.DMA((12,))],
        compiler_params=pltpu.CompilerParams(vmem_limit_bytes=VMEM_SMALL),
        name="pack",
    )(
        *(pltpu.with_memory_space_constraint(v, pltpu.HBM) for v in (source, conductivity)),
        shift,
        *(pltpu.with_memory_space_constraint(v, pltpu.HBM) for v in (observed, weight)),
    )


def stations_kernel(grid_rows, own_rows, cells, weights, places, count, features, marks, staged):
    member = lax.axis_index("period")
    first_own = member * own_rows
    first_row = window_row(member, grid_rows, own_rows)
    first_narrow = narrow_row(member, grid_rows, own_rows)
    plane_size = grid_rows * LANES
    cell = cells[...]
    x = cell // plane_size - first_window_plane()
    y = (cell // LANES) % grid_rows
    reached = (
        (x >= 0) & (x < PLANES)
        & (y >= first_own - HALO - 1) & (y < first_own + own_rows + HALO + 1)
    )
    row = jnp.where(reached, x * WINDOW + y - first_row, 0).astype(jnp.float32)
    narrow = jnp.where(reached, x * NARROW + y - first_narrow, 0).astype(jnp.float32)
    weight = jnp.where(reached, weights[...], 0.0)
    present = jnp.max(jnp.where(reached, 1.0, 0.0), axis=0, keepdims=True)
    blocks = cell.shape[1] // LANES
    staged[...] = jnp.zeros(staged.shape, jnp.float32)
    staged[0:4, :] = row
    staged[4:8, :] = (cell % LANES).astype(jnp.float32)
    staged[20:24, :] = narrow
    for number, part in enumerate(parts_of(weight)):
        staged[8 + 4 * number : 12 + 4 * number, :] = part.astype(jnp.float32)
    for block in range(blocks):
        marks[block : block + 1, :] = present[:, block * LANES : (block + 1) * LANES]
    mark = marks[...]
    square = (LANES, LANES)
    upto = jnp.where(iota(square, 0) <= iota(square, 1), 1.0, 0.0).astype(jnp.bfloat16)
    inner = dot_nn(mark.astype(jnp.bfloat16), upto)
    totals = dot_nn(mark.astype(jnp.bfloat16), jnp.ones(square, jnp.bfloat16))
    earlier = jnp.where(iota((blocks, blocks), 0) > iota((blocks, blocks), 1), 1.0, 0.0)
    offsets = dot_nn(earlier.astype(jnp.bfloat16), totals.astype(jnp.bfloat16))
    places[...] = jnp.where(mark > 0.0, inner + offsets - 1.0, -1.0).astype(jnp.int32)
    chunks = (jnp.sum(mark).astype(jnp.int32) + LANES - 1) // LANES
    count[0] = chunks

    def one_chunk(chunk, carry):
        gathered = jnp.zeros((staged.shape[0], LANES), jnp.float32)
        for block in range(blocks):
            feature = staged[:, block * LANES : (block + 1) * LANES].astype(jnp.bfloat16)
            gathered += dot_nt(feature, picks(places, block, chunk))
        features[chunk] = gathered
        return carry

    features[0] = jnp.zeros(features.shape[1:], jnp.float32)
    lax.fori_loop(0, chunks, one_chunk, 0)


def picks(places, block, chunk):
    wanted = places[block : block + 1, :] - chunk * LANES
    return jnp.where(iota((LANES, LANES), 0) == wanted, 1.0, 0.0).astype(jnp.bfloat16)


def stations(cells, weights, grid_rows, members):
    blocks = cells.shape[1] // LANES
    shape = jax.ShapeDtypeStruct
    vmem = pl.BlockSpec(memory_space=pltpu.VMEM)
    return pl.pallas_call(
        lambda *refs: stations_kernel(grid_rows, grid_rows // members, *refs),
        out_shape=(
            shape((blocks, LANES), jnp.int32),
            shape((1,), jnp.int32),
            shape((blocks, 32, LANES), jnp.float32),
        ),
        in_specs=[vmem, vmem],
        out_specs=(vmem, pl.BlockSpec(memory_space=pltpu.SMEM), vmem),
        scratch_shapes=[
            pltpu.VMEM((blocks, LANES), jnp.float32),
            pltpu.VMEM((32, cells.shape[1]), jnp.float32),
        ],
        compiler_params=pltpu.CompilerParams(vmem_limit_bytes=VMEM_LIMIT),
        cost_estimate=pl.CostEstimate(flops=10_000_000, bytes_accessed=200_000, transcendentals=0),
        name="stations",
    )(cells, weights)


def row_weights(feature, field, first, count):
    rows = (iota((count, LANES), 0) + first).astype(jnp.float32)
    total = jnp.zeros((count, LANES), jnp.float32)
    for q in range(4):
        weight = feature[8 + q : 9 + q] + feature[12 + q : 13 + q] + feature[16 + q : 17 + q]
        total += jnp.where(rows == feature[field + q : field + q + 1], weight, 0.0)
    return total


def depth_picks(feature):
    depth = iota((LANES, LANES), 0).astype(jnp.float32)
    return jnp.where(depth == feature[4:5], 1.0, 0.0).astype(jnp.bfloat16)


def depth_picks_and_differences(feature):
    depth = iota((LANES, LANES), 0).astype(jnp.float32)
    here = jnp.where(depth == feature[4:5], 1.0, 0.0)
    change = jnp.where(depth + 1.0 == feature[4:5], 1.0, 0.0) - here
    return jnp.concatenate([here, change], axis=0).astype(jnp.bfloat16)


def forward_kernel(
    grid_rows, own_rows, grid_planes, slab, mate, beside, far_a, far_b, places, count, features,
    field, sent, mass, window, d1, d2,
):
    first_plane = first_window_plane()
    even = lax.axis_index("space") % 2 == 0
    lower = (lax.axis_index("space") // 2) % 2 == 0
    for plane in range(2):
        here, there = mate[:, plane], beside[:, plane]
        window[:, 1 + plane] = jnp.where(even, there, here)
        window[:, 3 + plane] = slab[:, plane]
        window[:, 5 + plane] = jnp.where(even, here, there)
    window[0:6, 0] = jnp.where(lower, far_b[...], far_a[...])
    window[0:6, PLANES - 1] = jnp.where(lower, far_a[...], far_b[...])
    mass[...] = window[6, 1 : PLANES - 1]

    def part(number, plane):
        return window[number, plane]

    for pol in range(2):
        def b(plane, pol=pol):
            return tuple(part(3 * pol + c, plane) for c in range(3))

        for plane, here, curled in curl_curl(b, 1, 6, first_plane, grid_planes):
            m = mass[plane - 1]
            for c in range(3):
                heavy = m * here[c]
                d1[0, pol, c, plane - 1] = (
                    (1.0 + MOMENTUM[1]) * here[c] - STEP[0] * (curled[c] + CENTER * heavy)
                )
                d1[1, pol, c, plane - 1] = -STEP[0] * heavy

        def level1(j, pol=pol):
            return lambda plane: tuple(d1[j, pol, c, plane - 1] for c in range(3))

        for j in range(2):
            for plane, here, curled in curl_curl(level1(j), 2, 5, first_plane, grid_planes):
                m = mass[plane - 1]
                for c in range(3):
                    mixed = CENTER * here[c]
                    if j == 1:
                        mixed = mixed + d1[0, pol, c, plane - 1]
                    value = (1.0 + MOMENTUM[2]) * here[c] - STEP[1] * (curled[c] + m * mixed)
                    if j == 0:
                        value = value - MOMENTUM[1] * part(3 * pol + c, plane)
                    d2[j, pol, c, plane - 2] = value
                    if j == 1:
                        d2[2, pol, c, plane - 2] = -STEP[1] * (m * here[c])

        def level2(j, pol=pol):
            return lambda plane: tuple(d2[j, pol, c, plane - 2] for c in range(3))

        for j in range(3):
            for plane, here, curled in curl_curl(level2(j), 3, 4, first_plane, grid_planes):
                m = mass[plane - 1]
                for c in range(3):
                    mixed = CENTER * here[c]
                    if j > 0:
                        mixed = mixed + d2[j - 1, pol, c, plane - 2]
                    last = (1.0 + MOMENTUM[3]) * here[c] - STEP[2] * (curled[c] + m * mixed)
                    value = STEP[2] * here[c]
                    if j < 2:
                        first = d1[j, pol, c, plane - 1]
                        last = last - MOMENTUM[2] * first
                        value = value + STEP[1] * first
                    if j == 0:
                        value = value + STEP[0] * part(3 * pol + c, plane)
                    field[j, pol, c, plane - 3] = value + STEP[3] * last
                    if j == 2:
                        field[3, pol, c, plane - 3] = -(STEP[3] * STEP[2]) * (m * here[c])

    members = sent.shape[0]
    sent[...] = jnp.zeros(sent.shape, jnp.float32)

    def one_chunk(chunk, carry):
        feature = features[chunk]
        weight = row_weights(feature, 0, HALO * WINDOW, 2 * WINDOW)
        depth = depth_picks(feature)
        rows = []
        stacked = jnp.concatenate([depth] * 3, axis=0)
        for j in range(DEGREE):
            values = field[j, :, 0:2].reshape(8 * WINDOW, LANES)
            at_depth = dot_nn(jnp.concatenate(parts_of(values), axis=1), stacked)
            for number in range(4):
                part = at_depth[2 * WINDOW * number : 2 * WINDOW * (number + 1)]
                rows.append(jnp.sum(part * weight, axis=0, keepdims=True))
        read = jnp.concatenate(rows, axis=0)
        pieces = jnp.concatenate(parts_of(read), axis=0)
        for block in range(members):
            spread = dot_nn(pieces, picks(places, block, chunk))
            sent[block] += spread[0:16] + spread[16:32] + spread[32:48]
        return carry

    lax.fori_loop(0, count[0], one_chunk, 0)


def forward_solve(windows, station_parts, grid_rows, members, grid_planes):
    shape = jax.ShapeDtypeStruct
    vmem = pl.BlockSpec(memory_space=pltpu.VMEM)
    smem = pl.BlockSpec(memory_space=pltpu.SMEM)
    blocks = station_parts[0].shape[0]
    return pl.pallas_call(
        lambda *refs: forward_kernel(grid_rows, grid_rows // members, grid_planes, *refs),
        out_shape=(
            shape((DEGREE, 2, 3, 2, WINDOW, LANES), jnp.float32),
            shape((blocks, 4 * DEGREE, LANES), jnp.float32),
            shape((PLANES - 2, WINDOW, LANES), jnp.float32),
        ),
        in_specs=[vmem] * 6 + [smem, vmem],
        out_specs=(vmem, vmem, vmem),
        scratch_shapes=[
            pltpu.VMEM((7, PLANES, WINDOW, LANES), jnp.float32),
            pltpu.VMEM((2, 2, 3, PLANES - 2, WINDOW, LANES), jnp.float32),
            pltpu.VMEM((3, 2, 3, PLANES - 4, WINDOW, LANES), jnp.float32),
        ],
        compiler_params=pltpu.CompilerParams(vmem_limit_bytes=VMEM_LIMIT),
        cost_estimate=pl.CostEstimate(flops=20_000_000_000, bytes_accessed=3_000_000, transcendentals=0),
        name="forward_solve",
    )(*windows, *station_parts)


def residual_kernel(grid_rows, own_rows, read, data, cells, moments, owned, staged):
    members = data.shape[0]
    total = read[0]
    for member in range(1, read.shape[0]):
        total = total + read[member]
    coefficients = [total[4 * j : 4 * j + 4] for j in range(DEGREE)]
    first = pl.multiple_of(lax.axis_index("space") * LANES, LANES)
    cell = cells[:, pl.ds(first, LANES)]
    y = jnp.min((cell // LANES) % grid_rows, axis=0, keepdims=True)
    mine = (y // own_rows) == lax.axis_index("period")
    sums = [jnp.zeros((4, LANES), jnp.float32) for _ in range(MOMENTS)]
    for member in range(members):
        shift = data[member, 8:9, :]
        delta = shift - CENTER
        value = coefficients[DEGREE - 1]
        for j in range(DEGREE - 2, -1, -1):
            value = value * delta + coefficients[j]
        owned[member] = jnp.where(mine, value, 0.0)
        weight = data[member, 4:8, :]
        term = shift * (weight * weight * (value - data[member, 0:4, :]))
        for number in range(MOMENTS):
            sums[number] = sums[number] + term
            if number + 1 < MOMENTS:
                term = term * delta
    staged[...] = jnp.zeros(staged.shape, jnp.float32)
    for number in range(MOMENTS):
        staged[4 * number : 4 * number + 4, :] = sums[number]
    value = staged[...]
    for member in range(moments.shape[0]):
        moments[member] = value


def residuals(read, data, cells, grid_rows, members):
    shape = jax.ShapeDtypeStruct
    vmem = pl.BlockSpec(memory_space=pltpu.VMEM)
    return pl.pallas_call(
        lambda *refs: residual_kernel(grid_rows, grid_rows // members, *refs),
        out_shape=(
            shape((read.shape[0], 32, LANES), jnp.float32),
            shape((members, 4, LANES), jnp.float32),
        ),
        in_specs=[vmem, vmem, vmem],
        out_specs=(vmem, vmem),
        scratch_shapes=[pltpu.VMEM((32, LANES), jnp.float32)],
        compiler_params=pltpu.CompilerParams(vmem_limit_bytes=VMEM_SMALL),
        name="residuals",
    )(read, data, cells)


def adjoint_kernel(
    grid_rows, own_rows, grid_planes, periods, moments, places, count, features, mass, field,
    gradient, d0, slope, d1, d2, picked, total,
):
    first_plane = first_window_plane()
    member = lax.axis_index("period")
    first_row = narrow_row(member, grid_rows, own_rows)
    inner = pl.ds(first_row - window_row(member, grid_rows, own_rows), NARROW)
    own = pl.ds(member * own_rows - first_row, own_rows)
    blocks = moments.shape[0]
    window_rows = PLANES * NARROW

    def add_chunk(chunk, fresh):
        feature = features[chunk]
        weight = row_weights(feature, 20, 0, window_rows)
        depth = depth_picks_and_differences(feature)
        depth = jnp.concatenate([depth, depth], axis=1)
        gathered = jnp.zeros((96, LANES), jnp.float32)
        for block in range(blocks):
            pieces = jnp.concatenate(parts_of(moments[block]), axis=0)
            gathered += dot_nt(pieces, picks(places, block, chunk))
        picked[...] = gathered[0:32] + gathered[32:64] + gathered[64:96]

        def one_field(number, carry):
            values = weight * picked[pl.ds(number, 1), :]
            high = values.astype(jnp.bfloat16)
            low = (values - high.astype(jnp.float32)).astype(jnp.bfloat16)
            placed = dot_nt(jnp.concatenate([high, low], axis=1), depth)
            if fresh:
                d0[number] = placed[:, :LANES]
                slope[number] = placed[:, LANES:]
            else:
                d0[number] += placed[:, :LANES]
                slope[number] += placed[:, LANES:]
            return carry

        lax.fori_loop(0, 4 * MOMENTS, one_field, 0, unroll=2 * MOMENTS)

    add_chunk(0, True)

    def one_chunk(chunk, carry):
        add_chunk(chunk, False)
        return carry

    lax.fori_loop(1, count[0], one_chunk, 0)

    def start(f, c, plane):
        return d0[2 * f + c, plane * NARROW : (plane + 1) * NARROW, :]

    def level_one(f, carry):
        def b(plane):
            return start(f, 0, plane), start(f, 1, plane), None

        def along_z(plane, c):
            return slope[2 * f + c, plane * NARROW : (plane + 1) * NARROW, :]

        for plane, here, curled in curl_curl(b, 1, 6, first_plane, grid_planes, along_z):
            m = mass[plane - 1, inner, :]
            for c in range(2):
                mixed = CENTER * here[c] + start(f + 2, c, plane)
                d1[f, c, plane - 1] = (
                    (1.0 + MOMENTUM[1]) * here[c] - STEP[0] * (curled[c] + m * mixed)
                )
            d1[f, 2, plane - 1] = -STEP[0] * curled[2]
        return carry

    lax.fori_loop(0, 2 * (MOMENTS - 1), level_one, 0, unroll=4)

    def level_two(f, carry):
        def get(plane):
            return tuple(d1[f, c, plane - 1] for c in range(3))

        for plane, here, curled in curl_curl(get, 2, 5, first_plane, grid_planes):
            m = mass[plane - 1, inner, :]
            for c in range(3):
                mixed = CENTER * here[c] + d1[f + 2, c, plane - 1]
                value = (1.0 + MOMENTUM[2]) * here[c] - STEP[1] * (curled[c] + m * mixed)
                if c < 2:
                    value = value - MOMENTUM[1] * start(f, c, plane)
                d2[f, c, plane - 2] = value
        return carry

    lax.fori_loop(0, 2 * (MOMENTS - 2), level_two, 0, unroll=2)

    total[...] = jnp.zeros(total.shape, jnp.float32)

    def level_three(f, carry):
        def get(plane):
            return tuple(d2[f, c, plane - 2] for c in range(3))

        for plane, here, curled in curl_curl(get, 3, 4, first_plane, grid_planes):
            m = mass[plane - 1, inner, :]
            added = None
            for c in range(3):
                mixed = CENTER * here[c] + d2[f + 2, c, plane - 2]
                first = d1[f, c, plane - 1]
                last = (
                    (1.0 + MOMENTUM[3]) * here[c] - MOMENTUM[2] * first
                    - STEP[2] * (curled[c] + m * mixed)
                )
                value = STEP[1] * first + STEP[2] * here[c] + STEP[3] * last
                if c < 2:
                    value = value + STEP[0] * start(f, c, plane)
                term = value * field[f, c, plane - 3, inner, :]
                added = term if added is None else added + term
            total[plane - 3] += added
        return carry

    lax.fori_loop(0, 2 * DEGREE, level_three, 0, unroll=8)
    gradient[...] = total[:, own, :] * (-1.0 / periods)


def adjoint_solve(moments, station_parts, mass, field, grid_rows, members, grid_planes):
    vmem = pl.BlockSpec(memory_space=pltpu.VMEM)
    smem = pl.BlockSpec(memory_space=pltpu.SMEM)
    own_rows = grid_rows // members
    return pl.pallas_call(
        lambda *refs: adjoint_kernel(grid_rows, own_rows, grid_planes, members, *refs),
        out_shape=jax.ShapeDtypeStruct((2, own_rows, LANES), jnp.float32),
        in_specs=[vmem, vmem, smem, vmem, vmem, vmem],
        out_specs=vmem,
        scratch_shapes=[
            pltpu.VMEM((4 * MOMENTS, PLANES * NARROW, LANES), jnp.float32),
            pltpu.VMEM((4 * MOMENTS, PLANES * NARROW, LANES), jnp.float32),
            pltpu.VMEM((2 * (MOMENTS - 1), 3, PLANES - 2, NARROW, LANES), jnp.float32),
            pltpu.VMEM((2 * (MOMENTS - 2), 3, PLANES - 4, NARROW, LANES), jnp.float32),
            pltpu.VMEM((32, LANES), jnp.float32),
            pltpu.VMEM((2, NARROW, LANES), jnp.float32),
        ],
        compiler_params=pltpu.CompilerParams(vmem_limit_bytes=VMEM_LIMIT),
        cost_estimate=pl.CostEstimate(flops=200_000_000, bytes_accessed=3_000_000, transcendentals=0),
        name="adjoint_solve",
    )(moments, *station_parts, mass, field.reshape(2 * DEGREE, 3, 2, WINDOW, LANES))


def shards(source, conductivity, period_shift, site_cells, site_weights, observed, data_weight):
    grid_rows = conductivity.shape[1]
    count = lax.axis_size("space")
    members = lax.axis_size("period")
    grid_planes = conductivity.shape[0] * count
    slab, beside, far_a, far_b, data = pack(
        source, conductivity, period_shift, observed, data_weight, members
    )

    def swapped(values, partner):
        pairs = []
        for i in range(count):
            j = partner(i)
            flip = 0 if i // 2 == j // 2 else 1
            if 0 <= j < count:
                pairs += [(i * members + t, j * members + (t ^ flip)) for t in range(members)]
        return lax.ppermute(values, ("space", "period"), pairs)

    windows = (
        slab,
        swapped(slab, lambda i: i ^ 1),
        swapped(beside, lambda i: i + 1 if i % 2 else i - 1),
        swapped(far_a, lambda i: i ^ 2),
        swapped(far_b, lambda i: i + 2 if i & 2 else i - 2),
    )
    mate, data, late_cells = lax.optimization_barrier((windows[1], data, site_cells))
    windows = (windows[0], mate, *windows[2:])
    data = lax.all_to_all(data, "period", 0, 0, tiled=True)
    station_parts = stations(late_cells, site_weights, grid_rows, members)
    field, sent, mass = forward_solve(windows, station_parts, grid_rows, members, grid_planes)
    sent, data = lax.optimization_barrier((sent, data))
    read = lax.all_to_all(sent, "space", 0, 0, tiled=True)
    moments, owned = residuals(read, data, site_cells, grid_rows, members)
    moments = lax.all_to_all(moments, "space", 0, 0, tiled=True)
    moments, owned = lax.optimization_barrier((moments, owned))
    owned = lax.all_to_all(owned, "period", 0, 0, tiled=True)
    gradient = adjoint_solve(moments, station_parts, mass, field, grid_rows, members, grid_planes)
    return jnp.sum(owned, axis=0, keepdims=True), gradient


def solution(mesh):
    placed = (
        P(None, None, "space", None, None),
        P("space", None, None),
        P("period"),
        P(),
        P(),
        P("period", None, "space"),
        P("period", None, "space"),
    )
    return jax.shard_map(
        shards,
        mesh=mesh,
        in_specs=placed,
        out_specs=(P("period", None, "space"), P("space", "period", None)),
        check_vma=False,
    )
```

```python
import jax
import jax.numpy as jnp
from jax import lax
from jax.experimental import pallas as pl
from jax.experimental.pallas import tpu as pltpu
from jax.sharding import PartitionSpec as P

SWEEPS = 4
LOWER_BOUND = 0.05
UPPER_BOUND = 16.0

CENTER = 1.25
HALO = SWEEPS - 1
PLANES = 2 + 2 * HALO
WINDOW = 32
NARROW = 24
DEGREE = SWEEPS
MOMENTS = 2 * SWEEPS - 1
LANES = 128
VMEM_SMALL = 6 * 1024 * 1024
VMEM_LIMIT = 16 * 1024 * 1024


def chebyshev_steps(sweep_count):
    center = 0.5 * (UPPER_BOUND + LOWER_BOUND)
    spread = 0.5 * (UPPER_BOUND - LOWER_BOUND)
    step_sizes = []
    momenta = []
    step_size = 1.0 / center
    for number in range(sweep_count):
        if number == 0:
            momentum = 0.0
        elif number == 1:
            momentum = 0.5 * (spread * step_size) ** 2
        else:
            momentum = (0.5 * spread * step_size) ** 2
        if number > 0:
            step_size = 1.0 / (center - momentum / step_size)
        step_sizes.append(step_size)
        momenta.append(momentum)
    return (step_sizes, momenta)


STEP, MOMENTUM = chebyshev_steps(SWEEPS)


def window_row(member, grid_rows, own_rows):
    first = member * own_rows - (WINDOW - own_rows) // 2
    return pl.multiple_of(jnp.clip(first, 0, grid_rows - WINDOW), 8)


def narrow_row(member, grid_rows, own_rows):
    return jnp.clip(member * own_rows - (NARROW - own_rows) // 2, 0, grid_rows - NARROW)


def first_window_plane():
    return lax.axis_index("space") * 2 - HALO


def iota(shape, dim):
    return lax.broadcasted_iota(jnp.int32, shape, dim)


def parts_of(values):
    high = values.astype(jnp.bfloat16)
    rest = values - high.astype(jnp.float32)
    middle = rest.astype(jnp.bfloat16)
    low = (rest - middle.astype(jnp.float32)).astype(jnp.bfloat16)
    return high, middle, low


def dot_nt(left, right):
    return lax.dot_general(left, right, (((1,), (1,)), ((), ())), preferred_element_type=jnp.float32)


def dot_nn(left, right):
    return lax.dot_general(left, right, (((1,), (0,)), ((), ())), preferred_element_type=jnp.float32)


def next_z(v):
    return jnp.where(iota(v.shape, 1) == v.shape[1] - 1, 0.0, pltpu.roll(v, v.shape[1] - 1, 1))


def last_z(v):
    return jnp.where(iota(v.shape, 1) == 0, 0.0, pltpu.roll(v, 1, 1))


def next_y(v):
    return jnp.where(iota(v.shape, 0) == v.shape[0] - 1, 0.0, pltpu.roll(v, v.shape[0] - 1, 0))


def last_y(v):
    return jnp.where(iota(v.shape, 0) == 0, 0.0, pltpu.roll(v, 1, 0))


def curl_curl(get, first, last, first_plane, planes_in_grid, along_z=None):
    before = None
    here = get(first - 1)
    for plane in range(first - 1, last + 1):
        after = get(plane + 1)
        east, north, down = here
        c2 = along_z(plane, 0) if along_z else next_z(east) - east
        if down is not None:
            c2 = c2 - (after[2] - down)
        c3 = (after[1] - north) - (next_y(east) - east)
        if plane < HALO and plane % 2 == 0:
            inside = jnp.where(first_plane + plane < 0, 0.0, 1.0)
            c2 = c2 * inside
            c3 = c3 * inside
        if plane >= first:
            c1 = -along_z(plane, 1) if along_z else north - next_z(north)
            if down is not None:
                c1 = c1 + (next_y(down) - down)
            a1 = (c3 - last_y(c3)) - (c2 - last_z(c2))
            a2 = (c1 - last_z(c1)) - (c3 - before[1])
            a3 = (c2 - before[0]) - (c1 - last_y(c1))
            if plane == HALO + 2:
                inside = jnp.where(first_plane + plane >= planes_in_grid, 0.0, 1.0)
                a1, a2, a3 = a1 * inside, a2 * inside, a3 * inside
            yield plane, here, (a1, a2, a3)
        before = (c2, c3)
        here = after


def pack_kernel(
    grid_rows, own_rows, source, conductivity, shift, observed, weight,
    slab, beside, data, pairs, sems,
):
    member = lax.axis_index("period")
    odd = lax.axis_index("space") % 2
    copies = [(observed.at[0], pairs.at[0]), (weight.at[0], pairs.at[1])]
    rows = pl.ds(window_row(member, grid_rows, own_rows), WINDOW)
    for pol in range(2):
        copies.append((source.at[pol, :, :, rows, :], slab.at[pl.ds(3 * pol, 3)]))
    copies.append((conductivity.at[:, rows, :], slab.at[6]))
    rows = pl.ds(window_row(member + 1 - 2 * (member % 2), grid_rows, own_rows), WINDOW)
    for pol in range(2):
        copies.append((source.at[pol, :, :, rows, :], beside.at[pl.ds(3 * pol, 3)]))
        for c in range(3):
            number = 3 * pol + c
            copies.append((source.at[pol, c, 1 - odd, rows, :], slab.at[7 + number // 2, number % 2]))
    copies.append((conductivity.at[:, rows, :], beside.at[6]))
    started = [pltpu.make_async_copy(a, b, sems.at[i]) for i, (a, b) in enumerate(copies)]
    for copy in started:
        copy.start()
    for copy in started:
        copy.wait()
    for member in range(data.shape[0]):
        data[member, 0:4, :] = pairs[0]
        data[member, 4:8, :] = pairs[1]
        data[member, 8:16, :] = jnp.full((8, LANES), shift[0], jnp.float32)


def pack(source, conductivity, shift, observed, weight, members):
    grid_rows = source.shape[3]
    shape = jax.ShapeDtypeStruct
    hbm = pl.BlockSpec(memory_space=pltpu.HBM)
    vmem = pl.BlockSpec(memory_space=pltpu.VMEM)
    smem = pl.BlockSpec(memory_space=pltpu.SMEM)
    return pl.pallas_call(
        lambda *refs: pack_kernel(grid_rows, grid_rows // members, *refs),
        out_shape=(
            shape((10, 2, WINDOW, LANES), jnp.float32),
            shape((7, 2, WINDOW, LANES), jnp.float32),
        )
        + (shape((members, 16, LANES), jnp.float32),),
        in_specs=[hbm, hbm, smem, hbm, hbm],
        out_specs=(vmem,) * 3,
        scratch_shapes=[pltpu.VMEM((2, 4, LANES), jnp.float32), pltpu.SemaphoreType.DMA((14,))],
        compiler_params=pltpu.CompilerParams(vmem_limit_bytes=VMEM_SMALL),
        name="pack",
    )(
        *(pltpu.with_memory_space_constraint(v, pltpu.HBM) for v in (source, conductivity)),
        shift,
        *(pltpu.with_memory_space_constraint(v, pltpu.HBM) for v in (observed, weight)),
    )


def extend_kernel(beside, mate, payload):
    payload[0:7] = beside[...]
    payload[7:10] = mate[7:10]


def extend(beside, mate):
    vmem = pl.BlockSpec(memory_space=pltpu.VMEM)
    return pl.pallas_call(
        extend_kernel,
        out_shape=jax.ShapeDtypeStruct((10, 2, WINDOW, LANES), jnp.float32),
        in_specs=[vmem, vmem],
        out_specs=vmem,
        compiler_params=pltpu.CompilerParams(vmem_limit_bytes=VMEM_SMALL),
        name="extend",
    )(beside, mate)


def stations_kernel(grid_rows, own_rows, cells, weights, places, count, features, marks, staged):
    member = lax.axis_index("period")
    first_own = member * own_rows
    first_row = window_row(member, grid_rows, own_rows)
    first_narrow = narrow_row(member, grid_rows, own_rows)
    plane_size = grid_rows * LANES
    cell = cells[...]
    x = cell // plane_size - first_window_plane()
    y = (cell // LANES) % grid_rows
    reached = (
        (x >= 0) & (x < PLANES)
        & (y >= first_own - HALO - 1) & (y < first_own + own_rows + HALO + 1)
    )
    row = jnp.where(reached, x * WINDOW + y - first_row, 0).astype(jnp.float32)
    narrow = jnp.where(reached, x * NARROW + y - first_narrow, 0).astype(jnp.float32)
    weight = jnp.where(reached, weights[...], 0.0)
    present = jnp.max(jnp.where(reached, 1.0, 0.0), axis=0, keepdims=True)
    blocks = cell.shape[1] // LANES
    staged[...] = jnp.zeros(staged.shape, jnp.float32)
    staged[0:4, :] = row
    staged[4:8, :] = (cell % LANES).astype(jnp.float32)
    staged[20:24, :] = narrow
    for number, part in enumerate(parts_of(weight)):
        staged[8 + 4 * number : 12 + 4 * number, :] = part.astype(jnp.float32)
    for block in range(blocks):
        marks[block : block + 1, :] = present[:, block * LANES : (block + 1) * LANES]
    mark = marks[...]
    square = (LANES, LANES)
    upto = jnp.where(iota(square, 0) <= iota(square, 1), 1.0, 0.0).astype(jnp.bfloat16)
    inner = dot_nn(mark.astype(jnp.bfloat16), upto)
    totals = dot_nn(mark.astype(jnp.bfloat16), jnp.ones(square, jnp.bfloat16))
    earlier = jnp.where(iota((blocks, blocks), 0) > iota((blocks, blocks), 1), 1.0, 0.0)
    offsets = dot_nn(earlier.astype(jnp.bfloat16), totals.astype(jnp.bfloat16))
    places[...] = jnp.where(mark > 0.0, inner + offsets - 1.0, -1.0).astype(jnp.int32)
    chunks = (jnp.sum(mark).astype(jnp.int32) + LANES - 1) // LANES
    count[0] = chunks

    def one_chunk(chunk, carry):
        gathered = jnp.zeros((staged.shape[0], LANES), jnp.float32)
        for block in range(blocks):
            feature = staged[:, block * LANES : (block + 1) * LANES].astype(jnp.bfloat16)
            gathered += dot_nt(feature, picks(places, block, chunk))
        features[chunk] = gathered
        return carry

    features[0] = jnp.zeros(features.shape[1:], jnp.float32)
    lax.fori_loop(0, chunks, one_chunk, 0)


def picks(places, block, chunk):
    wanted = places[block : block + 1, :] - chunk * LANES
    return jnp.where(iota((LANES, LANES), 0) == wanted, 1.0, 0.0).astype(jnp.bfloat16)


def stations(cells, weights, grid_rows, members):
    blocks = cells.shape[1] // LANES
    shape = jax.ShapeDtypeStruct
    vmem = pl.BlockSpec(memory_space=pltpu.VMEM)
    return pl.pallas_call(
        lambda *refs: stations_kernel(grid_rows, grid_rows // members, *refs),
        out_shape=(
            shape((blocks, LANES), jnp.int32),
            shape((1,), jnp.int32),
            shape((blocks, 32, LANES), jnp.float32),
        ),
        in_specs=[vmem, vmem],
        out_specs=(vmem, pl.BlockSpec(memory_space=pltpu.SMEM), vmem),
        scratch_shapes=[
            pltpu.VMEM((blocks, LANES), jnp.float32),
            pltpu.VMEM((32, cells.shape[1]), jnp.float32),
        ],
        compiler_params=pltpu.CompilerParams(vmem_limit_bytes=VMEM_LIMIT),
        cost_estimate=pl.CostEstimate(flops=10_000_000, bytes_accessed=200_000, transcendentals=0),
        name="stations",
    )(cells, weights)


def row_weights(feature, field, first, count):
    rows = (iota((count, LANES), 0) + first).astype(jnp.float32)
    total = jnp.zeros((count, LANES), jnp.float32)
    for q in range(4):
        weight = feature[8 + q : 9 + q] + feature[12 + q : 13 + q] + feature[16 + q : 17 + q]
        total += jnp.where(rows == feature[field + q : field + q + 1], weight, 0.0)
    return total


def depth_picks(feature):
    depth = iota((LANES, LANES), 0).astype(jnp.float32)
    return jnp.where(depth == feature[4:5], 1.0, 0.0).astype(jnp.bfloat16)


def depth_picks_and_differences(feature):
    depth = iota((LANES, LANES), 0).astype(jnp.float32)
    here = jnp.where(depth == feature[4:5], 1.0, 0.0)
    change = jnp.where(depth + 1.0 == feature[4:5], 1.0, 0.0) - here
    return jnp.concatenate([here, change], axis=0).astype(jnp.bfloat16)


def forward_kernel(
    grid_rows, own_rows, grid_planes, slab, mate, beside, relay, places, count, features,
    field, sent, mass, window, d1, d2,
):
    first_plane = first_window_plane()
    even = lax.axis_index("space") % 2 == 0
    for plane in range(2):
        here, there = mate[0:7, plane], beside[0:7, plane]
        window[:, 1 + plane] = jnp.where(even, there, here)
        window[:, 3 + plane] = slab[0:7, plane]
        window[:, 5 + plane] = jnp.where(even, here, there)
    far = beside[7:10].reshape(6, WINDOW, LANES)
    window[0:6, 0] = jnp.where(even, far, relay[0:6, 1])
    window[0:6, PLANES - 1] = jnp.where(even, relay[0:6, 0], far)
    mass[...] = window[6, 1 : PLANES - 1]

    def part(number, plane):
        return window[number, plane]

    for pol in range(2):
        def b(plane, pol=pol):
            return tuple(part(3 * pol + c, plane) for c in range(3))

        for plane, here, curled in curl_curl(b, 1, 6, first_plane, grid_planes):
            m = mass[plane - 1]
            for c in range(3):
                heavy = m * here[c]
                d1[0, pol, c, plane - 1] = (
                    (1.0 + MOMENTUM[1]) * here[c] - STEP[0] * (curled[c] + CENTER * heavy)
                )
                d1[1, pol, c, plane - 1] = -STEP[0] * heavy

        def level1(j, pol=pol):
            return lambda plane: tuple(d1[j, pol, c, plane - 1] for c in range(3))

        for j in range(2):
            for plane, here, curled in curl_curl(level1(j), 2, 5, first_plane, grid_planes):
                m = mass[plane - 1]
                for c in range(3):
                    mixed = CENTER * here[c]
                    if j == 1:
                        mixed = mixed + d1[0, pol, c, plane - 1]
                    value = (1.0 + MOMENTUM[2]) * here[c] - STEP[1] * (curled[c] + m * mixed)
                    if j == 0:
                        value = value - MOMENTUM[1] * part(3 * pol + c, plane)
                    d2[j, pol, c, plane - 2] = value
                    if j == 1:
                        d2[2, pol, c, plane - 2] = -STEP[1] * (m * here[c])

        def level2(j, pol=pol):
            return lambda plane: tuple(d2[j, pol, c, plane - 2] for c in range(3))

        for j in range(3):
            for plane, here, curled in curl_curl(level2(j), 3, 4, first_plane, grid_planes):
                m = mass[plane - 1]
                for c in range(3):
                    mixed = CENTER * here[c]
                    if j > 0:
                        mixed = mixed + d2[j - 1, pol, c, plane - 2]
                    last = (1.0 + MOMENTUM[3]) * here[c] - STEP[2] * (curled[c] + m * mixed)
                    value = STEP[2] * here[c]
                    if j < 2:
                        first = d1[j, pol, c, plane - 1]
                        last = last - MOMENTUM[2] * first
                        value = value + STEP[1] * first
                    if j == 0:
                        value = value + STEP[0] * part(3 * pol + c, plane)
                    field[j, pol, c, plane - 3] = value + STEP[3] * last
                    if j == 2:
                        field[3, pol, c, plane - 3] = -(STEP[3] * STEP[2]) * (m * here[c])

    members = sent.shape[0]
    sent[...] = jnp.zeros(sent.shape, jnp.float32)

    def one_chunk(chunk, carry):
        feature = features[chunk]
        weight = row_weights(feature, 0, HALO * WINDOW, 2 * WINDOW)
        depth = depth_picks(feature)
        rows = []
        stacked = jnp.concatenate([depth] * 3, axis=0)
        for j in range(DEGREE):
            values = field[j, :, 0:2].reshape(8 * WINDOW, LANES)
            at_depth = dot_nn(jnp.concatenate(parts_of(values), axis=1), stacked)
            for number in range(4):
                part = at_depth[2 * WINDOW * number : 2 * WINDOW * (number + 1)]
                rows.append(jnp.sum(part * weight, axis=0, keepdims=True))
        read = jnp.concatenate(rows, axis=0)
        pieces = jnp.concatenate(parts_of(read), axis=0)
        for block in range(members):
            spread = dot_nn(pieces, picks(places, block, chunk))
            sent[block] += spread[0:16] + spread[16:32] + spread[32:48]
        return carry

    lax.fori_loop(0, count[0], one_chunk, 0)


def forward_solve(windows, station_parts, grid_rows, members, grid_planes):
    shape = jax.ShapeDtypeStruct
    vmem = pl.BlockSpec(memory_space=pltpu.VMEM)
    smem = pl.BlockSpec(memory_space=pltpu.SMEM)
    blocks = station_parts[0].shape[0]
    return pl.pallas_call(
        lambda *refs: forward_kernel(grid_rows, grid_rows // members, grid_planes, *refs),
        out_shape=(
            shape((DEGREE, 2, 3, 2, WINDOW, LANES), jnp.float32),
            shape((blocks, 4 * DEGREE, LANES), jnp.float32),
            shape((PLANES - 2, WINDOW, LANES), jnp.float32),
        ),
        in_specs=[vmem] * 5 + [smem, vmem],
        out_specs=(vmem, vmem, vmem),
        scratch_shapes=[
            pltpu.VMEM((7, PLANES, WINDOW, LANES), jnp.float32),
            pltpu.VMEM((2, 2, 3, PLANES - 2, WINDOW, LANES), jnp.float32),
            pltpu.VMEM((3, 2, 3, PLANES - 4, WINDOW, LANES), jnp.float32),
        ],
        compiler_params=pltpu.CompilerParams(vmem_limit_bytes=VMEM_LIMIT),
        cost_estimate=pl.CostEstimate(flops=20_000_000_000, bytes_accessed=3_000_000, transcendentals=0),
        name="forward_solve",
    )(*windows, *station_parts)


def residual_kernel(grid_rows, own_rows, read, data, cells, moments, owned, staged):
    members = data.shape[0]
    total = read[0]
    for member in range(1, read.shape[0]):
        total = total + read[member]
    coefficients = [total[4 * j : 4 * j + 4] for j in range(DEGREE)]
    first = pl.multiple_of(lax.axis_index("space") * LANES, LANES)
    cell = cells[:, pl.ds(first, LANES)]
    y = jnp.min((cell // LANES) % grid_rows, axis=0, keepdims=True)
    mine = (y // own_rows) == lax.axis_index("period")
    sums = [jnp.zeros((4, LANES), jnp.float32) for _ in range(MOMENTS)]
    for member in range(members):
        shift = data[member, 8:9, :]
        delta = shift - CENTER
        value = coefficients[DEGREE - 1]
        for j in range(DEGREE - 2, -1, -1):
            value = value * delta + coefficients[j]
        owned[member] = jnp.where(mine, value, 0.0)
        weight = data[member, 4:8, :]
        term = shift * (weight * weight * (value - data[member, 0:4, :]))
        for number in range(MOMENTS):
            sums[number] = sums[number] + term
            if number + 1 < MOMENTS:
                term = term * delta
    staged[...] = jnp.zeros(staged.shape, jnp.float32)
    for number in range(MOMENTS):
        staged[4 * number : 4 * number + 4, :] = sums[number]
    value = staged[...]
    for member in range(moments.shape[0]):
        moments[member] = value


def residuals(read, data, cells, grid_rows, members):
    shape = jax.ShapeDtypeStruct
    vmem = pl.BlockSpec(memory_space=pltpu.VMEM)
    return pl.pallas_call(
        lambda *refs: residual_kernel(grid_rows, grid_rows // members, *refs),
        out_shape=(
            shape((read.shape[0], 32, LANES), jnp.float32),
            shape((members, 4, LANES), jnp.float32),
        ),
        in_specs=[vmem, vmem, vmem],
        out_specs=(vmem, vmem),
        scratch_shapes=[pltpu.VMEM((32, LANES), jnp.float32)],
        compiler_params=pltpu.CompilerParams(vmem_limit_bytes=VMEM_SMALL),
        name="residuals",
    )(read, data, cells)


def adjoint_kernel(
    grid_rows, own_rows, grid_planes, periods, moments, places, count, features, mass, field,
    gradient, d0, slope, d1, d2, picked, total,
):
    first_plane = first_window_plane()
    member = lax.axis_index("period")
    first_row = narrow_row(member, grid_rows, own_rows)
    inner = pl.ds(first_row - window_row(member, grid_rows, own_rows), NARROW)
    own = pl.ds(member * own_rows - first_row, own_rows)
    blocks = moments.shape[0]
    window_rows = PLANES * NARROW

    def add_chunk(chunk, fresh):
        feature = features[chunk]
        weight = row_weights(feature, 20, 0, window_rows)
        depth = depth_picks_and_differences(feature)
        depth = jnp.concatenate([depth, depth], axis=1)
        gathered = jnp.zeros((96, LANES), jnp.float32)
        for block in range(blocks):
            pieces = jnp.concatenate(parts_of(moments[block]), axis=0)
            gathered += dot_nt(pieces, picks(places, block, chunk))
        picked[...] = gathered[0:32] + gathered[32:64] + gathered[64:96]

        def one_field(number, carry):
            values = weight * picked[pl.ds(number, 1), :]
            high = values.astype(jnp.bfloat16)
            low = (values - high.astype(jnp.float32)).astype(jnp.bfloat16)
            placed = dot_nt(jnp.concatenate([high, low], axis=1), depth)
            if fresh:
                d0[number] = placed[:, :LANES]
                slope[number] = placed[:, LANES:]
            else:
                d0[number] += placed[:, :LANES]
                slope[number] += placed[:, LANES:]
            return carry

        lax.fori_loop(0, 4 * MOMENTS, one_field, 0, unroll=2 * MOMENTS)

    add_chunk(0, True)

    def one_chunk(chunk, carry):
        add_chunk(chunk, False)
        return carry

    lax.fori_loop(1, count[0], one_chunk, 0)

    def start(f, c, plane):
        return d0[2 * f + c, plane * NARROW : (plane + 1) * NARROW, :]

    def level_one(f, carry):
        def b(plane):
            return start(f, 0, plane), start(f, 1, plane), None

        def along_z(plane, c):
            return slope[2 * f + c, plane * NARROW : (plane + 1) * NARROW, :]

        for plane, here, curled in curl_curl(b, 1, 6, first_plane, grid_planes, along_z):
            m = mass[plane - 1, inner, :]
            for c in range(2):
                mixed = CENTER * here[c] + start(f + 2, c, plane)
                d1[f, c, plane - 1] = (
                    (1.0 + MOMENTUM[1]) * here[c] - STEP[0] * (curled[c] + m * mixed)
                )
            d1[f, 2, plane - 1] = -STEP[0] * curled[2]
        return carry

    lax.fori_loop(0, 2 * (MOMENTS - 1), level_one, 0, unroll=4)

    def level_two(f, carry):
        def get(plane):
            return tuple(d1[f, c, plane - 1] for c in range(3))

        for plane, here, curled in curl_curl(get, 2, 5, first_plane, grid_planes):
            m = mass[plane - 1, inner, :]
            for c in range(3):
                mixed = CENTER * here[c] + d1[f + 2, c, plane - 1]
                value = (1.0 + MOMENTUM[2]) * here[c] - STEP[1] * (curled[c] + m * mixed)
                if c < 2:
                    value = value - MOMENTUM[1] * start(f, c, plane)
                d2[f, c, plane - 2] = value
        return carry

    lax.fori_loop(0, 2 * (MOMENTS - 2), level_two, 0, unroll=2)

    total[...] = jnp.zeros(total.shape, jnp.float32)

    def level_three(f, carry):
        def get(plane):
            return tuple(d2[f, c, plane - 2] for c in range(3))

        for plane, here, curled in curl_curl(get, 3, 4, first_plane, grid_planes):
            m = mass[plane - 1, inner, :]
            added = None
            for c in range(3):
                mixed = CENTER * here[c] + d2[f + 2, c, plane - 2]
                first = d1[f, c, plane - 1]
                last = (
                    (1.0 + MOMENTUM[3]) * here[c] - MOMENTUM[2] * first
                    - STEP[2] * (curled[c] + m * mixed)
                )
                value = STEP[1] * first + STEP[2] * here[c] + STEP[3] * last
                if c < 2:
                    value = value + STEP[0] * start(f, c, plane)
                term = value * field[f, c, plane - 3, inner, :]
                added = term if added is None else added + term
            total[plane - 3] += added
        return carry

    lax.fori_loop(0, 2 * DEGREE, level_three, 0, unroll=8)
    gradient[...] = total[:, own, :] * (-1.0 / periods)


def adjoint_solve(moments, station_parts, mass, field, grid_rows, members, grid_planes):
    vmem = pl.BlockSpec(memory_space=pltpu.VMEM)
    smem = pl.BlockSpec(memory_space=pltpu.SMEM)
    own_rows = grid_rows // members
    return pl.pallas_call(
        lambda *refs: adjoint_kernel(grid_rows, own_rows, grid_planes, members, *refs),
        out_shape=jax.ShapeDtypeStruct((2, own_rows, LANES), jnp.float32),
        in_specs=[vmem, vmem, smem, vmem, vmem, vmem],
        out_specs=vmem,
        scratch_shapes=[
            pltpu.VMEM((4 * MOMENTS, PLANES * NARROW, LANES), jnp.float32),
            pltpu.VMEM((4 * MOMENTS, PLANES * NARROW, LANES), jnp.float32),
            pltpu.VMEM((2 * (MOMENTS - 1), 3, PLANES - 2, NARROW, LANES), jnp.float32),
            pltpu.VMEM((2 * (MOMENTS - 2), 3, PLANES - 4, NARROW, LANES), jnp.float32),
            pltpu.VMEM((32, LANES), jnp.float32),
            pltpu.VMEM((2, NARROW, LANES), jnp.float32),
        ],
        compiler_params=pltpu.CompilerParams(vmem_limit_bytes=VMEM_LIMIT),
        cost_estimate=pl.CostEstimate(flops=200_000_000, bytes_accessed=3_000_000, transcendentals=0),
        name="adjoint_solve",
    )(moments, *station_parts, mass, field.reshape(2 * DEGREE, 3, 2, WINDOW, LANES))


def shards(source, conductivity, period_shift, site_cells, site_weights, observed, data_weight):
    grid_rows = conductivity.shape[1]
    count = lax.axis_size("space")
    members = lax.axis_size("period")
    grid_planes = conductivity.shape[0] * count
    slab, beside, data = pack(
        source, conductivity, period_shift, observed, data_weight, members
    )

    def swapped(values, partner):
        pairs = []
        for i in range(count):
            j = partner(i)
            flip = 0 if i // 2 == j // 2 else 1
            if 0 <= j < count:
                pairs += [(i * members + t, j * members + (t ^ flip)) for t in range(members)]
        return lax.ppermute(values, ("space", "period"), pairs)

    mate = swapped(slab, lambda i: i ^ 1)
    payload, data, late_cells = lax.optimization_barrier((extend(beside, mate), data, site_cells))
    beside = swapped(payload, lambda i: i + 1 if i % 2 else i - 1)
    data = lax.all_to_all(data, "period", 0, 0, tiled=True)
    places, *lists = stations(late_cells, site_weights, grid_rows, members)
    beside, places = lax.optimization_barrier((beside, places))
    station_parts = (places, *lists)
    windows = (slab, mate, beside, swapped(beside, lambda i: i ^ 1))
    field, sent, mass = forward_solve(windows, station_parts, grid_rows, members, grid_planes)
    sent, data = lax.optimization_barrier((sent, data))
    read = lax.all_to_all(sent, "space", 0, 0, tiled=True)
    moments, owned = residuals(read, data, site_cells, grid_rows, members)
    moments = lax.all_to_all(moments, "space", 0, 0, tiled=True)
    moments, owned = lax.optimization_barrier((moments, owned))
    owned = lax.all_to_all(owned, "period", 0, 0, tiled=True)
    gradient = adjoint_solve(moments, station_parts, mass, field, grid_rows, members, grid_planes)
    return jnp.sum(owned, axis=0, keepdims=True), gradient


def solution(mesh):
    placed = (
        P(None, None, "space", None, None),
        P("space", None, None),
        P("period"),
        P(),
        P(),
        P("period", None, "space"),
        P("period", None, "space"),
    )
    return jax.shard_map(
        shards,
        mesh=mesh,
        in_specs=placed,
        out_specs=(P("period", None, "space"), P("space", "period", None)),
        check_vma=False,
    )
```
